128 devices in a mesh: dom: 16 (over z, x), orient: 8 (over y, core).
Axes of the slice: x: 4, y: 4, z: 4, core: 2. Of those that a mesh axis runs over, the one named last changes fastest.
Arguments:
- images: bfloat16 [3072, 256, 256], P('dom'), may hold values from -400 to 400
- defocus: float32 [3072], P('dom'), may hold values from 2 to 12
- noise_var: float32 [256, 128], replicated, may hold values from 1 to 4
- references: bfloat16 [4, 64, 256, 256], P(None, 'orient', 'dom'), may hold values from -0.12 to 0.12
- orient_list: int32 [3072, 16], P('dom'), may hold values from 0 to 63, all different within a row
- class_label: int32 [3072], P('dom'), may hold values from 0 to 3
- owner: int32 [64, 256, 1], replicated, may hold values from 0 to 15; in each aligned block of 128 rows (0 to 127, 128 to 255, ..., all dimensions but the last counted through in order) at most 16 rows name the same one
- slab_row: int32 [64, 256], replicated, may hold values from 0 to 511
- kernel_index: int32 [64, 256], replicated, may hold values from 0 to 3
- interp: bfloat16 [4, 128, 128], replicated, may hold values from -0.5 to 0.5
Outputs:
- volume: float32 [8192, 4, 256], P(('dom', 'orient'))
- log_evidence: float32 [3072], P('dom')
The draws below stay inside these ranges and needn't reach their ends.
Inputs may be any that keep to these rules, and one draw needn't show every extreme that they name: `orient_list`: each particle lists 16 distinct orientations. Taking slice rows in order of orientation then line, in each aligned block of 128 rows at most 16 rows name the same owner, and in every draw some owner is named by exactly 16 rows of some block.
All inputs are finite; a program needn't handle non-finite values.
Results may differ from the reference program's by a relative error of at most 0.022.
Values may be sent and summed in bfloat16 or wider, within the bound.
A program may use at most 256 MiB of HBM per device.

```python
import math
import jax
import jax.numpy as jnp
import numpy as np
from jax import lax

CLASSES = 4
LINES = 256
COLUMNS = 128
SHIFTS = 9
KERNELS = 4
LISTED = 16
PART_DEV = 192
SLAB_ROWS = 512
PARTICLES = 3072
ORIENTS = 64
VOL_ROWS = 8192
BLOCK_ROWS = 128
CAPACITY = 16
N_DOM = 16


def shared_fields(key):
    focus = jax.random.uniform(jax.random.fold_in(key, 202), (PARTICLES,), jnp.float32, 2.0, 12.0)
    return focus


def reference_values(key):
    values = jnp.clip(jax.random.normal(jax.random.fold_in(key, 505), (CLASSES, ORIENTS, LINES, 2 * COLUMNS), jnp.float32), -6.0, 6.0)
    return 0.02 * values


def draw_defocus(key, part):
    focus = shared_fields(key)
    return focus


def draw_images(key, part):
    focus = shared_fields(key)
    row_pos = jnp.arange(LINES).astype(jnp.float32) - LINES // 2
    col_pos = jnp.arange(COLUMNS).astype(jnp.float32)
    halfway = float(LINES // 2)
    radius = (row_pos[:, None] * row_pos[:, None] + col_pos[None, :] * col_pos[None, :]) / (halfway * halfway)
    contrast = jnp.sin(focus[:, None, None] * radius[None] + 0.3)
    factor = jnp.concatenate([contrast, contrast], axis=2)
    values = jnp.clip(jax.random.normal(jax.random.fold_in(key, 303), (PARTICLES, LINES, 2 * COLUMNS), jnp.float32), -6.0, 6.0)
    quarter = PARTICLES // 4
    refs = reference_values(key).astype(jnp.bfloat16).astype(jnp.float32)
    chosen_orient = jax.random.randint(jax.random.fold_in(key, 606), (quarter,), 0, ORIENTS)
    first_class = jax.random.randint(jax.random.fold_in(key, 707), (quarter,), 0, CLASSES)
    step_class = jax.random.randint(jax.random.fold_in(key, 808), (quarter,), 1, CLASSES)
    second_class = (first_class + step_class) % CLASSES
    target = jax.random.uniform(jax.random.fold_in(key, 909), (quarter, 1, 1), jnp.float32, 120.0, 400.0)
    gain_value = target / (float(LINES * 2 * COLUMNS) * 0.00016)
    aligned = refs[first_class, chosen_orient] + refs[second_class, chosen_orient]
    factor_blocks = factor.reshape(quarter, 4, LINES, 2 * COLUMNS)[:, 0]
    aligned = jnp.clip(gain_value * factor_blocks * aligned, -400.0, 400.0)
    values = values.reshape(quarter, 4, LINES, 2 * COLUMNS).at[:, 0].set(aligned)
    return values.reshape(PARTICLES, LINES, 2 * COLUMNS).astype(jnp.bfloat16)


def draw_references(key, part):
    return reference_values(key).astype(jnp.bfloat16)


def with_ends(values, key, least, largest):
    dims = values.shape
    place = [jax.random.randint(jax.random.fold_in(key, axis), (), 0, dims[axis]) for axis in range(len(dims))]
    values = values.at[tuple(place)].set(least)
    longest = dims.index(max(dims))
    place[longest] = (place[longest] + 1) % dims[longest]
    return values.at[tuple(place)].set(largest)


def picks_of(key, rows, number_of, top, lift):
    order = jax.random.permutation(jax.random.fold_in(key, 1), number_of)
    pull = order
    for power in range(3):
        pull = pull * pull // number_of
    pull = pull * lift // number_of
    chance = jax.random.randint(jax.random.fold_in(key, 2), (rows, number_of), 0, 4096) + pull
    fixed_rows = jax.random.permutation(jax.random.fold_in(key, 3), rows)[jnp.arange(number_of) % rows]
    chance = jnp.where(jnp.arange(rows)[:, None] == fixed_rows[None, :], 1 << 14, chance)
    score = chance * number_of + jnp.arange(number_of)
    return lax.top_k(score.astype(jnp.int32), top)[1].astype(jnp.int32)


def deal_out(own_key, own, number, rows, count, top, bound, skew):
    order = jax.random.permutation(own_key, count)
    crowded, usual = load_shares(count, rows * top, bound, skew, True), load_shares(count, rows * top, bound, skew, False)
    places = jnp.arange(count)

    def named(sizes, offset_by):
        used = int((sizes > 0).sum())
        fixed = max(1, used // 4)
        moved = fixed + (places - fixed + offset_by * (used - fixed)) % max(1, count - fixed)
        return jnp.zeros((count,), jnp.int32).at[order[jnp.where(places < fixed, places, moved)]].set(jnp.asarray(sizes, jnp.int32))

    sizes = jnp.where(number % 4 == 0, named(crowded, number // 4), named(usual, number - number // 4 - 1))
    mixed = jax.random.permutation(jax.random.fold_in(own, 3), count)
    donor, taker = mixed[0:count // 2 * 2:2], mixed[1:count // 2 * 2:2]
    slack = jnp.minimum(sizes[donor] - 1, bound - sizes[taker]) // 2
    slack = jnp.where((donor == order[0]) | (taker == order[0]) | (sizes[taker] == 0), 0, jnp.maximum(slack, 0))
    moved = jax.random.randint(jax.random.fold_in(own, 4), (count // 2,), 0, 1 << 20) % (slack + 1)
    sizes = sizes.at[donor].add(-moved).at[taker].add(moved)
    labels = jnp.searchsorted(jnp.cumsum(sizes), jnp.arange(rows * top), side="right").astype(jnp.int32)
    listing = labels.reshape(top, rows).T
    listing = listing[jax.random.permutation(jax.random.fold_in(own, 1), rows)]
    offset_by = jax.random.randint(jax.random.fold_in(own, 2), (rows, 1), 0, top)
    return jnp.take_along_axis(listing, (jnp.arange(top)[None, :] + offset_by) % top, axis=1)


def load_shares(amount, total, limit, lean, full):
    weights = [(1 << 20) // math.isqrt(standing ** lean) + 1 for standing in range(1, amount + 1)]
    largest = limit if full else min(limit, max(-(-total // amount), total * weights[0] // sum(weights)))
    least = 1 if total - largest >= amount - 1 else 0
    holding, rest = [largest] + [least] * (amount - 1), total - largest - least * (amount - 1)
    while rest > 0:
        movable = [i for i in range(1, amount) if holding[i] < largest] or [i for i in range(1, amount) if holding[i] < limit]
        pool, remaining = sum([weights[i] for i in movable]), rest
        for i in movable:
            extra = min(limit - holding[i], max(1, remaining * weights[i] // pool), rest)
            holding[i] = holding[i] + extra
            rest = rest - extra
    return np.array(holding)


def gaussian(stream_key, extent, width, reach, held_as=jnp.bfloat16):
    result = width * jax.random.normal(stream_key, extent, jnp.float32)
    return jnp.clip(result, min=-reach, max=reach).astype(held_as)


def setup_inputs(seed: int = 0) -> dict:
    key_of = jax.random.split(jax.random.key(seed), 11)
    images = draw_images(jax.random.fold_in(key_of[10], 71), 0)
    defocus = draw_defocus(jax.random.fold_in(key_of[10], 71), 0)
    noise_var = jnp.clip(jnp.exp(jax.random.uniform(key_of[2], (LINES, COLUMNS), jnp.float32, math.log(1.0), math.log(4.0))), 1.0, 4.0)
    references = draw_references(jax.random.fold_in(key_of[10], 71), 0)
    orient_list = picks_of(key_of[4], PARTICLES, ORIENTS, LISTED, 4096)
    class_label = with_ends(jax.random.randint(key_of[5], (PARTICLES,), 0, CLASSES), jax.random.fold_in(key_of[5], 1), 0, CLASSES - 1).astype(jnp.int32)
    owner_keys = jax.random.split(jax.random.fold_in(key_of[6], 1), ORIENTS * LINES // BLOCK_ROWS)
    owner_turns = jax.random.permutation(jax.random.fold_in(key_of[6], 3), ORIENTS * LINES // BLOCK_ROWS)
    owner = jax.vmap(lambda own, number: deal_out(jax.random.fold_in(key_of[6], 2), own, number, BLOCK_ROWS, N_DOM, 1, CAPACITY, 2))(owner_keys, owner_turns).reshape((ORIENTS, LINES, 1))
    slab_row = with_ends(jax.random.randint(key_of[7], (ORIENTS, LINES), 0, SLAB_ROWS), jax.random.fold_in(key_of[7], 1), 0, SLAB_ROWS - 1).astype(jnp.int32)
    kernel_index = with_ends(jax.random.randint(key_of[8], (ORIENTS, LINES), 0, KERNELS), jax.random.fold_in(key_of[8], 1), 0, KERNELS - 1).astype(jnp.int32)
    interp = gaussian(key_of[9], (KERNELS, COLUMNS, COLUMNS), COLUMNS ** -0.5, 0.5)
    return dict(images=images, defocus=defocus, noise_var=noise_var, references=references, orient_list=orient_list, class_label=class_label, owner=owner, slab_row=slab_row, kernel_index=kernel_index, interp=interp)


prior_hit = math.log(0.55)
prior_miss = math.log(0.15)
excluded = -1.0e30


def radius_sq(first_line, line_count, line_total, columns):
    row_pos = (first_line + jnp.arange(line_count)).astype(jnp.float32) - (line_total // 2)
    col_pos = jnp.arange(columns).astype(jnp.float32)
    halfway = float(line_total // 2)
    return (row_pos[:, None] * row_pos[:, None] + col_pos[None, :] * col_pos[None, :]) / (halfway * halfway)


def shift_waves(first_line, line_count, line_total, columns):
    row_pos = (first_line + jnp.arange(line_count)).astype(jnp.float32) - (line_total // 2)
    col_pos = jnp.arange(columns).astype(jnp.float32)
    offsets = jnp.arange(9)
    across = (offsets // 3 - 1).astype(jnp.float32)
    upward = (offsets % 3 - 1).astype(jnp.float32)
    phases = math.pi * (across[:, None, None] * col_pos[None, None, :] / columns
                        + upward[:, None, None] * row_pos[None, :, None] / (line_total // 2))
    return jnp.cos(phases), jnp.sin(phases)


def reference(images, defocus, noise_var, references, orient_list, class_label, owner, slab_row, kernel_index, interp):
    row_width = 2 * COLUMNS
    radius = radius_sq(0, LINES, LINES, COLUMNS)
    cosine, sine = shift_waves(0, LINES, LINES, COLUMNS)
    ref_real = references[..., :COLUMNS].astype(jnp.float32)
    ref_imag = references[..., COLUMNS:].astype(jnp.float32)
    ref_power = lax.optimization_barrier((ref_real * ref_real + ref_imag * ref_imag).astype(jnp.bfloat16)).astype(jnp.float32)
    wanted = jnp.arange(ORIENTS).astype(jnp.int32)
    image_blocks = images.reshape(N_DOM, PART_DEV, LINES, row_width)
    focus_blocks = defocus.reshape(N_DOM, PART_DEV)
    list_blocks = orient_list.reshape(N_DOM, PART_DEV, LISTED)
    label_blocks = class_label.reshape(N_DOM, PART_DEV)

    def per_block(accum, block):
        block_images, block_focus, block_list, block_label = block
        contrast = jnp.sin(block_focus[:, None, None] * radius[None] + 0.3)
        factor = contrast / noise_var[None]
        weighted = lax.optimization_barrier(
            (block_images.astype(jnp.float32) * jnp.concatenate([factor, factor], axis=2)).astype(jnp.bfloat16)).astype(jnp.float32)
        ctf_power = lax.optimization_barrier((contrast * factor).astype(jnp.bfloat16)).astype(jnp.float32)
        energy = jnp.einsum("nlc,kolc->nko", ctf_power, ref_power)
        cross_terms = []
        for shift in range(SHIFTS):
            cos_t = cosine[shift]
            sin_t = sine[shift]
            shifted = jnp.concatenate([ref_real * cos_t - ref_imag * sin_t, ref_imag * cos_t + ref_real * sin_t], axis=-1)
            shifted = lax.optimization_barrier(shifted.astype(jnp.bfloat16)).astype(jnp.float32)
            cross_terms.append(jnp.einsum("nlj,kolj->nko", weighted, shifted))
        cross_sum = jnp.stack(cross_terms, axis=1)
        allowed = jnp.any(block_list[:, :, None] == wanted[None, None, :], axis=1)
        prior = jnp.where(block_label[:, None] == jnp.arange(CLASSES).astype(jnp.int32)[None, :], prior_hit, prior_miss)
        score = cross_sum - 0.5 * energy[:, None] + prior[:, None, :, None]
        usable = jnp.broadcast_to(allowed[:, None, None, :], score.shape)
        masked = jnp.where(usable, score, excluded)
        peak_score = jnp.max(masked, axis=(1, 2, 3))
        weights = jnp.where(usable, jnp.exp(masked - peak_score[:, None, None, None]), 0.0)
        total_mass = jnp.sum(weights, axis=(1, 2, 3))
        evidence = peak_score + jnp.log(total_mass)
        posterior = lax.optimization_barrier((weights / total_mass[:, None, None, None]).astype(jnp.bfloat16)).astype(jnp.float32)
        partial_value = jnp.zeros((CLASSES, ORIENTS, LINES, row_width), jnp.float32)
        for shift in range(SHIFTS):
            stacked = jnp.einsum("nko,nlj->kolj", posterior[:, shift], weighted)
            real_part = stacked[..., :COLUMNS]
            imag_part = stacked[..., COLUMNS:]
            cos_t = cosine[shift]
            sin_t = sine[shift]
            partial_value = partial_value + jnp.concatenate([real_part * cos_t + imag_part * sin_t,
                                                 imag_part * cos_t - real_part * sin_t], axis=-1)
        accum = accum + lax.optimization_barrier(partial_value.astype(jnp.bfloat16)).astype(jnp.float32)
        return accum, evidence

    start = jnp.zeros((CLASSES, ORIENTS, LINES, row_width), jnp.float32)
    summed, evidence = lax.scan(per_block, start, (image_blocks, focus_blocks, list_blocks, label_blocks))
    slices = lax.optimization_barrier(summed.astype(jnp.bfloat16)).astype(jnp.float32)
    split = slices.reshape(CLASSES, ORIENTS, LINES, 2, COLUMNS)
    inserted = jnp.zeros((CLASSES, ORIENTS, LINES, 2, COLUMNS), jnp.float32)
    for kernel in range(KERNELS):
        chosen = (kernel_index == kernel)[None, :, :, None, None]
        mapped = jnp.einsum("kolxc,cd->kolxd", split, interp[kernel].astype(jnp.float32))
        inserted = inserted + jnp.where(chosen, mapped, 0.0)
    inserted = lax.optimization_barrier(inserted.astype(jnp.bfloat16)).astype(jnp.float32)
    rows_major = jnp.transpose(inserted, (1, 2, 0, 3, 4)).reshape(ORIENTS * LINES, CLASSES * row_width)
    target = (owner[:, :, 0] * SLAB_ROWS + slab_row).reshape(-1).astype(jnp.int32)
    volume = jax.ops.segment_sum(rows_major, target, num_segments=VOL_ROWS)
    return volume.reshape(VOL_ROWS, CLASSES, row_width), evidence.reshape(PARTICLES)
```

```python
import functools
import math

import jax
import jax.numpy as jnp
import numpy as np
from jax import lax
from jax.experimental import pallas as pl
from jax.experimental.pallas import tpu as pltpu
from jax.sharding import PartitionSpec as P

SLAB_ROWS = 512
LINES = 256
COLS = 128
WIDE = 2 * COLS
N = 192
CL = 4
OG = 8
KO = CL * OG
PL = 16
NP = LINES // PL
PK = PL * WIDE
SIDE = 4
GROUPS = 8
BASES = 9
CAP = 16

prior_hit = math.log(0.55)
prior_miss = math.log(0.15)
excluded = -1e30
MESH = pl.DeviceIdType.MESH
bf16 = jnp.bfloat16
f32 = jnp.float32

ORDER = (
    (0, 0), (0, 1), (0, 3), (1, 0), (3, 0), (1, 1), (1, 3), (3, 1), (3, 3),
    (0, 2), (2, 0), (1, 2), (3, 2), (2, 1), (2, 3), (2, 2),
)


def gather_plan():
    msgs = []
    for first, lo in (("x", 0), ("z", PL // 2)):
        mid, hi = lo + PL // 4, lo + PL // 2
        second = "z" if first == "x" else "x"

        def rel(f, s):
            return (s, f) if first == "x" else (f, s)

        msgs += [(0, rel(0, 0), lo, hi, first, d) for d in (1, -1)]
        msgs += [(1, rel(1, 0), lo, mid, first, -1), (1, rel(3, 0), mid, hi, first, 1)]
        for rank, f in ((0.5, 0), (2, 1), (2, 3), (4, 2)):
            msgs += [(rank, rel(f, 0), lo, hi, second, d) for d in (1, -1)]
            msgs += [
                (rank + 1, rel(f, 1), lo, mid, second, -1),
                (rank + 1, rel(f, 3), mid, hi, second, 1),
            ]
    msgs.sort(key=lambda m: m[0])
    msgs = [m[1:] for m in msgs]

    def landing(m):
        (dz, dx), lo, hi, axis, d = m
        return ((dz, (dx - d) % 4) if axis == "x" else ((dz - d) % 4, dx), lo, hi)

    land = [landing(m) for m in msgs]
    early = {
        1: [(0, 1, 0), (0, 3, 0), (1, 0, 1), (3, 0, 1), (0, 1, 1), (0, 3, 1), (1, 0, 0), (3, 0, 0)],
        3: [(0, 2, 0), (2, 0, 1)],
        5: [(1, 1, 0), (3, 1, 0), (1, 3, 0), (3, 3, 0), (1, 1, 1), (1, 3, 1), (3, 1, 1), (3, 3, 1)],
        10: [(1, 2, 0), (3, 2, 0), (2, 1, 1), (2, 3, 1)],
    }
    have = {((0, 0), line) for line in range(PL)}
    waited, sent, steps = set(), set(), []

    def ready(m):
        return all((m[0], line) in have for line in range(m[1], m[2]))

    for step in range(NP):
        acts = []
        if step == 0:
            for i, m in enumerate(msgs):
                if ready(m):
                    acts.append(("send", i))
                    sent.add(i)
        wanted = [((dz, dx), half) for dz, dx, half in early.get(step, [])]
        wanted += [(ORDER[step], half) for half in (0, 1)] if step else []
        for piece, half in wanted:
            for i, (at, lo, hi) in enumerate(land):
                if at == piece and lo // (PL // 2) == half and i not in waited:
                    waited.add(i)
                    acts.append(("wait", i))
                    have |= {(at, line) for line in range(lo, hi)}
            for i, m in enumerate(msgs):
                if i not in sent and ready(m):
                    acts.append(("send", i))
                    sent.add(i)
        steps.append(acts)
    assert len(waited) == len(msgs) == len(sent)
    return msgs, land, steps


MSGS, LAND, STEPS = gather_plan()


def fine_sin(angle):
    turns = jnp.floor(angle * (1.0 / math.pi) + 0.5)
    x = angle - turns * 3.140625
    x = x - turns * (math.pi - 3.140625)
    odd = turns - 2.0 * jnp.floor(turns * 0.5)
    x2 = x * x
    poly = -1.0 / 39916800.0
    for c in (1.0 / 362880.0, -1.0 / 5040.0, 1.0 / 120.0, -1.0 / 6.0):
        poly = poly * x2 + c
    s = x + x * x2 * poly
    return s * (1.0 - 2.0 * odd)


def pick(step, values):
    out = jnp.int32(0)
    for i, v in enumerate(values):
        if v:
            out = out + jnp.where(step == i, v, 0)
    return out


def score_kernel(
    refs_ref, images_hbm, focus_ref, noise_ref, list_ref, label_ref, rowtab_ref, offs_ref, coltab_ref, lines_ref,
    post_ref, evid_ref, weighted_hbm,
    refs_all, ibuf, fre, fim, wbuf, cbuf, sbuf, rbuf, acc, eacc, colsin, colcos, angtab, sc, stats,
    send_sem, recv_sem, ssend_sem, srecv_sem, in_sem, out_sem,
):
    dom = lax.axis_index("dom")
    group = lax.axis_index("orient")
    z, x = dom // SIDE, dom % SIDE

    def origin(dz, dx):
        return ((z + dz) % SIDE) * SIDE + (x + dx) % SIDE

    def step_origin(step):
        return origin(pick(step, [o[0] for o in ORDER]), pick(step, [o[1] for o in ORDER]))

    def image_copy(step):
        lines = pl.ds(pl.multiple_of(step_origin(step) * PL, PL), PL)
        return pltpu.make_async_copy(images_hbm.at[:, lines, :], ibuf.at[step % 2], in_sem.at[step % 2])

    def weighted_copy(step):
        return pltpu.make_async_copy(wbuf.at[step % 2], weighted_hbm.at[step_origin(step)], out_sem.at[step % 2])

    image_copy(0).start()

    barrier = pltpu.get_barrier_semaphore()
    for dz, dx in ((0, 1), (0, 3), (1, 0), (3, 0)):
        pl.semaphore_signal(barrier, inc=1, device_id=(origin(dz, dx), group), device_id_type=MESH)
    for k in range(1, GROUPS):
        pl.semaphore_signal(barrier, inc=1, device_id=(dom, (group + k) % GROUPS), device_id_type=MESH)
    pl.semaphore_wait(barrier, 4 + GROUPS - 1)

    def message(i):
        (dz, dx), lo, hi, axis, d = MSGS[i]
        to = origin(0, d % 4) if axis == "x" else origin(d % 4, 0)
        at = origin(dz, dx)
        rows = refs_all.at[at, pl.ds(lo, hi - lo)]
        src = refs_ref.at[pl.ds(lo, hi - lo)] if (dz, dx) == (0, 0) else rows
        return pltpu.make_async_remote_copy(
            src_ref=src, dst_ref=rows, send_sem=send_sem.at[i], recv_sem=recv_sem.at[i],
            device_id=(to, group), device_id_type=MESH,
        )

    def arrival(i):
        (dz, dx), lo, hi = LAND[i]
        rows = refs_all.at[origin(dz, dx), pl.ds(lo, hi - lo)]
        axis, d = MSGS[i][3:]
        frm = origin(0, -d % 4) if axis == "x" else origin(-d % 4, 0)
        return pltpu.make_async_remote_copy(
            src_ref=rows, dst_ref=rows, send_sem=send_sem.at[i], recv_sem=recv_sem.at[i],
            device_id=(frm, group), device_id_type=MESH,
        )

    def traffic(acts):
        for kind, i in acts:
            if kind == "send":
                message(i).start()
            else:
                arrival(i).wait_recv()

    traffic(STEPS[0])
    refs_all[dom] = refs_ref[...]
    focus = focus_ref[...]
    colang = focus[:, 0:1] * coltab_ref[0:1, :]
    colsin[...] = fine_sin(colang)
    colcos[...] = fine_sin(colang + math.pi / 2)
    acc[...] = jnp.zeros_like(acc)
    eacc[...] = jnp.zeros_like(eacc)

    def one_share(step, carry):
        for i in range(1, NP):
            if STEPS[i]:
                pl.when(step == i)(functools.partial(traffic, STEPS[i]))
        share = step_origin(step)
        slot = step % 2
        pl.when(step + 1 < NP)(lambda: image_copy(step + 1).start())
        angtab[...] = fine_sin(focus_ref[...] * rowtab_ref[share, 0:1, :] + offs_ref[0:1, :])
        image_copy(step).wait()

        def widen(i, c):
            part = ibuf[slot, pl.ds(pl.multiple_of(i * 8, 8), 8)].astype(f32)
            part = part.reshape(128, WIDE)
            rows = pl.ds(pl.multiple_of(i * 128, 128), 128)
            fre[rows, :] = part[:, :COLS]
            fim[rows, :] = part[:, COLS:]
            return c

        lax.fori_loop(0, N // 8, widen, 0)
        pl.when(step >= 2)(lambda: weighted_copy(step - 2).wait())

        def weigh(i, c):
            rows = pl.ds(pl.multiple_of(i * 32, 32), 32)
            cs, cc = colsin[rows, :], colcos[rows, :]
            ang = angtab[rows, :]
            for j in range(PL):
                inv = 1.0 / noise_ref[share, j : j + 1, :]
                con = ang[:, j : j + 1] * cc + ang[:, PL + j : PL + j + 1] * cs
                fac = con * inv
                take = pl.ds(i * (32 * PL) + j, 32, stride=PL)
                wbuf[slot, rows, j * WIDE : j * WIDE + COLS] = (fre[take, :] * fac).astype(bf16)
                wbuf[slot, rows, j * WIDE + COLS : (j + 1) * WIDE] = (fim[take, :] * fac).astype(bf16)
                cbuf[rows, j * COLS : (j + 1) * COLS] = (con * fac).astype(bf16)
            return c

        lax.fori_loop(0, N // 32, weigh, 0)
        weighted_copy(step).start()

        ca, sa = coltab_ref[1:2, :], coltab_ref[2:3, :]
        for j in range(PL):
            ref = refs_all[share, j].astype(f32)
            re, im = ref[:, :COLS], ref[:, COLS:]
            cp, sp = lines_ref[share, j : j + 1, :], lines_ref[share, PL + j : PL + j + 1, :]
            rbuf[:, j * COLS : (j + 1) * COLS] = (re * re + im * im).astype(bf16)
            for a, (r, m) in enumerate(((re, im), (re * ca, im * ca), (im * -sa, re * sa))):
                for b, (r2, m2) in enumerate(((r, m), (r * cp, m * cp), (m * -sp, r * sp))):
                    at = (a * 3 + b) * KO
                    sbuf[at : at + KO, j * WIDE : j * WIDE + COLS] = r2.astype(bf16)
                    sbuf[at : at + KO, j * WIDE + COLS : (j + 1) * WIDE] = m2.astype(bf16)
        nt = (((1,), (1,)), ((), ()))
        acc[...] += lax.dot_general(sbuf[...], wbuf[slot], nt, preferred_element_type=f32)
        eacc[...] += lax.dot_general(rbuf[...], cbuf[...], nt, preferred_element_type=f32)
        return carry

    lax.fori_loop(0, NP, one_share, 0)

    def band(ref, i):
        return ref[i * KO : (i + 1) * KO, :]

    row = lax.broadcasted_iota(jnp.int32, (KO, N), 0)
    wanted = group * OG + row // CL
    hits = jnp.zeros((KO, N), f32)
    for j in range(list_ref.shape[0]):
        hits = jnp.where(list_ref[j : j + 1, :] == wanted, 1.0, hits)
    usable = hits > 0.5
    base = jnp.where(label_ref[0:1, :] == row % CL, prior_hit, prior_miss) - 0.5 * eacc[...]
    xs = [[band(acc, a * 3 + b) for b in range(3)] for a in range(3)]
    peak = jnp.full((KO, N), excluded, f32)
    for t in range(BASES):
        a, b = t // 3 - 1, t % 3 - 1

        def along(row_):
            return row_[0] if b == 0 else row_[1] + b * row_[2]

        cross = along(xs[0]) if a == 0 else along(xs[1]) + a * along(xs[2])
        score = jnp.where(usable, cross + base, excluded)
        sc[t * KO : (t + 1) * KO, :] = score
        peak = jnp.maximum(peak, score)
    peak = jnp.max(peak, axis=0, keepdims=True)
    mass = jnp.zeros((KO, N), f32)
    for t in range(BASES):
        mass = mass + jnp.where(usable, jnp.exp(band(sc, t) - peak), 0.0)
    mass = jnp.sum(mass, axis=0, keepdims=True)
    stats[group, 0:8, :] = jnp.broadcast_to(peak, (8, N))
    stats[group, 8:16, :] = jnp.broadcast_to(mass, (8, N))

    def stat_copy(k, slot_group, to):
        mine = stats.at[slot_group]
        return pltpu.make_async_remote_copy(
            src_ref=mine, dst_ref=mine, send_sem=ssend_sem.at[k], recv_sem=srecv_sem.at[k],
            device_id=(dom, to), device_id_type=MESH,
        )

    for k in range(1, GROUPS):
        stat_copy(k, group, (group + k) % GROUPS).start()
    for k in range(1, GROUPS):
        frm = (group + GROUPS - k) % GROUPS
        stat_copy(k, frm, frm).wait_recv()
    top = stats[0, 0:1, :]
    for g in range(1, GROUPS):
        top = jnp.maximum(top, stats[g, 0:1, :])
    total = jnp.zeros((1, N), f32)
    for g in range(GROUPS):
        total = total + stats[g, 8:9, :] * jnp.exp(stats[g, 0:1, :] - top)
    evid_ref[...] = top + jnp.log(total)
    scale = 1.0 / total
    ps = [
        [jnp.where(usable, jnp.exp(band(sc, a * 3 + b) - top) * scale, 0.0) for b in range(3)]
        for a in range(3)
    ]
    basis = []
    for less, none, more in ps:
        basis.append((none, more + less, more - less))
    for b in range(3):
        less, none, more = basis[0][b], basis[1][b], basis[2][b]
        for a, v in enumerate((none, more + less, more - less)):
            post_ref[(a * 3 + b) * KO : (a * 3 + b + 1) * KO, :] = v.astype(bf16)

    weighted_copy(NP - 2).wait()
    weighted_copy(NP - 1).wait()
    for i in range(len(MSGS)):
        message(i).wait_send()
    for k in range(1, GROUPS):
        stat_copy(k, group, (group + k) % GROUPS).wait_send()


CHUNKS = 4
ROWS = 32 * CL
HALF = ROWS // 2
QUART = ROWS // 4


def back_kernel(
    post_ref, weighted_hbm, coltab_ref, lines_ref,
    out_ref,
    wbuf, part, r1, r2, p2, q1, q2,
    in_sem, send_sem, recv_sem,
):
    dom = lax.axis_index("dom")
    group = lax.axis_index("orient")
    z, x = dom // SIDE, dom % SIDE

    def neighbour(axis, d):
        return z * SIDE + (x + d) % SIDE if axis == "x" else ((z + d) % SIDE) * SIDE + x

    def share_of(i):
        return 2 * (i // 4) + i % 2 + 8 * ((i % 4) // 2)

    def load(i):
        return pltpu.make_async_copy(weighted_hbm.at[share_of(i)], wbuf.at[i % 3], in_sem.at[i % 3])

    load(0).start()
    load(1).start()
    barrier = pltpu.get_barrier_semaphore()
    for axis in ("x", "z"):
        for d in (1, 3):
            pl.semaphore_signal(barrier, inc=1, device_id=(neighbour(axis, d), group), device_id_type=MESH)
    pl.semaphore_wait(barrier, 4)

    ca, sa = coltab_ref[1:2, :], coltab_ref[2:3, :]

    def compute(i):
        load(i).wait()
        pl.when(i + 2 < NP)(lambda: load(i + 2).start())
        chunk, half, share = i // 4, (i % 4) // 2, share_of(i)
        for four in range(PL // 4):
            outs = []
            for j in range(four * 4, four * 4 + 4):
                g = jnp.dot(
                    post_ref[...], wbuf[i % 3, :, j * WIDE : (j + 1) * WIDE], preferred_element_type=f32
                )
                cp, sp = lines_ref[share, j : j + 1, :], lines_ref[share, PL + j : PL + j + 1, :]
                vs = []
                for a in range(3):
                    g0, gc, gs = (g[(a * 3 + b) * KO : (a * 3 + b + 1) * KO, :] for b in range(3))
                    vs.append(
                        (
                            g0[:, :COLS] + gc[:, :COLS] * cp + gs[:, COLS:] * sp,
                            g0[:, COLS:] + gc[:, COLS:] * cp - gs[:, :COLS] * sp,
                        )
                    )
                outs.append(
                    jnp.concatenate(
                        [
                            vs[0][0] + vs[1][0] * ca + vs[2][1] * sa,
                            vs[0][1] + vs[1][1] * ca - vs[2][0] * sa,
                        ],
                        axis=1,
                    )
                )
            row = pl.multiple_of((i % 2) * (PL * CL) + four * 16, 16)
            for o in range(OG):
                piece = jnp.concatenate([v[o * CL : (o + 1) * CL, :] for v in outs], axis=0)
                part[chunk, o // 2, (o % 2) * 2 + half, pl.ds(row, 16), :] = piece.astype(bf16)

    def setup(h):
        first, second = ("x", "z") if h == 0 else ("z", "x")
        return (first, x, second, z) if h == 0 else (first, z, second, x)

    def column(c, h, f, lo, size):
        rows = pl.ds(h * HALF + lo, size)
        return part.at[c, :, f, rows, :] if h == 0 else part.at[c, f, :, rows, :]

    def copy(src, dst, c, idx, axis, d):
        return pltpu.make_async_remote_copy(
            src_ref=src, dst_ref=dst, send_sem=send_sem.at[c, idx], recv_sem=recv_sem.at[c, idx],
            device_id=(neighbour(axis, d), group), device_id_type=MESH,
        )

    def copies(c, h, stage):
        first, f, second, s = setup(h)
        far_f, far_s = (f + 2) % 4, (s + 2) % 4
        out = []
        for n_, d in enumerate((3, 1)):
            idx = (h * 4 + stage) * 2 + n_
            if stage == 0:
                out.append(copy(column(c, h, far_f, n_ * QUART, QUART), r1.at[c, h, n_], c, idx, first, d))
            elif stage == 1:
                out.append(copy(column(c, h, (f + d) % 4, 0, HALF), r2.at[c, h, n_], c, idx, first, d))
            elif stage == 2:
                src = p2.at[c, h, far_s, pl.ds(n_ * QUART, QUART), :]
                out.append(copy(src, q1.at[c, h, n_], c, idx, second, d))
            else:
                out.append(copy(p2.at[c, h, (s + d) % 4], q2.at[c, h, n_], c, idx, second, d))
        return out

    def column_get(c, h, f, i, lo, size):
        rows = pl.ds(h * HALF + lo, size)
        return part[c, i, f, rows, :] if h == 0 else part[c, f, i, rows, :]

    def column_set(c, h, f, i, lo, size, value):
        rows = pl.ds(h * HALF + lo, size)
        if h == 0:
            part[c, i, f, rows, :] = value
        else:
            part[c, f, i, rows, :] = value

    def advance(c, stage):
        for h in (0, 1):
            first, f, second, s = setup(h)
            if stage > 0:
                for cp_ in copies(c, h, stage - 1):
                    cp_.wait_recv()
            if stage == 1:
                for n_, d in enumerate((3, 1)):
                    for i in range(SIDE):
                        to = (f + d) % 4
                        mine = column_get(c, h, to, i, n_ * QUART, QUART).astype(f32)
                        new = mine + r1[c, h, n_, i].astype(f32)
                        column_set(c, h, to, i, n_ * QUART, QUART, new.astype(bf16))
            elif stage == 2:
                for i in range(SIDE):
                    new = column_get(c, h, f, i, 0, HALF).astype(f32)
                    new = new + r2[c, h, 0, i].astype(f32) + r2[c, h, 1, i].astype(f32)
                    p2[c, h, i] = new.astype(bf16)
            elif stage == 3:
                for n_, d in enumerate((3, 1)):
                    rows = pl.ds(n_ * QUART, QUART)
                    to = (s + d) % 4
                    new = p2[c, h, to, rows, :].astype(f32) + q1[c, h, n_].astype(f32)
                    p2[c, h, to, rows, :] = new.astype(bf16)
            elif stage == 4:
                new = p2[c, h, s].astype(f32) + q2[c, h, 0].astype(f32) + q2[c, h, 1].astype(f32)
                out_ref[pl.ds(pl.multiple_of(c * ROWS, ROWS) + h * HALF, HALF), :] = new.astype(bf16)
            if stage < 4:
                for cp_ in copies(c, h, stage):
                    cp_.start()

    def tick(t, carry):
        @pl.when(t < CHUNKS)
        def _():
            def body(q, c):
                compute(t * 4 + q)
                return c

            lax.fori_loop(0, 4, body, 0)

        for stage in range(5):
            c = t - stage
            pl.when((c >= 0) & (c < CHUNKS))(functools.partial(advance, c, stage))
        return carry

    lax.fori_loop(0, CHUNKS + 4, tick, 0)
    for c in range(CHUNKS):
        for h in (0, 1):
            for stage in range(4):
                for cp_ in copies(c, h, stage):
                    cp_.wait_send()


VM = pl.BlockSpec(memory_space=pltpu.VMEM)
ANY = pl.BlockSpec(memory_space=pl.ANY)


def constants():
    c = np.arange(COLS, dtype=np.float32)
    l = np.arange(LINES, dtype=np.float32) - LINES // 2
    half = float(LINES // 2)
    coltab = np.zeros((8, COLS), np.float32)
    coltab[0] = c * c / (half * half)
    coltab[1] = np.cos(math.pi * c / COLS)
    coltab[2] = np.sin(math.pi * c / COLS)
    rowtab = np.zeros((NP, 8, COLS), np.float32)
    rsq = (l * l / (half * half)).reshape(NP, 1, PL)
    rowtab[:, :, :PL] = rsq
    rowtab[:, :, PL : 2 * PL] = rsq
    offs = np.zeros((8, COLS), np.float32)
    offs[:, :PL] = 0.3
    offs[:, PL : 2 * PL] = 0.3 + math.pi / 2
    ang = (math.pi * l / half).reshape(NP, PL, 1)
    lines = np.concatenate([np.cos(ang), np.sin(ang)], axis=1)
    lines = np.broadcast_to(lines, (NP, 2 * PL, COLS)).astype(np.float32)
    return coltab, rowtab, offs, lines


def shards(
    images, defocus, noise_var, references, orient_list, class_label, owner, slab_row, kernel_index, interp
):
    coltab, rowtab, offs, lines = (jnp.asarray(a) for a in constants())
    refs = jnp.transpose(references, (2, 1, 0, 3)).reshape(PL, KO, WIDE)
    focus = jnp.broadcast_to(defocus[:, None], (N, COLS))
    labels = jnp.broadcast_to(class_label[None, :], (8, N))
    post, evidence, weighted = pl.pallas_call(
        score_kernel,
        out_shape=(
            jax.ShapeDtypeStruct((BASES * KO, N), bf16),
            jax.ShapeDtypeStruct((1, N), f32),
            jax.ShapeDtypeStruct((NP, N, PK), bf16),
        ),
        in_specs=[VM, ANY] + [VM] * 8,
        out_specs=(VM, VM, ANY),
        scratch_shapes=[
            pltpu.VMEM((NP, PL, KO, WIDE), bf16),
            pltpu.VMEM((2, N, PL, WIDE), bf16),
            pltpu.VMEM((N * PL, COLS), f32),
            pltpu.VMEM((N * PL, COLS), f32),
            pltpu.VMEM((2, N, PK), bf16),
            pltpu.VMEM((N, PL * COLS), bf16),
            pltpu.VMEM((BASES * KO, PK), bf16),
            pltpu.VMEM((KO, PL * COLS), bf16),
            pltpu.VMEM((BASES * KO, N), f32),
            pltpu.VMEM((KO, N), f32),
            pltpu.VMEM((N, COLS), f32),
            pltpu.VMEM((N, COLS), f32),
            pltpu.VMEM((N, COLS), f32),
            pltpu.VMEM((BASES * KO, N), f32),
            pltpu.VMEM((GROUPS, 16, N), f32),
            pltpu.SemaphoreType.DMA((len(MSGS),)),
            pltpu.SemaphoreType.DMA((len(MSGS),)),
            pltpu.SemaphoreType.DMA((GROUPS,)),
            pltpu.SemaphoreType.DMA((GROUPS,)),
            pltpu.SemaphoreType.DMA((2,)),
            pltpu.SemaphoreType.DMA((2,)),
        ],
        compiler_params=pltpu.CompilerParams(
            collective_id=0, has_side_effects=True, vmem_limit_bytes=40 * 2**20
        ),
    )(
        refs, images, focus, noise_var.reshape(NP, PL, COLS), orient_list.T, labels, rowtab, offs, coltab, lines
    )
    block = pl.pallas_call(
        back_kernel,
        out_shape=jax.ShapeDtypeStruct((CHUNKS * ROWS, WIDE), bf16),
        in_specs=[VM, ANY, VM, VM],
        out_specs=VM,
        scratch_shapes=[
            pltpu.VMEM((3, N, PK), bf16),
            pltpu.VMEM((CHUNKS, SIDE, SIDE, ROWS, WIDE), bf16),
            pltpu.VMEM((CHUNKS, 2, 2, SIDE, QUART, WIDE), bf16),
            pltpu.VMEM((CHUNKS, 2, 2, SIDE, HALF, WIDE), bf16),
            pltpu.VMEM((CHUNKS, 2, SIDE, HALF, WIDE), bf16),
            pltpu.VMEM((CHUNKS, 2, 2, QUART, WIDE), bf16),
            pltpu.VMEM((CHUNKS, 2, 2, HALF, WIDE), bf16),
            pltpu.SemaphoreType.DMA((3,)),
            pltpu.SemaphoreType.DMA((CHUNKS, 16)),
            pltpu.SemaphoreType.DMA((CHUNKS, 16)),
        ],
        compiler_params=pltpu.CompilerParams(
            collective_id=1, has_side_effects=True, vmem_limit_bytes=40 * 2**20
        ),
    )(post, weighted, coltab, lines)

    group = lax.axis_index("orient")
    dom = lax.axis_index("dom")
    half_lines = LINES // 2

    def group_rows(a):
        return lax.dynamic_slice_in_dim(a, group * OG, OG, 0).reshape(NP, half_lines)

    owners, slabs, kernels = group_rows(owner[:, :, 0]), group_rows(slab_row), group_rows(kernel_index)
    mine = lax.dynamic_slice_in_dim(kernels, dom, 1, 0)[0]
    rows = block.reshape(half_lines, CL * 2, COLS)
    every = jnp.einsum("rxc,wcd->rwxd", rows, interp, preferred_element_type=f32)
    inserted = jnp.zeros(rows.shape, f32)
    for w in range(interp.shape[0]):
        inserted = jnp.where((mine == w)[:, None, None], every[:, w], inserted)
    inserted = inserted.astype(bf16).reshape(half_lines, CL * WIDE)
    earlier = np.tril(np.ones((half_lines, half_lines), bool), -1)
    rank = jnp.sum((owners[:, :, None] == owners[:, None, :]) & earlier[None], axis=2).astype(jnp.int32)
    own_mine = lax.dynamic_slice_in_dim(owners, dom, 1, 0)[0]
    rank_mine = lax.dynamic_slice_in_dim(rank, dom, 1, 0)[0]
    slot_ids = jnp.arange(NP * CAP)
    sendmap = ((own_mine * CAP + rank_mine)[None, :] == slot_ids[:, None]).astype(bf16)
    outgoing = jnp.dot(sendmap, inserted, preferred_element_type=f32).astype(bf16)
    received = lax.all_to_all(outgoing, "dom", 0, 0, tiled=True)
    live = (owners[:, None, :] == dom) & (rank[:, None, :] == jnp.arange(CAP)[None, :, None])
    target = jnp.max(jnp.where(live, slabs[:, None, :], -1), axis=2).reshape(-1)
    placement = (target[None, :] == jnp.arange(SLAB_ROWS)[:, None]).astype(bf16)
    slab = jnp.dot(placement, received, preferred_element_type=f32)
    slab = slab.reshape(SLAB_ROWS, CL, WIDE).astype(bf16)
    volume = lax.psum_scatter(slab, "orient", scatter_dimension=0, tiled=True).astype(f32)
    return volume, evidence.reshape(N)


def solution(mesh):
    return jax.shard_map(
        shards,
        mesh=mesh,
        in_specs=(
            P("dom", None, None),
            P("dom"),
            P(),
            P(None, "orient", "dom", None),
            P("dom", None),
            P("dom"),
            P(),
            P(),
            P(),
            P(),
        ),
        out_specs=(P(("dom", "orient"), None, None), P("dom")),
        check_vma=False,
    )
```

```python
import functools
import math

import jax
import jax.numpy as jnp
import numpy as np
from jax import lax
from jax.experimental import pallas as pl
from jax.experimental.pallas import tpu as pltpu
from jax.sharding import PartitionSpec as P

SLAB_ROWS = 512
LINES = 256
COLS = 128
WIDE = 2 * COLS
N = 192
CL = 4
OG = 8
KO = CL * OG
PL = 16
NP = LINES // PL
PK = PL * WIDE
SIDE = 4
GROUPS = 8
BASES = 9
CAP = 16

prior_hit = math.log(0.55)
prior_miss = math.log(0.15)
excluded = -1e30
MESH = pl.DeviceIdType.MESH
bf16 = jnp.bfloat16
f32 = jnp.float32

ORDER = (
    (0, 0), (0, 1), (0, 3), (1, 0), (3, 0), (1, 1), (1, 3), (3, 1), (3, 3),
    (0, 2), (2, 0), (1, 2), (3, 2), (2, 1), (2, 3), (2, 2),
)


def gather_plan():
    msgs = []
    for first, lo in (("x", 0), ("z", PL // 2)):
        mid, hi = lo + PL // 4, lo + PL // 2
        second = "z" if first == "x" else "x"

        def rel(f, s):
            return (s, f) if first == "x" else (f, s)

        msgs += [(0, rel(0, 0), lo, hi, first, d) for d in (1, -1)]
        msgs += [(1, rel(1, 0), lo, mid, first, -1), (1, rel(3, 0), mid, hi, first, 1)]
        for rank, f in ((0.5, 0), (2, 1), (2, 3), (4, 2)):
            msgs += [(rank, rel(f, 0), lo, hi, second, d) for d in (1, -1)]
            msgs += [
                (rank + 1, rel(f, 1), lo, mid, second, -1),
                (rank + 1, rel(f, 3), mid, hi, second, 1),
            ]
    msgs.sort(key=lambda m: m[0])
    msgs = [m[1:] for m in msgs]

    def landing(m):
        (dz, dx), lo, hi, axis, d = m
        return ((dz, (dx - d) % 4) if axis == "x" else ((dz - d) % 4, dx), lo, hi)

    land = [landing(m) for m in msgs]
    early = {
        1: [(0, 1, 0), (0, 3, 0), (1, 0, 1), (3, 0, 1), (0, 1, 1), (0, 3, 1), (1, 0, 0), (3, 0, 0)],
        3: [(0, 2, 0), (2, 0, 1)],
        5: [(1, 1, 0), (3, 1, 0), (1, 3, 0), (3, 3, 0), (1, 1, 1), (1, 3, 1), (3, 1, 1), (3, 3, 1)],
        10: [(1, 2, 0), (3, 2, 0), (2, 1, 1), (2, 3, 1)],
    }
    have = {((0, 0), line) for line in range(PL)}
    waited, sent, steps = set(), set(), []

    def ready(m):
        return all((m[0], line) in have for line in range(m[1], m[2]))

    for step in range(NP):
        acts = []
        if step == 0:
            for i, m in enumerate(msgs):
                if ready(m):
                    acts.append(("send", i))
                    sent.add(i)
        wanted = [((dz, dx), half) for dz, dx, half in early.get(step, [])]
        wanted += [(ORDER[step], half) for half in (0, 1)] if step else []
        for piece, half in wanted:
            for i, (at, lo, hi) in enumerate(land):
                if at == piece and lo // (PL // 2) == half and i not in waited:
                    waited.add(i)
                    acts.append(("wait", i))
                    have |= {(at, line) for line in range(lo, hi)}
            for i, m in enumerate(msgs):
                if i not in sent and ready(m):
                    acts.append(("send", i))
                    sent.add(i)
        steps.append(acts)
    assert len(waited) == len(msgs) == len(sent)
    return msgs, land, steps


MSGS, LAND, STEPS = gather_plan()


def fine_sin(angle):
    turns = jnp.floor(angle * (1.0 / math.pi) + 0.5)
    x = angle - turns * 3.140625
    x = x - turns * (math.pi - 3.140625)
    odd = turns - 2.0 * jnp.floor(turns * 0.5)
    x2 = x * x
    poly = -1.0 / 39916800.0
    for c in (1.0 / 362880.0, -1.0 / 5040.0, 1.0 / 120.0, -1.0 / 6.0):
        poly = poly * x2 + c
    s = x + x * x2 * poly
    return s * (1.0 - 2.0 * odd)


def pick(step, values):
    out = jnp.int32(0)
    for i, v in enumerate(values):
        if v:
            out = out + jnp.where(step == i, v, 0)
    return out


def score_kernel(
    refs_ref, images_hbm, focus_ref, noise_ref, list_ref, label_ref, rowtab_ref, offs_ref, coltab_ref, lines_ref,
    post_ref, evid_ref, weighted_hbm,
    refs_all, ibuf, fre, fim, wbuf, cbuf, sbuf, rbuf, acc, eacc, colsin, colcos, angtab, sc, stats,
    send_sem, recv_sem, ssend_sem, srecv_sem, in_sem, out_sem,
):
    dom = lax.axis_index("dom")
    group = lax.axis_index("orient")
    z, x = dom // SIDE, dom % SIDE

    def origin(dz, dx):
        return ((z + dz) % SIDE) * SIDE + (x + dx) % SIDE

    def step_origin(step):
        return origin(pick(step, [o[0] for o in ORDER]), pick(step, [o[1] for o in ORDER]))

    def image_copy(step):
        lines = pl.ds(pl.multiple_of(step_origin(step) * PL, PL), PL)
        return pltpu.make_async_copy(images_hbm.at[:, lines, :], ibuf.at[step % 2], in_sem.at[step % 2])

    def weighted_copy(step):
        return pltpu.make_async_copy(wbuf.at[step % 2], weighted_hbm.at[step_origin(step)], out_sem.at[step % 2])

    image_copy(0).start()

    barrier = pltpu.get_barrier_semaphore()
    for dz, dx in ((0, 1), (0, 3), (1, 0), (3, 0)):
        pl.semaphore_signal(barrier, inc=1, device_id=(origin(dz, dx), group), device_id_type=MESH)
    for k in range(1, GROUPS):
        pl.semaphore_signal(barrier, inc=1, device_id=(dom, (group + k) % GROUPS), device_id_type=MESH)
    pl.semaphore_wait(barrier, 4 + GROUPS - 1)

    def message(i):
        (dz, dx), lo, hi, axis, d = MSGS[i]
        to = origin(0, d % 4) if axis == "x" else origin(d % 4, 0)
        at = origin(dz, dx)
        rows = refs_all.at[at, pl.ds(lo, hi - lo)]
        src = refs_ref.at[pl.ds(lo, hi - lo)] if (dz, dx) == (0, 0) else rows
        return pltpu.make_async_remote_copy(
            src_ref=src, dst_ref=rows, send_sem=send_sem.at[i], recv_sem=recv_sem.at[i],
            device_id=(to, group), device_id_type=MESH,
        )

    def arrival(i):
        (dz, dx), lo, hi = LAND[i]
        rows = refs_all.at[origin(dz, dx), pl.ds(lo, hi - lo)]
        axis, d = MSGS[i][3:]
        frm = origin(0, -d % 4) if axis == "x" else origin(-d % 4, 0)
        return pltpu.make_async_remote_copy(
            src_ref=rows, dst_ref=rows, send_sem=send_sem.at[i], recv_sem=recv_sem.at[i],
            device_id=(frm, group), device_id_type=MESH,
        )

    def traffic(acts):
        for kind, i in acts:
            if kind == "send":
                message(i).start()
            else:
                arrival(i).wait_recv()

    traffic(STEPS[0])
    refs_all[dom] = refs_ref[...]
    focus = focus_ref[...]
    colang = focus[:, 0:1] * coltab_ref[0:1, :]
    colsin[...] = fine_sin(colang)
    colcos[...] = fine_sin(colang + math.pi / 2)
    acc[...] = jnp.zeros_like(acc)
    eacc[...] = jnp.zeros_like(eacc)

    def one_share(step, carry):
        for i in range(1, NP):
            if STEPS[i]:
                pl.when(step == i)(functools.partial(traffic, STEPS[i]))
        share = step_origin(step)
        slot = step % 2
        pl.when(step + 1 < NP)(lambda: image_copy(step + 1).start())
        angtab[...] = fine_sin(focus_ref[...] * rowtab_ref[share, 0:1, :] + offs_ref[0:1, :])
        image_copy(step).wait()

        def widen(i, c):
            part = ibuf[slot, pl.ds(pl.multiple_of(i * 8, 8), 8)].astype(f32)
            part = part.reshape(128, WIDE)
            rows = pl.ds(pl.multiple_of(i * 128, 128), 128)
            fre[rows, :] = part[:, :COLS]
            fim[rows, :] = part[:, COLS:]
            return c

        lax.fori_loop(0, N // 8, widen, 0)
        pl.when(step >= 2)(lambda: weighted_copy(step - 2).wait())

        def weigh(i, c):
            rows = pl.ds(pl.multiple_of(i * 32, 32), 32)
            cs, cc = colsin[rows, :], colcos[rows, :]
            ang = angtab[rows, :]
            for j in range(PL):
                inv = 1.0 / noise_ref[share, j : j + 1, :]
                con = ang[:, j : j + 1] * cc + ang[:, PL + j : PL + j + 1] * cs
                fac = con * inv
                take = pl.ds(i * (32 * PL) + j, 32, stride=PL)
                wbuf[slot, rows, j * WIDE : j * WIDE + COLS] = (fre[take, :] * fac).astype(bf16)
                wbuf[slot, rows, j * WIDE + COLS : (j + 1) * WIDE] = (fim[take, :] * fac).astype(bf16)
                cbuf[rows, j * COLS : (j + 1) * COLS] = (con * fac).astype(bf16)
            return c

        lax.fori_loop(0, N // 32, weigh, 0)
        weighted_copy(step).start()

        ca, sa = coltab_ref[1:2, :], coltab_ref[2:3, :]
        for j in range(PL):
            ref = refs_all[share, j].astype(f32)
            re, im = ref[:, :COLS], ref[:, COLS:]
            cp, sp = lines_ref[share, j : j + 1, :], lines_ref[share, PL + j : PL + j + 1, :]
            rbuf[:, j * COLS : (j + 1) * COLS] = (re * re + im * im).astype(bf16)
            for a, (r, m) in enumerate(((re, im), (re * ca, im * ca), (im * -sa, re * sa))):
                for b, (r2, m2) in enumerate(((r, m), (r * cp, m * cp), (m * -sp, r * sp))):
                    at = (a * 3 + b) * KO
                    sbuf[at : at + KO, j * WIDE : j * WIDE + COLS] = r2.astype(bf16)
                    sbuf[at : at + KO, j * WIDE + COLS : (j + 1) * WIDE] = m2.astype(bf16)
        nt = (((1,), (1,)), ((), ()))
        acc[...] += lax.dot_general(sbuf[...], wbuf[slot], nt, preferred_element_type=f32)
        eacc[...] += lax.dot_general(cbuf[...], rbuf[...], nt, preferred_element_type=f32)
        return carry

    lax.fori_loop(0, NP, one_share, 0)

    def band(ref, i):
        return ref[i * KO : (i + 1) * KO, :]

    row = lax.broadcasted_iota(jnp.int32, (KO, N), 0)
    wanted = group * OG + row // CL
    hits = jnp.zeros((KO, N), f32)
    for j in range(list_ref.shape[0]):
        hits = jnp.where(list_ref[j : j + 1, :] == wanted, 1.0, hits)
    usable = hits > 0.5
    base = jnp.where(label_ref[0:1, :] == row % CL, prior_hit, prior_miss) - 0.5 * jnp.transpose(eacc[...])
    xs = [[band(acc, a * 3 + b) for b in range(3)] for a in range(3)]
    peak = jnp.full((KO, N), excluded, f32)
    for t in range(BASES):
        a, b = t // 3 - 1, t % 3 - 1

        def along(row_):
            return row_[0] if b == 0 else row_[1] + b * row_[2]

        cross = along(xs[0]) if a == 0 else along(xs[1]) + a * along(xs[2])
        score = jnp.where(usable, cross + base, excluded)
        sc[t * KO : (t + 1) * KO, :] = score
        peak = jnp.maximum(peak, score)
    peak = jnp.max(peak, axis=0, keepdims=True)
    mass = jnp.zeros((KO, N), f32)
    for t in range(BASES):
        mass = mass + jnp.where(usable, jnp.exp(band(sc, t) - peak), 0.0)
    mass = jnp.sum(mass, axis=0, keepdims=True)
    stats[group, 0:8, :] = jnp.broadcast_to(peak, (8, N))
    stats[group, 8:16, :] = jnp.broadcast_to(mass, (8, N))

    def stat_copy(k, slot_group, to):
        mine = stats.at[slot_group]
        return pltpu.make_async_remote_copy(
            src_ref=mine, dst_ref=mine, send_sem=ssend_sem.at[k], recv_sem=srecv_sem.at[k],
            device_id=(dom, to), device_id_type=MESH,
        )

    for k in range(1, GROUPS):
        stat_copy(k, group, (group + k) % GROUPS).start()
    for k in range(1, GROUPS):
        frm = (group + GROUPS - k) % GROUPS
        stat_copy(k, frm, frm).wait_recv()
    top = stats[0, 0:1, :]
    for g in range(1, GROUPS):
        top = jnp.maximum(top, stats[g, 0:1, :])
    total = jnp.zeros((1, N), f32)
    for g in range(GROUPS):
        total = total + stats[g, 8:9, :] * jnp.exp(stats[g, 0:1, :] - top)
    evid_ref[...] = top + jnp.log(total)
    scale = 1.0 / total
    ps = [
        [jnp.where(usable, jnp.exp(band(sc, a * 3 + b) - top) * scale, 0.0) for b in range(3)]
        for a in range(3)
    ]
    basis = []
    for less, none, more in ps:
        basis.append((none, more + less, more - less))
    for b in range(3):
        less, none, more = basis[0][b], basis[1][b], basis[2][b]
        for a, v in enumerate((none, more + less, more - less)):
            post_ref[(a * 3 + b) * KO : (a * 3 + b + 1) * KO, :] = v.astype(bf16)

    weighted_copy(NP - 2).wait()
    weighted_copy(NP - 1).wait()
    for i in range(len(MSGS)):
        message(i).wait_send()
    for k in range(1, GROUPS):
        stat_copy(k, group, (group + k) % GROUPS).wait_send()


CHUNKS = 8
ROWS = PL * CL
HALF = ROWS // 2
QUART = ROWS // 4


def back_kernel(
    post_ref, weighted_hbm, coltab_ref, lines_ref, owner_ref, slab_ref, kernel_ref, interp_ref,
    out_ref,
    wbuf, part, r1, r2, p2, q1, q2,
    rowre, rowim, mapped, outgoing, received, placer, sender, slab, sib, chip, y1, y2,
    in_sem, send_sem, recv_sem, xsend, xrecv, ysend, yrecv,
):
    dom = lax.axis_index("dom")
    group = lax.axis_index("orient")
    z, x = dom // SIDE, dom % SIDE

    def neighbour(axis, d):
        return z * SIDE + (x + d) % SIDE if axis == "x" else ((z + d) % SIDE) * SIDE + x

    def share_of(i):
        return i // 2 + CHUNKS * (i % 2)

    def load(i):
        return pltpu.make_async_copy(weighted_hbm.at[share_of(i)], wbuf.at[i % 3], in_sem.at[i % 3])

    load(0).start()
    load(1).start()
    core, high = group % 2, group // 2
    sibling = high * 2 + 1 - core
    barrier = pltpu.get_barrier_semaphore()
    for k in range(1, NP):
        pl.semaphore_signal(barrier, inc=1, device_id=((dom + k) % NP, group), device_id_type=MESH)
    for to in (sibling, (group + 2) % GROUPS, (group + 6) % GROUPS):
        pl.semaphore_signal(barrier, inc=1, device_id=(dom, to), device_id_type=MESH)
    pl.semaphore_wait(barrier, NP + 2)

    ca, sa = coltab_ref[1:2, :], coltab_ref[2:3, :]

    def compute(i):
        load(i).wait()
        pl.when(i + 2 < NP)(lambda: load(i + 2).start())
        chunk, half, share = i // 2, i % 2, share_of(i)
        for four in range(PL // 4):
            outs = []
            for j in range(four * 4, four * 4 + 4):
                g = jnp.dot(
                    post_ref[...], wbuf[i % 3, :, j * WIDE : (j + 1) * WIDE], preferred_element_type=f32
                )
                cp, sp = lines_ref[share, j : j + 1, :], lines_ref[share, PL + j : PL + j + 1, :]
                vs = []
                for a in range(3):
                    g0, gc, gs = (g[(a * 3 + b) * KO : (a * 3 + b + 1) * KO, :] for b in range(3))
                    vs.append(
                        (
                            g0[:, :COLS] + gc[:, :COLS] * cp + gs[:, COLS:] * sp,
                            g0[:, COLS:] + gc[:, COLS:] * cp - gs[:, :COLS] * sp,
                        )
                    )
                outs.append(
                    jnp.concatenate(
                        [
                            vs[0][0] + vs[1][0] * ca + vs[2][1] * sa,
                            vs[0][1] + vs[1][1] * ca - vs[2][0] * sa,
                        ],
                        axis=1,
                    )
                )
            for o in range(OG):
                piece = jnp.concatenate([v[o * CL : (o + 1) * CL, :] for v in outs], axis=0)
                part[chunk, o // 2, (o % 2) * 2 + half, pl.ds(four * 16, 16), :] = piece.astype(bf16)

    def setup(h):
        first, second = ("x", "z") if h == 0 else ("z", "x")
        return (first, x, second, z) if h == 0 else (first, z, second, x)

    def column(c, h, f, lo, size):
        rows = pl.ds(h * HALF + lo, size)
        return part.at[c, :, f, rows, :] if h == 0 else part.at[c, f, :, rows, :]

    def copy(src, dst, c, idx, axis, d):
        return pltpu.make_async_remote_copy(
            src_ref=src, dst_ref=dst, send_sem=send_sem.at[c, idx], recv_sem=recv_sem.at[c, idx],
            device_id=(neighbour(axis, d), group), device_id_type=MESH,
        )

    def copies(c, h, stage):
        first, f, second, s = setup(h)
        far_f, far_s = (f + 2) % 4, (s + 2) % 4
        out = []
        for n_, d in enumerate((3, 1)):
            idx = (h * 4 + stage) * 2 + n_
            if stage == 0:
                out.append(copy(column(c, h, far_f, n_ * QUART, QUART), r1.at[c, h, n_], c, idx, first, d))
            elif stage == 1:
                out.append(copy(column(c, h, (f + d) % 4, 0, HALF), r2.at[c, h, n_], c, idx, first, d))
            elif stage == 2:
                src = p2.at[c, h, far_s, pl.ds(n_ * QUART, QUART), :]
                out.append(copy(src, q1.at[c, h, n_], c, idx, second, d))
            else:
                out.append(copy(p2.at[c, h, (s + d) % 4], q2.at[c, h, n_], c, idx, second, d))
        return out

    def column_get(c, h, f, i, lo, size):
        rows = pl.ds(h * HALF + lo, size)
        return part[c, i, f, rows, :] if h == 0 else part[c, f, i, rows, :]

    def column_set(c, h, f, i, lo, size, value):
        rows = pl.ds(h * HALF + lo, size)
        if h == 0:
            part[c, i, f, rows, :] = value
        else:
            part[c, f, i, rows, :] = value

    def advance(c, stage):
        for h in (0, 1):
            first, f, second, s = setup(h)
            if stage > 0:
                for cp_ in copies(c, h, stage - 1):
                    cp_.wait_recv()
            if stage == 1:
                for n_, d in enumerate((3, 1)):
                    for i in range(SIDE):
                        to = (f + d) % 4
                        mine = column_get(c, h, to, i, n_ * QUART, QUART).astype(f32)
                        new = mine + r1[c, h, n_, i].astype(f32)
                        column_set(c, h, to, i, n_ * QUART, QUART, new.astype(bf16))
            elif stage == 2:
                for i in range(SIDE):
                    new = column_get(c, h, f, i, 0, HALF).astype(f32)
                    new = new + r2[c, h, 0, i].astype(f32) + r2[c, h, 1, i].astype(f32)
                    p2[c, h, i] = new.astype(bf16)
            elif stage == 3:
                for n_, d in enumerate((3, 1)):
                    rows = pl.ds(n_ * QUART, QUART)
                    to = (s + d) % 4
                    new = p2[c, h, to, rows, :].astype(f32) + q1[c, h, n_].astype(f32)
                    p2[c, h, to, rows, :] = new.astype(bf16)
            elif stage == 4:
                new = p2[c, h, s].astype(f32) + q2[c, h, 0].astype(f32) + q2[c, h, 1].astype(f32)
                new = new.astype(bf16).astype(f32)
                rows = pl.ds(pl.multiple_of(c * ROWS, ROWS) + h * HALF, HALF)
                rowre[rows, :] = new[:, :COLS]
                rowim[rows, :] = new[:, COLS:]
            if stage < 4:
                for cp_ in copies(c, h, stage):
                    cp_.start()

    def ranks(own):
        hot = own == lax.broadcasted_iota(jnp.int32, (NP, COLS), 0)
        before = lax.broadcasted_iota(jnp.int32, (COLS, COLS), 0) < lax.broadcasted_iota(
            jnp.int32, (COLS, COLS), 1
        )
        hot = jnp.where(hot, 1.0, 0.0)
        counts = jnp.dot(
            hot.astype(bf16), jnp.where(before, 1.0, 0.0).astype(bf16), preferred_element_type=f32
        )
        return jnp.sum(hot * counts, axis=0, keepdims=True).astype(jnp.int32)

    def prepare():
        slot_row = lax.broadcasted_iota(jnp.int32, (CAP, COLS), 0)
        mine = pl.ds(pl.multiple_of(group * OG, OG), OG)
        owners, slabs, kernels = owner_ref[mine, :], slab_ref[mine, :].astype(f32), kernel_ref[mine, :]

        def block(a, b):
            return a[b // 2 : b // 2 + 1, (b % 2) * COLS : (b % 2 + 1) * COLS]

        def own_block(a):
            a = jnp.where(dom % 2 == 0, a[:, :COLS], a[:, COLS:]).astype(f32)
            row = lax.broadcasted_iota(jnp.int32, (OG, COLS), 0)
            return jnp.sum(jnp.where(row == dom // 2, a, 0.0), axis=0, keepdims=True).astype(jnp.int32)

        for b in range(NP):
            own = block(owners, b)
            live = (own == dom) & (ranks(own) == slot_row)
            target = jnp.sum(jnp.where(live, block(slabs, b) + 1.0, 0.0), axis=1, keepdims=True)
            spot = lax.broadcasted_iota(jnp.int32, (CAP, SLAB_ROWS), 1).astype(f32) + 1.0
            placer[b * CAP : (b + 1) * CAP, :] = jnp.where(target == spot, 1.0, 0.0)
        own = own_block(owners)
        slot = own * CAP + ranks(own)
        hit = slot == lax.broadcasted_iota(jnp.int32, (NP * CAP, COLS), 0)
        kern = own_block(kernels)
        for w in range(4):
            sender[:, w * COLS : (w + 1) * COLS] = jnp.where(hit & (kern == w), 1.0, 0.0).astype(bf16)

    def tick(t, carry):
        @pl.when(t < CHUNKS)
        def _():
            def body(q, c):
                compute(t * 2 + q)
                return c

            lax.fori_loop(0, 2, body, 0)

        pl.when(t == CHUNKS)(prepare)
        for stage in range(5):
            c = t - stage
            pl.when((c >= 0) & (c < CHUNKS))(functools.partial(advance, c, stage))
        return carry

    lax.fori_loop(0, CHUNKS + 4, tick, 0)

    for k in range(CL):
        for n_, ref in enumerate((rowre, rowim)):
            rows = ref[pl.ds(k, COLS, stride=CL), :].astype(bf16)
            for w in range(4):
                new = jnp.dot(rows, interp_ref[w], preferred_element_type=f32)
                at = (2 * k + n_) * COLS
                mapped[w * COLS : (w + 1) * COLS, at : at + COLS] = new.astype(bf16)
    rows = jnp.dot(sender[...], mapped[...], preferred_element_type=f32)
    outgoing[...] = rows.astype(bf16).reshape(NP, CAP, CL * WIDE)

    def to_owner(k, src, dst, dev):
        return pltpu.make_async_remote_copy(
            src_ref=src, dst_ref=dst, send_sem=xsend.at[k], recv_sem=xrecv.at[k],
            device_id=(dev, group), device_id_type=MESH,
        )

    for k in range(1, NP):
        to = (dom + k) % NP
        to_owner(k, outgoing.at[to], received.at[dom], to).start()
    received[dom] = outgoing[dom]
    place = jnp.transpose(placer[...]).astype(bf16)
    for k in range(1, NP):
        frm = (dom + NP - k) % NP
        to_owner(k, outgoing.at[frm], received.at[frm], frm).wait_recv()
    rows = jnp.dot(place, received[...].reshape(NP * CAP, CL * WIDE), preferred_element_type=f32)
    slab[...] = rows.astype(bf16).reshape(SIDE, 2, SLAB_ROWS // GROUPS, CL * WIDE)

    def over_orient(i, src, dst, dev):
        return pltpu.make_async_remote_copy(
            src_ref=src, dst_ref=dst, send_sem=ysend.at[i], recv_sem=yrecv.at[i],
            device_id=(dom, dev), device_id_type=MESH,
        )

    swap = over_orient(0, slab.at[:, 1 - core], sib, sibling)
    swap.start()
    swap.wait_recv()
    part_rows = SLAB_ROWS // GROUPS // 2
    sides = ((6, 3), (2, 1))
    far = (high + 2) % SIDE
    chip[far] = (slab[far, core].astype(f32) + sib[far].astype(f32)).astype(bf16)
    first = [
        over_orient(1 + n_, chip.at[far, pl.ds(n_ * part_rows, part_rows)], y1.at[n_], (group + d) % GROUPS)
        for n_, (d, _) in enumerate(sides)
    ]
    for c in first:
        c.start()
    for d in (3, 1, 0):
        to = (high + d) % SIDE
        chip[to] = (slab[to, core].astype(f32) + sib[to].astype(f32)).astype(bf16)
    second = []
    for n_, (d, dy) in enumerate(sides):
        to = (high + dy) % SIDE
        first[n_].wait_recv()
        rows = pl.ds(n_ * part_rows, part_rows)
        chip[to, rows] = (chip[to, rows].astype(f32) + y1[n_].astype(f32)).astype(bf16)
        c = over_orient(3 + n_, chip.at[to], y2.at[n_], (group + d) % GROUPS)
        c.start()
        second.append(c)
    for c in second:
        c.wait_recv()
    out_ref[...] = chip[high].astype(f32) + y2[0].astype(f32) + y2[1].astype(f32)

    for c in range(CHUNKS):
        for h in (0, 1):
            for stage in range(4):
                for cp_ in copies(c, h, stage):
                    cp_.wait_send()
    for k in range(1, NP):
        to = (dom + k) % NP
        to_owner(k, outgoing.at[to], received.at[dom], to).wait_send()
    for c in (swap, *first, *second):
        c.wait_send()


VM = pl.BlockSpec(memory_space=pltpu.VMEM)
ANY = pl.BlockSpec(memory_space=pl.ANY)


def constants():
    c = np.arange(COLS, dtype=np.float32)
    l = np.arange(LINES, dtype=np.float32) - LINES // 2
    half = float(LINES // 2)
    coltab = np.zeros((8, COLS), np.float32)
    coltab[0] = c * c / (half * half)
    coltab[1] = np.cos(math.pi * c / COLS)
    coltab[2] = np.sin(math.pi * c / COLS)
    rowtab = np.zeros((NP, 8, COLS), np.float32)
    rsq = (l * l / (half * half)).reshape(NP, 1, PL)
    rowtab[:, :, :PL] = rsq
    rowtab[:, :, PL : 2 * PL] = rsq
    offs = np.zeros((8, COLS), np.float32)
    offs[:, :PL] = 0.3
    offs[:, PL : 2 * PL] = 0.3 + math.pi / 2
    ang = (math.pi * l / half).reshape(NP, PL, 1)
    lines = np.concatenate([np.cos(ang), np.sin(ang)], axis=1)
    lines = np.broadcast_to(lines, (NP, 2 * PL, COLS)).astype(np.float32)
    return coltab, rowtab, offs, lines


def shards(
    images, defocus, noise_var, references, orient_list, class_label, owner, slab_row, kernel_index, interp
):
    coltab, rowtab, offs, lines = (jnp.asarray(a) for a in constants())
    refs = jnp.transpose(references, (2, 1, 0, 3)).reshape(PL, KO, WIDE)
    focus = jnp.broadcast_to(defocus[:, None], (N, COLS))
    labels = jnp.broadcast_to(class_label[None, :], (8, N))
    post, evidence, weighted = pl.pallas_call(
        score_kernel,
        out_shape=(
            jax.ShapeDtypeStruct((BASES * KO, N), bf16),
            jax.ShapeDtypeStruct((1, N), f32),
            jax.ShapeDtypeStruct((NP, N, PK), bf16),
        ),
        in_specs=[VM, ANY] + [VM] * 8,
        out_specs=(VM, VM, ANY),
        scratch_shapes=[
            pltpu.VMEM((NP, PL, KO, WIDE), bf16),
            pltpu.VMEM((2, N, PL, WIDE), bf16),
            pltpu.VMEM((N * PL, COLS), f32),
            pltpu.VMEM((N * PL, COLS), f32),
            pltpu.VMEM((2, N, PK), bf16),
            pltpu.VMEM((N, PL * COLS), bf16),
            pltpu.VMEM((BASES * KO, PK), bf16),
            pltpu.VMEM((KO, PL * COLS), bf16),
            pltpu.VMEM((BASES * KO, N), f32),
            pltpu.VMEM((N, KO), f32),
            pltpu.VMEM((N, COLS), f32),
            pltpu.VMEM((N, COLS), f32),
            pltpu.VMEM((N, COLS), f32),
            pltpu.VMEM((BASES * KO, N), f32),
            pltpu.VMEM((GROUPS, 16, N), f32),
            pltpu.SemaphoreType.DMA((len(MSGS),)),
            pltpu.SemaphoreType.DMA((len(MSGS),)),
            pltpu.SemaphoreType.DMA((GROUPS,)),
            pltpu.SemaphoreType.DMA((GROUPS,)),
            pltpu.SemaphoreType.DMA((2,)),
            pltpu.SemaphoreType.DMA((2,)),
        ],
        compiler_params=pltpu.CompilerParams(
            collective_id=0, has_side_effects=True, vmem_limit_bytes=40 * 2**20
        ),
    )(
        refs, images, focus, noise_var.reshape(NP, PL, COLS), orient_list.T, labels, rowtab, offs, coltab, lines
    )
    piece = SLAB_ROWS // GROUPS
    volume = pl.pallas_call(
        back_kernel,
        out_shape=jax.ShapeDtypeStruct((piece, CL * WIDE), f32),
        in_specs=[VM, ANY] + [VM] * 6,
        out_specs=VM,
        scratch_shapes=[
            pltpu.VMEM((3, N, PK), bf16),
            pltpu.VMEM((CHUNKS, SIDE, SIDE, ROWS, WIDE), bf16),
            pltpu.VMEM((CHUNKS, 2, 2, SIDE, QUART, WIDE), bf16),
            pltpu.VMEM((CHUNKS, 2, 2, SIDE, HALF, WIDE), bf16),
            pltpu.VMEM((CHUNKS, 2, SIDE, HALF, WIDE), bf16),
            pltpu.VMEM((CHUNKS, 2, 2, QUART, WIDE), bf16),
            pltpu.VMEM((CHUNKS, 2, 2, HALF, WIDE), bf16),
            pltpu.VMEM((CHUNKS * ROWS, COLS), f32),
            pltpu.VMEM((CHUNKS * ROWS, COLS), f32),
            pltpu.VMEM((4 * COLS, CL * WIDE), bf16),
            pltpu.VMEM((NP, CAP, CL * WIDE), bf16),
            pltpu.VMEM((NP, CAP, CL * WIDE), bf16),
            pltpu.VMEM((NP * CAP, SLAB_ROWS), f32),
            pltpu.VMEM((NP * CAP, 4 * COLS), bf16),
            pltpu.VMEM((SIDE, 2, piece, CL * WIDE), bf16),
            pltpu.VMEM((SIDE, piece, CL * WIDE), bf16),
            pltpu.VMEM((SIDE, piece, CL * WIDE), bf16),
            pltpu.VMEM((2, piece // 2, CL * WIDE), bf16),
            pltpu.VMEM((2, piece, CL * WIDE), bf16),
            pltpu.SemaphoreType.DMA((3,)),
            pltpu.SemaphoreType.DMA((CHUNKS, 16)),
            pltpu.SemaphoreType.DMA((CHUNKS, 16)),
            pltpu.SemaphoreType.DMA((NP,)),
            pltpu.SemaphoreType.DMA((NP,)),
            pltpu.SemaphoreType.DMA((5,)),
            pltpu.SemaphoreType.DMA((5,)),
        ],
        compiler_params=pltpu.CompilerParams(
            collective_id=1, has_side_effects=True, vmem_limit_bytes=40 * 2**20
        ),
    )(post, weighted, coltab, lines, owner[:, :, 0], slab_row, kernel_index, interp)
    return volume.reshape(piece, CL, WIDE), evidence.reshape(N)


def solution(mesh):
    return jax.shard_map(
        shards,
        mesh=mesh,
        in_specs=(
            P("dom", None, None),
            P("dom"),
            P(),
            P(None, "orient", "dom", None),
            P("dom", None),
            P("dom"),
            P(),
            P(),
            P(),
            P(),
        ),
        out_specs=(P(("dom", "orient"), None, None), P("dom")),
        check_vma=False,
    )
```

```python
import functools
import math

import jax
import jax.numpy as jnp
import numpy as np
from jax import lax
from jax.experimental import pallas as pl
from jax.experimental.pallas import tpu as pltpu
from jax.sharding import PartitionSpec as P

SLAB_ROWS = 512
LINES = 256
COLS = 128
WIDE = 2 * COLS
N = 192
CL = 4
OG = 8
KO = CL * OG
PL = 16
NP = LINES // PL
PK = PL * WIDE
SIDE = 4
GROUPS = 8
BASES = 9
SHARED = N // 2
CAP = 16

prior_hit = math.log(0.55)
prior_miss = math.log(0.15)
excluded = -1e30
MESH = pl.DeviceIdType.MESH
bf16 = jnp.bfloat16
f32 = jnp.float32

ORDER = (
    (0, 0), (0, 1), (0, 3), (1, 0), (3, 0), (1, 1), (1, 3), (3, 1), (3, 3),
    (0, 2), (2, 0), (1, 2), (3, 2), (2, 1), (2, 3), (2, 2),
)


def gather_plan():
    msgs = []
    for first, lo in (("x", 0), ("z", PL // 2)):
        mid, hi = lo + PL // 4, lo + PL // 2
        second = "z" if first == "x" else "x"

        def rel(f, s):
            return (s, f) if first == "x" else (f, s)

        msgs += [(0, rel(0, 0), lo, hi, first, d) for d in (1, -1)]
        msgs += [(1, rel(1, 0), lo, mid, first, -1), (1, rel(3, 0), mid, hi, first, 1)]
        for rank, f in ((0.5, 0), (2, 1), (2, 3), (4, 2)):
            msgs += [(rank, rel(f, 0), lo, hi, second, d) for d in (1, -1)]
            msgs += [
                (rank + 1, rel(f, 1), lo, mid, second, -1),
                (rank + 1, rel(f, 3), mid, hi, second, 1),
            ]
    msgs.sort(key=lambda m: m[0])
    msgs = [m[1:] for m in msgs]

    def landing(m):
        (dz, dx), lo, hi, axis, d = m
        return ((dz, (dx - d) % 4) if axis == "x" else ((dz - d) % 4, dx), lo, hi)

    land = [landing(m) for m in msgs]
    early = {
        1: [(0, 1, 0), (0, 3, 0), (1, 0, 1), (3, 0, 1), (0, 1, 1), (0, 3, 1), (1, 0, 0), (3, 0, 0)],
        3: [(0, 2, 0), (2, 0, 1)],
        5: [(1, 1, 0), (3, 1, 0), (1, 3, 0), (3, 3, 0), (1, 1, 1), (1, 3, 1), (3, 1, 1), (3, 3, 1)],
        10: [(1, 2, 0), (3, 2, 0), (2, 1, 1), (2, 3, 1)],
    }
    have = {((0, 0), line) for line in range(PL)}
    waited, sent, steps = set(), set(), []

    def ready(m):
        return all((m[0], line) in have for line in range(m[1], m[2]))

    for step in range(NP):
        acts = []
        if step == 0:
            for i, m in enumerate(msgs):
                if ready(m):
                    acts.append(("send", i))
                    sent.add(i)
        wanted = [((dz, dx), half) for dz, dx, half in early.get(step, [])]
        wanted += [(ORDER[step], half) for half in (0, 1)] if step else []
        for piece, half in wanted:
            for i, (at, lo, hi) in enumerate(land):
                if at == piece and lo // (PL // 2) == half and i not in waited:
                    waited.add(i)
                    acts.append(("wait", i))
                    have |= {(at, line) for line in range(lo, hi)}
            for i, m in enumerate(msgs):
                if i not in sent and ready(m):
                    acts.append(("send", i))
                    sent.add(i)
        steps.append(acts)
    assert len(waited) == len(msgs) == len(sent)
    return msgs, land, steps


MSGS, LAND, STEPS = gather_plan()


def fine_sin(angle):
    turns = jnp.floor(angle * (1.0 / math.pi) + 0.5)
    x = angle - turns * 3.140625
    x = x - turns * (math.pi - 3.140625)
    odd = turns - 2.0 * jnp.floor(turns * 0.5)
    x2 = x * x
    poly = -1.0 / 39916800.0
    for c in (1.0 / 362880.0, -1.0 / 5040.0, 1.0 / 120.0, -1.0 / 6.0):
        poly = poly * x2 + c
    s = x + x * x2 * poly
    return s * (1.0 - 2.0 * odd)


def column_waves():
    ang = lax.broadcasted_iota(jnp.int32, (1, COLS), 1).astype(f32) * (math.pi / COLS)
    return fine_sin(ang + math.pi / 2), fine_sin(ang)


def line_waves(share):
    row = lax.broadcasted_iota(jnp.int32, (2 * PL, COLS), 0)
    line = (share * PL - LINES // 2 + row % PL).astype(f32)
    return fine_sin(line * (2 * math.pi / LINES) + jnp.where(row < PL, math.pi / 2, 0.0))


def line_angles(share):
    lane = lax.broadcasted_iota(jnp.int32, (1, COLS), 1)
    line = (share * PL - LINES // 2 + lane % PL).astype(f32) * (2.0 / LINES)
    return line * line, jnp.where(lane < PL, 0.3, 0.3 + math.pi / 2)


def pick(step, values):
    out = jnp.int32(0)
    for i, v in enumerate(values):
        if v:
            out = out + jnp.where(step == i, v, 0)
    return out


def score_kernel(
    refs_ref, images_hbm, focus_ref, noise_ref, list_ref, label_ref,
    post_ref, evid_ref, weighted_hbm,
    refs_all, ibuf, fre, fim, wall, call, sbuf, rbuf, acc, eacc, focus, colsin, colcos, angtab, waves, sc, stats,
    send_sem, recv_sem, ssend_sem, srecv_sem, in_sem, out_sem, wsend, wrecv, csend, crecv,
):
    dom = lax.axis_index("dom")
    group = lax.axis_index("orient")
    z, x = dom // SIDE, dom % SIDE
    core = group % 2
    sibling = group + 1 - 2 * core
    mine = pl.ds(pl.multiple_of(core * SHARED, SHARED), SHARED)
    theirs = pl.ds(pl.multiple_of((1 - core) * SHARED, SHARED), SHARED)

    def origin(dz, dx):
        return ((z + dz) % SIDE) * SIDE + (x + dx) % SIDE

    def step_origin(step):
        return origin(pick(step, [o[0] for o in ORDER]), pick(step, [o[1] for o in ORDER]))

    def image_copy(step):
        lines = pl.ds(pl.multiple_of(step_origin(step) * PL, PL), PL)
        return pltpu.make_async_copy(images_hbm.at[mine, lines, :], ibuf.at[step % 2], in_sem.at[step % 2])

    def weighted_copy(step):
        return pltpu.make_async_copy(wall.at[step], weighted_hbm.at[step_origin(step)], out_sem.at[step])

    def swap(step, rows):
        def one(buf, send, recv):
            part = buf.at[step, rows]
            return pltpu.make_async_remote_copy(
                src_ref=part, dst_ref=part, send_sem=send.at[step], recv_sem=recv.at[step],
                device_id=(dom, sibling), device_id_type=MESH,
            )

        return one(wall, wsend, wrecv), one(call, csend, crecv)

    image_copy(0).start()

    barrier = pltpu.get_barrier_semaphore()
    for dz, dx in ((0, 1), (0, 3), (1, 0), (3, 0)):
        pl.semaphore_signal(barrier, inc=1, device_id=(origin(dz, dx), group), device_id_type=MESH)
    for k in range(1, GROUPS):
        pl.semaphore_signal(barrier, inc=1, device_id=(dom, (group + k) % GROUPS), device_id_type=MESH)
    pl.semaphore_wait(barrier, 4 + GROUPS - 1)

    def message(i):
        (dz, dx), lo, hi, axis, d = MSGS[i]
        to = origin(0, d % 4) if axis == "x" else origin(d % 4, 0)
        at = origin(dz, dx)
        rows = refs_all.at[at, pl.ds(lo, hi - lo)]
        src = refs_ref.at[pl.ds(lo, hi - lo)] if (dz, dx) == (0, 0) else rows
        return pltpu.make_async_remote_copy(
            src_ref=src, dst_ref=rows, send_sem=send_sem.at[i], recv_sem=recv_sem.at[i],
            device_id=(to, group), device_id_type=MESH,
        )

    def arrival(i):
        (dz, dx), lo, hi = LAND[i]
        rows = refs_all.at[origin(dz, dx), pl.ds(lo, hi - lo)]
        axis, d = MSGS[i][3:]
        frm = origin(0, -d % 4) if axis == "x" else origin(-d % 4, 0)
        return pltpu.make_async_remote_copy(
            src_ref=rows, dst_ref=rows, send_sem=send_sem.at[i], recv_sem=recv_sem.at[i],
            device_id=(frm, group), device_id_type=MESH,
        )

    def traffic(acts):
        for kind, i in acts:
            if kind == "send":
                message(i).start()
            else:
                arrival(i).wait_recv()

    traffic(STEPS[0])
    refs_all[dom] = refs_ref[...]
    wide = jnp.transpose(jnp.broadcast_to(focus_ref[...], (COLS, N)))
    focus[...] = jnp.where(core == 0, wide[:SHARED, :], wide[SHARED:, :])
    col = lax.broadcasted_iota(jnp.int32, (1, COLS), 1).astype(f32) * (2.0 / LINES)
    colang = focus[...] * (col * col)
    colsin[...] = fine_sin(colang)
    colcos[...] = fine_sin(colang + math.pi / 2)
    acc[...] = jnp.zeros_like(acc)
    eacc[...] = jnp.zeros_like(eacc)

    def weigh_share(step):
        share = step_origin(step)
        slot = step % 2
        pl.when(step + 1 < NP)(lambda: image_copy(step + 1).start())
        far, start = line_angles(share)
        angtab[...] = fine_sin(focus[...] * far + start)
        image_copy(step).wait()

        def widen(i, c):
            part = ibuf[slot, pl.ds(pl.multiple_of(i * 8, 8), 8)].astype(f32)
            part = part.reshape(128, WIDE)
            rows = pl.ds(pl.multiple_of(i * 128, 128), 128)
            fre[rows, :] = part[:, :COLS]
            fim[rows, :] = part[:, COLS:]
            return c

        lax.fori_loop(0, SHARED // 8, widen, 0)

        def weigh(i, c):
            rows = pl.ds(pl.multiple_of(i * 32, 32), 32)
            to = pl.ds(pl.multiple_of(core * SHARED + i * 32, 32), 32)
            cs, cc = colsin[rows, :], colcos[rows, :]
            ang = angtab[rows, :]
            for j in range(PL):
                inv = 1.0 / noise_ref[share, j : j + 1, :]
                con = ang[:, j : j + 1] * cc + ang[:, PL + j : PL + j + 1] * cs
                fac = con * inv
                take = pl.ds(i * (32 * PL) + j, 32, stride=PL)
                wall[step, to, j * WIDE : j * WIDE + COLS] = (fre[take, :] * fac).astype(bf16)
                wall[step, to, j * WIDE + COLS : (j + 1) * WIDE] = (fim[take, :] * fac).astype(bf16)
                call[step, to, j * COLS : (j + 1) * COLS] = (con * fac).astype(bf16)
            return c

        lax.fori_loop(0, SHARED // 32, weigh, 0)
        for c in swap(step, mine):
            c.start()

    weigh_share(0)

    def one_share(step, carry):
        pl.when(step + 1 < NP)(lambda: weigh_share(step + 1))
        for i in range(1, NP):
            if STEPS[i]:
                pl.when(step == i)(functools.partial(traffic, STEPS[i]))
        share = step_origin(step)
        waves[...] = line_waves(share)
        ca, sa = column_waves()
        for j in range(PL):
            ref = refs_all[share, j].astype(f32)
            re, im = ref[:, :COLS], ref[:, COLS:]
            cp, sp = waves[j : j + 1, :], waves[PL + j : PL + j + 1, :]
            rbuf[:, j * COLS : (j + 1) * COLS] = (re * re + im * im).astype(bf16)
            for a, (r, m) in enumerate(((re, im), (re * ca, im * ca), (im * -sa, re * sa))):
                for b, (r2, m2) in enumerate(((r, m), (r * cp, m * cp), (m * -sp, r * sp))):
                    at = (a * 3 + b) * KO
                    sbuf[at : at + KO, j * WIDE : j * WIDE + COLS] = r2.astype(bf16)
                    sbuf[at : at + KO, j * WIDE + COLS : (j + 1) * WIDE] = m2.astype(bf16)
        nt = (((1,), (1,)), ((), ()))
        for c in swap(step, theirs):
            c.wait_recv()
        weighted_copy(step).start()
        acc[...] += lax.dot_general(sbuf[...], wall[step], nt, preferred_element_type=f32)
        eacc[...] += lax.dot_general(call[step], rbuf[...], nt, preferred_element_type=f32)
        return carry

    lax.fori_loop(0, NP, one_share, 0)

    def band(ref, i):
        return ref[i * KO : (i + 1) * KO, :]

    row = lax.broadcasted_iota(jnp.int32, (KO, N), 0)
    wanted = group * OG + row // CL
    hits = jnp.zeros((KO, N), f32)
    for j in range(list_ref.shape[0]):
        hits = jnp.where(list_ref[j : j + 1, :] == wanted, 1.0, hits)
    usable = hits > 0.5
    base = jnp.where(label_ref[0:1, :] == row % CL, prior_hit, prior_miss) - 0.5 * jnp.transpose(eacc[...])
    xs = [[band(acc, a * 3 + b) for b in range(3)] for a in range(3)]
    peak = jnp.full((KO, N), excluded, f32)
    for t in range(BASES):
        a, b = t // 3 - 1, t % 3 - 1

        def along(row_):
            return row_[0] if b == 0 else row_[1] + b * row_[2]

        cross = along(xs[0]) if a == 0 else along(xs[1]) + a * along(xs[2])
        score = jnp.where(usable, cross + base, excluded)
        sc[t * KO : (t + 1) * KO, :] = score
        peak = jnp.maximum(peak, score)
    peak = jnp.max(peak, axis=0, keepdims=True)
    mass = jnp.zeros((KO, N), f32)
    for t in range(BASES):
        mass = mass + jnp.where(usable, jnp.exp(band(sc, t) - peak), 0.0)
    mass = jnp.sum(mass, axis=0, keepdims=True)
    stats[group, 0:8, :] = jnp.broadcast_to(peak, (8, N))
    stats[group, 8:16, :] = jnp.broadcast_to(mass, (8, N))

    def stat_copy(k, slot_group, to):
        mine = stats.at[slot_group]
        return pltpu.make_async_remote_copy(
            src_ref=mine, dst_ref=mine, send_sem=ssend_sem.at[k], recv_sem=srecv_sem.at[k],
            device_id=(dom, to), device_id_type=MESH,
        )

    for k in range(1, GROUPS):
        stat_copy(k, group, (group + k) % GROUPS).start()
    for k in range(1, GROUPS):
        frm = (group + GROUPS - k) % GROUPS
        stat_copy(k, frm, frm).wait_recv()
    top = stats[0, 0:1, :]
    for g in range(1, GROUPS):
        top = jnp.maximum(top, stats[g, 0:1, :])
    total = jnp.zeros((1, N), f32)
    for g in range(GROUPS):
        total = total + stats[g, 8:9, :] * jnp.exp(stats[g, 0:1, :] - top)
    evid_ref[...] = top + jnp.log(total)
    scale = 1.0 / total
    ps = [
        [jnp.where(usable, jnp.exp(band(sc, a * 3 + b) - top) * scale, 0.0) for b in range(3)]
        for a in range(3)
    ]
    basis = []
    for less, none, more in ps:
        basis.append((none, more + less, more - less))
    for b in range(3):
        less, none, more = basis[0][b], basis[1][b], basis[2][b]
        for a, v in enumerate((none, more + less, more - less)):
            post_ref[(a * 3 + b) * KO : (a * 3 + b + 1) * KO, :] = v.astype(bf16)

    for i in range(NP):
        weighted_copy(i).wait()
        for c in swap(i, mine):
            c.wait_send()
    for i in range(len(MSGS)):
        message(i).wait_send()
    for k in range(1, GROUPS):
        stat_copy(k, group, (group + k) % GROUPS).wait_send()


CHUNKS = 8
LAG = 2
ROWS = PL * CL
HALF = ROWS // 2
QUART = ROWS // 4


def back_kernel(
    post_ref, weighted_hbm, owner_ref, slab_ref, kernel_ref, interp_ref,
    out_ref,
    wbuf, part, r1, r2, p2, q1, q2,
    rowre, rowim, mapped, outgoing, received, placer, sender, slab, sib, chip, y1, y2, waves,
    in_sem, send_sem, recv_sem, xsend, xrecv, ysend, yrecv,
):
    dom = lax.axis_index("dom")
    group = lax.axis_index("orient")
    z, x = dom // SIDE, dom % SIDE

    def neighbour(axis, d):
        return z * SIDE + (x + d) % SIDE if axis == "x" else ((z + d) % SIDE) * SIDE + x

    def share_of(i):
        return i // 2 + CHUNKS * (i % 2)

    def load(i):
        return pltpu.make_async_copy(weighted_hbm.at[share_of(i)], wbuf.at[i % 3], in_sem.at[i % 3])

    load(0).start()
    load(1).start()
    core, high = group % 2, group // 2
    sibling = high * 2 + 1 - core
    barrier = pltpu.get_barrier_semaphore()
    for k in range(1, NP):
        pl.semaphore_signal(barrier, inc=1, device_id=((dom + k) % NP, group), device_id_type=MESH)
    for to in (sibling, (group + 2) % GROUPS, (group + 6) % GROUPS):
        pl.semaphore_signal(barrier, inc=1, device_id=(dom, to), device_id_type=MESH)
    pl.semaphore_wait(barrier, NP + 2)

    ca, sa = column_waves()

    def compute(i):
        load(i).wait()
        pl.when(i + 2 < NP)(lambda: load(i + 2).start())
        chunk, half = i // 2, i % 2
        waves[...] = line_waves(share_of(i))
        for four in range(PL // 4):
            outs = []
            for j in range(four * 4, four * 4 + 4):
                g = jnp.dot(
                    post_ref[...], wbuf[i % 3, :, j * WIDE : (j + 1) * WIDE], preferred_element_type=f32
                )
                cp, sp = waves[j : j + 1, :], waves[PL + j : PL + j + 1, :]
                vs = []
                for a in range(3):
                    g0, gc, gs = (g[(a * 3 + b) * KO : (a * 3 + b + 1) * KO, :] for b in range(3))
                    vs.append(
                        (
                            g0[:, :COLS] + gc[:, :COLS] * cp + gs[:, COLS:] * sp,
                            g0[:, COLS:] + gc[:, COLS:] * cp - gs[:, :COLS] * sp,
                        )
                    )
                outs.append(
                    jnp.concatenate(
                        [
                            vs[0][0] + vs[1][0] * ca + vs[2][1] * sa,
                            vs[0][1] + vs[1][1] * ca - vs[2][0] * sa,
                        ],
                        axis=1,
                    )
                )
            for o in range(OG):
                piece = jnp.concatenate([v[o * CL : (o + 1) * CL, :] for v in outs], axis=0)
                part[chunk, o // 2, (o % 2) * 2 + half, pl.ds(four * 16, 16), :] = piece.astype(bf16)

    def setup(h):
        first, second = ("x", "z") if h == 0 else ("z", "x")
        return (first, x, second, z) if h == 0 else (first, z, second, x)

    def column(c, h, f, lo, size):
        rows = pl.ds(h * HALF + lo, size)
        return part.at[c, :, f, rows, :] if h == 0 else part.at[c, f, :, rows, :]

    def copy(src, dst, c, idx, axis, d):
        return pltpu.make_async_remote_copy(
            src_ref=src, dst_ref=dst, send_sem=send_sem.at[c, idx], recv_sem=recv_sem.at[c, idx],
            device_id=(neighbour(axis, d), group), device_id_type=MESH,
        )

    def copies(c, h, stage):
        first, f, second, s = setup(h)
        far_f, far_s = (f + 2) % 4, (s + 2) % 4
        out = []
        for n_, d in enumerate((3, 1)):
            idx = (h * 4 + stage) * 2 + n_
            if stage == 0:
                out.append(copy(column(c, h, far_f, n_ * QUART, QUART), r1.at[c, h, n_], c, idx, first, d))
            elif stage == 1:
                out.append(copy(column(c, h, (f + d) % 4, 0, HALF), r2.at[c, h, n_], c, idx, first, d))
            elif stage == 2:
                src = p2.at[c, h, far_s, pl.ds(n_ * QUART, QUART), :]
                out.append(copy(src, q1.at[c, h, n_], c, idx, second, d))
            else:
                out.append(copy(p2.at[c, h, (s + d) % 4], q2.at[c, h, n_], c, idx, second, d))
        return out

    def column_get(c, h, f, i, lo, size):
        rows = pl.ds(h * HALF + lo, size)
        return part[c, i, f, rows, :] if h == 0 else part[c, f, i, rows, :]

    def column_set(c, h, f, i, lo, size, value):
        rows = pl.ds(h * HALF + lo, size)
        if h == 0:
            part[c, i, f, rows, :] = value
        else:
            part[c, f, i, rows, :] = value

    def advance(c, stage):
        for h in (0, 1):
            first, f, second, s = setup(h)
            if stage > 0:
                for cp_ in copies(c, h, stage - 1):
                    cp_.wait_recv()
            if stage == 1:
                for n_, d in enumerate((3, 1)):
                    for i in range(SIDE):
                        to = (f + d) % 4
                        mine = column_get(c, h, to, i, n_ * QUART, QUART).astype(f32)
                        new = mine + r1[c, h, n_, i].astype(f32)
                        column_set(c, h, to, i, n_ * QUART, QUART, new.astype(bf16))
            elif stage == 2:
                for i in range(SIDE):
                    new = column_get(c, h, f, i, 0, HALF).astype(f32)
                    new = new + r2[c, h, 0, i].astype(f32) + r2[c, h, 1, i].astype(f32)
                    p2[c, h, i] = new.astype(bf16)
            elif stage == 3:
                for n_, d in enumerate((3, 1)):
                    rows = pl.ds(n_ * QUART, QUART)
                    to = (s + d) % 4
                    new = p2[c, h, to, rows, :].astype(f32) + q1[c, h, n_].astype(f32)
                    p2[c, h, to, rows, :] = new.astype(bf16)
            elif stage == 4:
                new = p2[c, h, s].astype(f32) + q2[c, h, 0].astype(f32) + q2[c, h, 1].astype(f32)
                new = new.astype(bf16).astype(f32)
                rows = pl.ds(pl.multiple_of(c * ROWS, ROWS) + h * HALF, HALF)
                rowre[rows, :] = new[:, :COLS]
                rowim[rows, :] = new[:, COLS:]
            if stage < 4:
                for cp_ in copies(c, h, stage):
                    cp_.start()

    def ranks(own):
        hot = own == lax.broadcasted_iota(jnp.int32, (NP, COLS), 0)
        before = lax.broadcasted_iota(jnp.int32, (COLS, COLS), 0) < lax.broadcasted_iota(
            jnp.int32, (COLS, COLS), 1
        )
        hot = jnp.where(hot, 1.0, 0.0)
        counts = jnp.dot(
            hot.astype(bf16), jnp.where(before, 1.0, 0.0).astype(bf16), preferred_element_type=f32
        )
        return jnp.sum(hot * counts, axis=0, keepdims=True).astype(jnp.int32)

    def prepare():
        slot_row = lax.broadcasted_iota(jnp.int32, (CAP, COLS), 0)
        mine = pl.ds(pl.multiple_of(group * OG, OG), OG)
        owners, slabs, kernels = owner_ref[mine, :], slab_ref[mine, :].astype(f32), kernel_ref[mine, :]

        def block(a, b):
            return a[b // 2 : b // 2 + 1, (b % 2) * COLS : (b % 2 + 1) * COLS]

        def own_block(a):
            a = jnp.where(dom % 2 == 0, a[:, :COLS], a[:, COLS:]).astype(f32)
            row = lax.broadcasted_iota(jnp.int32, (OG, COLS), 0)
            return jnp.sum(jnp.where(row == dom // 2, a, 0.0), axis=0, keepdims=True).astype(jnp.int32)

        for b in range(NP):
            own = block(owners, b)
            live = (own == dom) & (ranks(own) == slot_row)
            target = jnp.sum(jnp.where(live, block(slabs, b) + 1.0, 0.0), axis=1, keepdims=True)
            spot = lax.broadcasted_iota(jnp.int32, (CAP, SLAB_ROWS), 1).astype(f32) + 1.0
            placer[b * CAP : (b + 1) * CAP, :] = jnp.where(target == spot, 1.0, 0.0)
        own = own_block(owners)
        slot = own * CAP + ranks(own)
        hit = slot == lax.broadcasted_iota(jnp.int32, (NP * CAP, COLS), 0)
        kern = own_block(kernels)
        for w in range(4):
            sender[:, w * COLS : (w + 1) * COLS] = jnp.where(hit & (kern == w), 1.0, 0.0).astype(bf16)

    def tick(t, carry):
        @pl.when(t < CHUNKS)
        def _():
            def body(q, c):
                compute(t * 2 + q)
                return c

            lax.fori_loop(0, 2, body, 0)

        pl.when(t == CHUNKS)(prepare)
        for stage in range(5):
            c = t - LAG * stage
            pl.when((c >= 0) & (c < CHUNKS))(functools.partial(advance, c, stage))
        return carry

    lax.fori_loop(0, CHUNKS + 4 * LAG, tick, 0)

    for k in range(CL):
        for n_, ref in enumerate((rowre, rowim)):
            rows = ref[pl.ds(k, COLS, stride=CL), :].astype(bf16)
            for w in range(4):
                new = jnp.dot(rows, interp_ref[w], preferred_element_type=f32)
                at = (2 * k + n_) * COLS
                mapped[w * COLS : (w + 1) * COLS, at : at + COLS] = new.astype(bf16)
    rows = jnp.dot(sender[...], mapped[...], preferred_element_type=f32)
    outgoing[...] = rows.astype(bf16).reshape(NP, CAP, CL * WIDE)

    def to_owner(k, src, dst, dev):
        return pltpu.make_async_remote_copy(
            src_ref=src, dst_ref=dst, send_sem=xsend.at[k], recv_sem=xrecv.at[k],
            device_id=(dev, group), device_id_type=MESH,
        )

    for k in range(1, NP):
        to = (dom + k) % NP
        to_owner(k, outgoing.at[to], received.at[dom], to).start()
    received[dom] = outgoing[dom]
    place = jnp.transpose(placer[...]).astype(bf16)
    for k in range(1, NP):
        frm = (dom + NP - k) % NP
        to_owner(k, outgoing.at[frm], received.at[frm], frm).wait_recv()
    rows = jnp.dot(place, received[...].reshape(NP * CAP, CL * WIDE), preferred_element_type=f32)
    slab[...] = rows.astype(bf16).reshape(SIDE, 2, SLAB_ROWS // GROUPS, CL * WIDE)

    def over_orient(i, src, dst, dev):
        return pltpu.make_async_remote_copy(
            src_ref=src, dst_ref=dst, send_sem=ysend.at[i], recv_sem=yrecv.at[i],
            device_id=(dom, dev), device_id_type=MESH,
        )

    swap = over_orient(0, slab.at[:, 1 - core], sib, sibling)
    swap.start()
    swap.wait_recv()
    part_rows = SLAB_ROWS // GROUPS // 2
    sides = ((6, 3), (2, 1))
    far = (high + 2) % SIDE
    chip[far] = (slab[far, core].astype(f32) + sib[far].astype(f32)).astype(bf16)
    first = [
        over_orient(1 + n_, chip.at[far, pl.ds(n_ * part_rows, part_rows)], y1.at[n_], (group + d) % GROUPS)
        for n_, (d, _) in enumerate(sides)
    ]
    for c in first:
        c.start()
    for d in (3, 1, 0):
        to = (high + d) % SIDE
        chip[to] = (slab[to, core].astype(f32) + sib[to].astype(f32)).astype(bf16)
    second = []
    for n_, (d, dy) in enumerate(sides):
        to = (high + dy) % SIDE
        first[n_].wait_recv()
        rows = pl.ds(n_ * part_rows, part_rows)
        chip[to, rows] = (chip[to, rows].astype(f32) + y1[n_].astype(f32)).astype(bf16)
        c = over_orient(3 + n_, chip.at[to], y2.at[n_], (group + d) % GROUPS)
        c.start()
        second.append(c)
    for c in second:
        c.wait_recv()
    out_ref[...] = chip[high].astype(f32) + y2[0].astype(f32) + y2[1].astype(f32)

    for c in range(CHUNKS):
        for h in (0, 1):
            for stage in range(4):
                for cp_ in copies(c, h, stage):
                    cp_.wait_send()
    for k in range(1, NP):
        to = (dom + k) % NP
        to_owner(k, outgoing.at[to], received.at[dom], to).wait_send()
    for c in (swap, *first, *second):
        c.wait_send()


VM = pl.BlockSpec(memory_space=pltpu.VMEM)
ANY = pl.BlockSpec(memory_space=pl.ANY)


def shards(
    images, defocus, noise_var, references, orient_list, class_label, owner, slab_row, kernel_index, interp
):
    refs = jnp.transpose(references, (2, 1, 0, 3)).reshape(PL, KO, WIDE)
    post, evidence, weighted = pl.pallas_call(
        score_kernel,
        out_shape=(
            jax.ShapeDtypeStruct((BASES * KO, N), bf16),
            jax.ShapeDtypeStruct((1, N), f32),
            jax.ShapeDtypeStruct((NP, N, PK), bf16),
        ),
        in_specs=[VM, ANY] + [VM] * 4,
        out_specs=(VM, VM, ANY),
        scratch_shapes=[
            pltpu.VMEM((NP, PL, KO, WIDE), bf16),
            pltpu.VMEM((2, SHARED, PL, WIDE), bf16),
            pltpu.VMEM((SHARED * PL, COLS), f32),
            pltpu.VMEM((SHARED * PL, COLS), f32),
            pltpu.VMEM((NP, N, PK), bf16),
            pltpu.VMEM((NP, N, PL * COLS), bf16),
            pltpu.VMEM((BASES * KO, PK), bf16),
            pltpu.VMEM((KO, PL * COLS), bf16),
            pltpu.VMEM((BASES * KO, N), f32),
            pltpu.VMEM((N, KO), f32),
            pltpu.VMEM((SHARED, COLS), f32),
            pltpu.VMEM((SHARED, COLS), f32),
            pltpu.VMEM((SHARED, COLS), f32),
            pltpu.VMEM((SHARED, COLS), f32),
            pltpu.VMEM((2 * PL, COLS), f32),
            pltpu.VMEM((BASES * KO, N), f32),
            pltpu.VMEM((GROUPS, 16, N), f32),
            pltpu.SemaphoreType.DMA((len(MSGS),)),
            pltpu.SemaphoreType.DMA((len(MSGS),)),
            pltpu.SemaphoreType.DMA((GROUPS,)),
            pltpu.SemaphoreType.DMA((GROUPS,)),
            pltpu.SemaphoreType.DMA((2,)),
        ]
        + [pltpu.SemaphoreType.DMA((NP,))] * 5,
        compiler_params=pltpu.CompilerParams(
            collective_id=0, has_side_effects=True, vmem_limit_bytes=58 * 2**20
        ),
    )(
        refs, images, defocus.reshape(1, N), noise_var.reshape(NP, PL, COLS), orient_list.T, class_label.reshape(1, N)
    )
    piece = SLAB_ROWS // GROUPS
    volume = pl.pallas_call(
        back_kernel,
        out_shape=jax.ShapeDtypeStruct((piece, CL * WIDE), f32),
        in_specs=[VM, ANY] + [VM] * 4,
        out_specs=VM,
        scratch_shapes=[
            pltpu.VMEM((3, N, PK), bf16),
            pltpu.VMEM((CHUNKS, SIDE, SIDE, ROWS, WIDE), bf16),
            pltpu.VMEM((CHUNKS, 2, 2, SIDE, QUART, WIDE), bf16),
            pltpu.VMEM((CHUNKS, 2, 2, SIDE, HALF, WIDE), bf16),
            pltpu.VMEM((CHUNKS, 2, SIDE, HALF, WIDE), bf16),
            pltpu.VMEM((CHUNKS, 2, 2, QUART, WIDE), bf16),
            pltpu.VMEM((CHUNKS, 2, 2, HALF, WIDE), bf16),
            pltpu.VMEM((CHUNKS * ROWS, COLS), f32),
            pltpu.VMEM((CHUNKS * ROWS, COLS), f32),
            pltpu.VMEM((4 * COLS, CL * WIDE), bf16),
            pltpu.VMEM((NP, CAP, CL * WIDE), bf16),
            pltpu.VMEM((NP, CAP, CL * WIDE), bf16),
            pltpu.VMEM((NP * CAP, SLAB_ROWS), f32),
            pltpu.VMEM((NP * CAP, 4 * COLS), bf16),
            pltpu.VMEM((SIDE, 2, piece, CL * WIDE), bf16),
            pltpu.VMEM((SIDE, piece, CL * WIDE), bf16),
            pltpu.VMEM((SIDE, piece, CL * WIDE), bf16),
            pltpu.VMEM((2, piece // 2, CL * WIDE), bf16),
            pltpu.VMEM((2, piece, CL * WIDE), bf16),
            pltpu.VMEM((2 * PL, COLS), f32),
            pltpu.SemaphoreType.DMA((3,)),
            pltpu.SemaphoreType.DMA((CHUNKS, 16)),
            pltpu.SemaphoreType.DMA((CHUNKS, 16)),
            pltpu.SemaphoreType.DMA((NP,)),
            pltpu.SemaphoreType.DMA((NP,)),
            pltpu.SemaphoreType.DMA((5,)),
            pltpu.SemaphoreType.DMA((5,)),
        ],
        compiler_params=pltpu.CompilerParams(
            collective_id=1, has_side_effects=True, vmem_limit_bytes=40 * 2**20
        ),
    )(post, weighted, owner[:, :, 0], slab_row, kernel_index, interp)
    return volume.reshape(piece, CL, WIDE), evidence.reshape(N)


def solution(mesh):
    return jax.shard_map(
        shards,
        mesh=mesh,
        in_specs=(
            P("dom", None, None),
            P("dom"),
            P(),
            P(None, "orient", "dom", None),
            P("dom", None),
            P("dom"),
            P(),
            P(),
            P(),
            P(),
        ),
        out_specs=(P(("dom", "orient"), None, None), P("dom")),
        check_vma=False,
    )
```

```python
import functools
import math

import jax
import jax.numpy as jnp
import numpy as np
from jax import lax
from jax.experimental import pallas as pl
from jax.experimental.pallas import tpu as pltpu
from jax.sharding import PartitionSpec as P

SLAB_ROWS = 512
LINES = 256
COLS = 128
WIDE = 2 * COLS
N = 192
CL = 4
OG = 8
KO = CL * OG
PL = 16
NP = LINES // PL
PK = PL * WIDE
SIDE = 4
GROUPS = 8
BASES = 9
SHARED = N // 2
CAP = 16

prior_hit = math.log(0.55)
prior_miss = math.log(0.15)
excluded = -1e30
MESH = pl.DeviceIdType.MESH
bf16 = jnp.bfloat16
f32 = jnp.float32

ORDER = (
    (0, 0), (0, 1), (0, 3), (1, 0), (3, 0), (1, 1), (1, 3), (3, 1), (3, 3),
    (0, 2), (2, 0), (1, 2), (3, 2), (2, 1), (2, 3), (2, 2),
)


def gather_plan():
    msgs = []
    for first, lo in (("x", 0), ("z", PL // 2)):
        mid, hi = lo + PL // 4, lo + PL // 2
        second = "z" if first == "x" else "x"

        def rel(f, s):
            return (s, f) if first == "x" else (f, s)

        msgs += [(0, rel(0, 0), lo, hi, first, d) for d in (1, -1)]
        msgs += [(1, rel(1, 0), lo, mid, first, -1), (1, rel(3, 0), mid, hi, first, 1)]
        for rank, f in ((0.5, 0), (2, 1), (2, 3), (4, 2)):
            msgs += [(rank, rel(f, 0), lo, hi, second, d) for d in (1, -1)]
            msgs += [
                (rank + 1, rel(f, 1), lo, mid, second, -1),
                (rank + 1, rel(f, 3), mid, hi, second, 1),
            ]
    msgs.sort(key=lambda m: m[0])
    msgs = [m[1:] for m in msgs]

    def landing(m):
        (dz, dx), lo, hi, axis, d = m
        return ((dz, (dx - d) % 4) if axis == "x" else ((dz - d) % 4, dx), lo, hi)

    land = [landing(m) for m in msgs]
    early = {
        1: [(0, 1, 0), (0, 3, 0), (1, 0, 1), (3, 0, 1), (0, 1, 1), (0, 3, 1), (1, 0, 0), (3, 0, 0)],
        3: [(0, 2, 0), (2, 0, 1)],
        5: [(1, 1, 0), (3, 1, 0), (1, 3, 0), (3, 3, 0), (1, 1, 1), (1, 3, 1), (3, 1, 1), (3, 3, 1)],
        10: [(1, 2, 0), (3, 2, 0), (2, 1, 1), (2, 3, 1)],
    }
    have = {((0, 0), line) for line in range(PL)}
    waited, sent, steps = set(), set(), []

    def ready(m):
        return all((m[0], line) in have for line in range(m[1], m[2]))

    for step in range(NP):
        acts = []
        if step == 0:
            for i, m in enumerate(msgs):
                if ready(m):
                    acts.append(("send", i))
                    sent.add(i)
        wanted = [((dz, dx), half) for dz, dx, half in early.get(step, [])]
        wanted += [(ORDER[step], half) for half in (0, 1)] if step else []
        for piece, half in wanted:
            for i, (at, lo, hi) in enumerate(land):
                if at == piece and lo // (PL // 2) == half and i not in waited:
                    waited.add(i)
                    acts.append(("wait", i))
                    have |= {(at, line) for line in range(lo, hi)}
            for i, m in enumerate(msgs):
                if i not in sent and ready(m):
                    acts.append(("send", i))
                    sent.add(i)
        steps.append(acts)
    assert len(waited) == len(msgs) == len(sent)
    return msgs, land, steps


MSGS, LAND, STEPS = gather_plan()


def fine_sin(angle):
    turns = jnp.floor(angle * (1.0 / math.pi) + 0.5)
    x = angle - turns * 3.140625
    x = x - turns * (math.pi - 3.140625)
    odd = turns - 2.0 * jnp.floor(turns * 0.5)
    x2 = x * x
    poly = -1.0 / 39916800.0
    for c in (1.0 / 362880.0, -1.0 / 5040.0, 1.0 / 120.0, -1.0 / 6.0):
        poly = poly * x2 + c
    s = x + x * x2 * poly
    return s * (1.0 - 2.0 * odd)


def column_waves():
    ang = lax.broadcasted_iota(jnp.int32, (1, COLS), 1).astype(f32) * (math.pi / COLS)
    return fine_sin(ang + math.pi / 2), fine_sin(ang)


def line_waves(share):
    row = lax.broadcasted_iota(jnp.int32, (2 * PL, COLS), 0)
    line = (share * PL - LINES // 2 + row % PL).astype(f32)
    return fine_sin(line * (2 * math.pi / LINES) + jnp.where(row < PL, math.pi / 2, 0.0))


def line_angles(share):
    lane = lax.broadcasted_iota(jnp.int32, (1, COLS), 1)
    line = (share * PL - LINES // 2 + lane % PL).astype(f32) * (2.0 / LINES)
    return line * line, jnp.where(lane < PL, 0.3, 0.3 + math.pi / 2)


def pick(step, values):
    out = jnp.int32(0)
    for i, v in enumerate(values):
        if v:
            out = out + jnp.where(step == i, v, 0)
    return out


def score_kernel(
    refs_ref, images_hbm, focus_ref, noise_ref, list_ref, label_ref,
    post_ref, evid_ref, weighted_hbm,
    refs_all, ibuf, fre, fim, wall, call, sbuf, rbuf, acc, eacc, focus, colsin, colcos, angtab, waves, sc, stats,
    send_sem, recv_sem, ssend_sem, srecv_sem, in_sem, out_sem, wsend, wrecv, csend, crecv,
):
    dom = lax.axis_index("dom")
    group = lax.axis_index("orient")
    z, x = dom // SIDE, dom % SIDE
    core = group % 2
    sibling = group + 1 - 2 * core
    mine = pl.ds(pl.multiple_of(core * SHARED, SHARED), SHARED)
    theirs = pl.ds(pl.multiple_of((1 - core) * SHARED, SHARED), SHARED)

    def origin(dz, dx):
        return ((z + dz) % SIDE) * SIDE + (x + dx) % SIDE

    def step_origin(step):
        return origin(pick(step, [o[0] for o in ORDER]), pick(step, [o[1] for o in ORDER]))

    def image_copy(step):
        lines = pl.ds(pl.multiple_of(step_origin(step) * PL, PL), PL)
        return pltpu.make_async_copy(images_hbm.at[mine, lines, :], ibuf.at[step % 2], in_sem.at[step % 2])

    def weighted_copy(step):
        return pltpu.make_async_copy(wall.at[step], weighted_hbm.at[step_origin(step)], out_sem.at[step])

    def swap(step, rows):
        def one(buf, send, recv):
            part = buf.at[step, rows]
            return pltpu.make_async_remote_copy(
                src_ref=part, dst_ref=part, send_sem=send.at[step], recv_sem=recv.at[step],
                device_id=(dom, sibling), device_id_type=MESH,
            )

        return one(wall, wsend, wrecv), one(call, csend, crecv)

    image_copy(0).start()

    barrier = pltpu.get_barrier_semaphore()
    for dz, dx in ((0, 1), (0, 3), (1, 0), (3, 0)):
        pl.semaphore_signal(barrier, inc=1, device_id=(origin(dz, dx), group), device_id_type=MESH)
    for k in range(1, GROUPS):
        pl.semaphore_signal(barrier, inc=1, device_id=(dom, (group + k) % GROUPS), device_id_type=MESH)
    pl.semaphore_wait(barrier, 4 + GROUPS - 1)

    def message(i):
        (dz, dx), lo, hi, axis, d = MSGS[i]
        to = origin(0, d % 4) if axis == "x" else origin(d % 4, 0)
        at = origin(dz, dx)
        rows = refs_all.at[at, pl.ds(lo, hi - lo)]
        src = refs_ref.at[pl.ds(lo, hi - lo)] if (dz, dx) == (0, 0) else rows
        return pltpu.make_async_remote_copy(
            src_ref=src, dst_ref=rows, send_sem=send_sem.at[i], recv_sem=recv_sem.at[i],
            device_id=(to, group), device_id_type=MESH,
        )

    def arrival(i):
        (dz, dx), lo, hi = LAND[i]
        rows = refs_all.at[origin(dz, dx), pl.ds(lo, hi - lo)]
        axis, d = MSGS[i][3:]
        frm = origin(0, -d % 4) if axis == "x" else origin(-d % 4, 0)
        return pltpu.make_async_remote_copy(
            src_ref=rows, dst_ref=rows, send_sem=send_sem.at[i], recv_sem=recv_sem.at[i],
            device_id=(frm, group), device_id_type=MESH,
        )

    def traffic(acts):
        for kind, i in acts:
            if kind == "send":
                message(i).start()
            else:
                arrival(i).wait_recv()

    traffic(STEPS[0])
    refs_all[dom] = refs_ref[...]
    wide = jnp.transpose(jnp.broadcast_to(focus_ref[...], (COLS, N)))
    focus[...] = jnp.where(core == 0, wide[:SHARED, :], wide[SHARED:, :])
    col = lax.broadcasted_iota(jnp.int32, (1, COLS), 1).astype(f32) * (2.0 / LINES)
    colang = focus[...] * (col * col)
    colsin[...] = fine_sin(colang)
    colcos[...] = fine_sin(colang + math.pi / 2)
    acc[...] = jnp.zeros_like(acc)
    eacc[...] = jnp.zeros_like(eacc)

    def weigh_share(step):
        share = step_origin(step)
        slot = step % 2
        pl.when(step + 1 < NP)(lambda: image_copy(step + 1).start())
        far, start = line_angles(share)
        angtab[...] = fine_sin(focus[...] * far + start)
        image_copy(step).wait()

        def widen(i, c):
            part = ibuf[slot, pl.ds(pl.multiple_of(i * 8, 8), 8)].astype(f32)
            part = part.reshape(128, WIDE)
            rows = pl.ds(pl.multiple_of(i * 128, 128), 128)
            fre[rows, :] = part[:, :COLS]
            fim[rows, :] = part[:, COLS:]
            return c

        lax.fori_loop(0, SHARED // 8, widen, 0)

        def weigh(i, c):
            rows = pl.ds(pl.multiple_of(i * 32, 32), 32)
            to = pl.ds(pl.multiple_of(core * SHARED + i * 32, 32), 32)
            cs, cc = colsin[rows, :], colcos[rows, :]
            ang = angtab[rows, :]
            for j in range(PL):
                inv = 1.0 / noise_ref[share, j : j + 1, :]
                con = ang[:, j : j + 1] * cc + ang[:, PL + j : PL + j + 1] * cs
                fac = con * inv
                take = pl.ds(i * (32 * PL) + j, 32, stride=PL)
                wall[step, to, j * WIDE : j * WIDE + COLS] = (fre[take, :] * fac).astype(bf16)
                wall[step, to, j * WIDE + COLS : (j + 1) * WIDE] = (fim[take, :] * fac).astype(bf16)
                call[step, to, j * COLS : (j + 1) * COLS] = (con * fac).astype(bf16)
            for half in (0, 1):
                for cp in swap(step, pl.ds(pl.multiple_of(core * SHARED + i * 32 + half * 16, 16), 16)):
                    cp.start()
            return c

        lax.fori_loop(0, SHARED // 32, weigh, 0)

    weigh_share(0)

    def one_share(step, carry):
        pl.when(step + 1 < NP)(lambda: weigh_share(step + 1))
        for i in range(1, NP):
            if STEPS[i]:
                pl.when(step == i)(functools.partial(traffic, STEPS[i]))
        share = step_origin(step)
        waves[...] = line_waves(share)
        ca, sa = column_waves()
        for j in range(PL):
            ref = refs_all[share, j].astype(f32)
            re, im = ref[:, :COLS], ref[:, COLS:]
            cp, sp = waves[j : j + 1, :], waves[PL + j : PL + j + 1, :]
            rbuf[:, j * COLS : (j + 1) * COLS] = (re * re + im * im).astype(bf16)
            for a, (r, m) in enumerate(((re, im), (re * ca, im * ca), (im * -sa, re * sa))):
                for b, (r2, m2) in enumerate(((r, m), (r * cp, m * cp), (m * -sp, r * sp))):
                    at = (a * 3 + b) * KO
                    sbuf[at : at + KO, j * WIDE : j * WIDE + COLS] = r2.astype(bf16)
                    sbuf[at : at + KO, j * WIDE + COLS : (j + 1) * WIDE] = m2.astype(bf16)
        nt = (((1,), (1,)), ((), ()))
        for c in swap(step, theirs):
            c.wait_recv()
        weighted_copy(step).start()
        acc[...] += lax.dot_general(sbuf[...], wall[step], nt, preferred_element_type=f32)
        eacc[...] += lax.dot_general(call[step], rbuf[...], nt, preferred_element_type=f32)
        return carry

    lax.fori_loop(0, NP, one_share, 0)

    def band(ref, i):
        return ref[i * KO : (i + 1) * KO, :]

    row = lax.broadcasted_iota(jnp.int32, (KO, N), 0)
    wanted = group * OG + row // CL
    hits = jnp.zeros((KO, N), f32)
    for j in range(list_ref.shape[0]):
        hits = jnp.where(list_ref[j : j + 1, :] == wanted, 1.0, hits)
    usable = hits > 0.5
    base = jnp.where(label_ref[0:1, :] == row % CL, prior_hit, prior_miss) - 0.5 * jnp.transpose(eacc[...])
    xs = [[band(acc, a * 3 + b) for b in range(3)] for a in range(3)]
    peak = jnp.full((KO, N), excluded, f32)
    for t in range(BASES):
        a, b = t // 3 - 1, t % 3 - 1

        def along(row_):
            return row_[0] if b == 0 else row_[1] + b * row_[2]

        cross = along(xs[0]) if a == 0 else along(xs[1]) + a * along(xs[2])
        score = jnp.where(usable, cross + base, excluded)
        sc[t * KO : (t + 1) * KO, :] = score
        peak = jnp.maximum(peak, score)
    peak = jnp.max(peak, axis=0, keepdims=True)
    mass = jnp.zeros((KO, N), f32)
    for t in range(BASES):
        mass = mass + jnp.where(usable, jnp.exp(band(sc, t) - peak), 0.0)
    mass = jnp.sum(mass, axis=0, keepdims=True)
    stats[group, 0:8, :] = jnp.broadcast_to(peak, (8, N))
    stats[group, 8:16, :] = jnp.broadcast_to(mass, (8, N))

    def stat_copy(k, slot_group, to):
        mine = stats.at[slot_group]
        return pltpu.make_async_remote_copy(
            src_ref=mine, dst_ref=mine, send_sem=ssend_sem.at[k], recv_sem=srecv_sem.at[k],
            device_id=(dom, to), device_id_type=MESH,
        )

    for k in range(1, GROUPS):
        stat_copy(k, group, (group + k) % GROUPS).start()
    for k in range(1, GROUPS):
        frm = (group + GROUPS - k) % GROUPS
        stat_copy(k, frm, frm).wait_recv()
    top = stats[0, 0:1, :]
    for g in range(1, GROUPS):
        top = jnp.maximum(top, stats[g, 0:1, :])
    total = jnp.zeros((1, N), f32)
    for g in range(GROUPS):
        total = total + stats[g, 8:9, :] * jnp.exp(stats[g, 0:1, :] - top)
    evid_ref[...] = top + jnp.log(total)
    scale = 1.0 / total
    ps = [
        [jnp.where(usable, jnp.exp(band(sc, a * 3 + b) - top) * scale, 0.0) for b in range(3)]
        for a in range(3)
    ]
    basis = []
    for less, none, more in ps:
        basis.append((none, more + less, more - less))
    for b in range(3):
        less, none, more = basis[0][b], basis[1][b], basis[2][b]
        for a, v in enumerate((none, more + less, more - less)):
            post_ref[(a * 3 + b) * KO : (a * 3 + b + 1) * KO, :] = v.astype(bf16)

    for i in range(NP):
        weighted_copy(i).wait()
        for c in swap(i, mine):
            c.wait_send()
    for i in range(len(MSGS)):
        message(i).wait_send()
    for k in range(1, GROUPS):
        stat_copy(k, group, (group + k) % GROUPS).wait_send()


CHUNKS = 8
LAG = 2
ROWS = PL * CL
HALF = ROWS // 2


def back_kernel(
    post_ref, weighted_hbm, owner_ref, slab_ref, kernel_ref, interp_ref,
    out_ref,
    wbuf, part, r1, p2, q1,
    rowre, rowim, mapped, outgoing, received, placer, sender, slab, sib, chip, y1, y2, waves,
    in_sem, send_sem, recv_sem, xsend, xrecv, ysend, yrecv,
):
    dom = lax.axis_index("dom")
    group = lax.axis_index("orient")
    z, x = dom // SIDE, dom % SIDE

    def neighbour(axis, d):
        return z * SIDE + (x + d) % SIDE if axis == "x" else ((z + d) % SIDE) * SIDE + x

    def share_of(i):
        return i // 2 + CHUNKS * (i % 2)

    def load(i):
        return pltpu.make_async_copy(weighted_hbm.at[share_of(i)], wbuf.at[i % 3], in_sem.at[i % 3])

    load(0).start()
    load(1).start()
    core, high = group % 2, group // 2
    sibling = high * 2 + 1 - core
    barrier = pltpu.get_barrier_semaphore()
    for k in range(1, NP):
        pl.semaphore_signal(barrier, inc=1, device_id=((dom + k) % NP, group), device_id_type=MESH)
    for to in (sibling, (group + 2) % GROUPS, (group + 6) % GROUPS):
        pl.semaphore_signal(barrier, inc=1, device_id=(dom, to), device_id_type=MESH)
    pl.semaphore_wait(barrier, NP + 2)

    ca, sa = column_waves()

    def compute(i):
        load(i).wait()
        pl.when(i + 2 < NP)(lambda: load(i + 2).start())
        chunk, half = i // 2, i % 2
        waves[...] = line_waves(share_of(i))
        for four in range(PL // 4):
            outs = []
            for j in range(four * 4, four * 4 + 4):
                g = jnp.dot(
                    post_ref[...], wbuf[i % 3, :, j * WIDE : (j + 1) * WIDE], preferred_element_type=f32
                )
                cp, sp = waves[j : j + 1, :], waves[PL + j : PL + j + 1, :]
                vs = []
                for a in range(3):
                    g0, gc, gs = (g[(a * 3 + b) * KO : (a * 3 + b + 1) * KO, :] for b in range(3))
                    vs.append(
                        (
                            g0[:, :COLS] + gc[:, :COLS] * cp + gs[:, COLS:] * sp,
                            g0[:, COLS:] + gc[:, COLS:] * cp - gs[:, :COLS] * sp,
                        )
                    )
                outs.append(
                    jnp.concatenate(
                        [
                            vs[0][0] + vs[1][0] * ca + vs[2][1] * sa,
                            vs[0][1] + vs[1][1] * ca - vs[2][0] * sa,
                        ],
                        axis=1,
                    )
                )
            for o in range(OG):
                piece = jnp.concatenate([v[o * CL : (o + 1) * CL, :] for v in outs], axis=0)
                part[chunk, o // 2, (o % 2) * 2 + half, pl.ds(four * 16, 16), :] = piece.astype(bf16)

    def setup(h):
        return ("x", x, "z", z) if h == 0 else ("z", z, "x", x)

    def column(c, h, f):
        rows = pl.ds(h * HALF, HALF)
        return part.at[c, :, f, rows, :] if h == 0 else part.at[c, f, :, rows, :]

    def copies(c, h, stage):
        first, f, second, s = setup(h)
        out = []
        for k in (2, 1, 3):
            idx = (h * 2 + stage) * 3 + k - 1
            if stage == 0:
                src, dst, axis = column(c, h, (f + k) % SIDE), r1.at[c, h, k - 1], first
            else:
                src, dst, axis = p2.at[c, h, (s + k) % SIDE], q1.at[c, h, k - 1], second
            out.append(
                pltpu.make_async_remote_copy(
                    src_ref=src, dst_ref=dst, send_sem=send_sem.at[c, idx], recv_sem=recv_sem.at[c, idx],
                    device_id=(neighbour(axis, k), group), device_id_type=MESH,
                )
            )
        return out

    def advance(c, stage):
        for h in (0, 1):
            first, f, second, s = setup(h)
            if stage > 0:
                for cp_ in copies(c, h, stage - 1):
                    cp_.wait_recv()
            if stage == 1:
                for i in range(SIDE):
                    rows = pl.ds(h * HALF, HALF)
                    new = (part[c, i, f, rows, :] if h == 0 else part[c, f, i, rows, :]).astype(f32)
                    for k in range(3):
                        new = new + r1[c, h, k, i].astype(f32)
                    p2[c, h, i] = new.astype(bf16)
            elif stage == 2:
                new = p2[c, h, s].astype(f32)
                for k in range(3):
                    new = new + q1[c, h, k].astype(f32)
                new = new.astype(bf16).astype(f32)
                rows = pl.ds(pl.multiple_of(c * ROWS, ROWS) + h * HALF, HALF)
                rowre[rows, :] = new[:, :COLS]
                rowim[rows, :] = new[:, COLS:]
            if stage < 2:
                for cp_ in copies(c, h, stage):
                    cp_.start()

    def ranks(own):
        hot = own == lax.broadcasted_iota(jnp.int32, (NP, COLS), 0)
        before = lax.broadcasted_iota(jnp.int32, (COLS, COLS), 0) < lax.broadcasted_iota(
            jnp.int32, (COLS, COLS), 1
        )
        hot = jnp.where(hot, 1.0, 0.0)
        counts = jnp.dot(
            hot.astype(bf16), jnp.where(before, 1.0, 0.0).astype(bf16), preferred_element_type=f32
        )
        return jnp.sum(hot * counts, axis=0, keepdims=True).astype(jnp.int32)

    def prepare():
        slot_row = lax.broadcasted_iota(jnp.int32, (CAP, COLS), 0)
        mine = pl.ds(pl.multiple_of(group * OG, OG), OG)
        owners, slabs, kernels = owner_ref[mine, :], slab_ref[mine, :].astype(f32), kernel_ref[mine, :]

        def block(a, b):
            return a[b // 2 : b // 2 + 1, (b % 2) * COLS : (b % 2 + 1) * COLS]

        def own_block(a):
            a = jnp.where(dom % 2 == 0, a[:, :COLS], a[:, COLS:]).astype(f32)
            row = lax.broadcasted_iota(jnp.int32, (OG, COLS), 0)
            return jnp.sum(jnp.where(row == dom // 2, a, 0.0), axis=0, keepdims=True).astype(jnp.int32)

        for b in range(NP):
            own = block(owners, b)
            live = (own == dom) & (ranks(own) == slot_row)
            target = jnp.sum(jnp.where(live, block(slabs, b) + 1.0, 0.0), axis=1, keepdims=True)
            spot = lax.broadcasted_iota(jnp.int32, (CAP, SLAB_ROWS), 1).astype(f32) + 1.0
            placer[b * CAP : (b + 1) * CAP, :] = jnp.where(target == spot, 1.0, 0.0)
        own = own_block(owners)
        slot = own * CAP + ranks(own)
        hit = slot == lax.broadcasted_iota(jnp.int32, (NP * CAP, COLS), 0)
        kern = own_block(kernels)
        for w in range(4):
            sender[:, w * COLS : (w + 1) * COLS] = jnp.where(hit & (kern == w), 1.0, 0.0).astype(bf16)

    def tick(t, carry):
        @pl.when(t < CHUNKS)
        def _():
            def body(q, c):
                compute(t * 2 + q)
                return c

            lax.fori_loop(0, 2, body, 0)

        pl.when(t == CHUNKS)(prepare)
        for stage in range(3):
            c = t - LAG * stage
            pl.when((c >= 0) & (c < CHUNKS))(functools.partial(advance, c, stage))
        return carry

    lax.fori_loop(0, CHUNKS + 2 * LAG, tick, 0)

    for k in range(CL):
        for n_, ref in enumerate((rowre, rowim)):
            rows = ref[pl.ds(k, COLS, stride=CL), :].astype(bf16)
            for w in range(4):
                new = jnp.dot(rows, interp_ref[w], preferred_element_type=f32)
                at = (2 * k + n_) * COLS
                mapped[w * COLS : (w + 1) * COLS, at : at + COLS] = new.astype(bf16)
    rows = jnp.dot(sender[...], mapped[...], preferred_element_type=f32)
    outgoing[...] = rows.astype(bf16).reshape(NP, CAP, CL * WIDE)

    def to_owner(k, src, dst, dev):
        return pltpu.make_async_remote_copy(
            src_ref=src, dst_ref=dst, send_sem=xsend.at[k], recv_sem=xrecv.at[k],
            device_id=(dev, group), device_id_type=MESH,
        )

    for k in range(1, NP):
        to = (dom + k) % NP
        to_owner(k, outgoing.at[to], received.at[dom], to).start()
    received[dom] = outgoing[dom]
    place = jnp.transpose(placer[...]).astype(bf16)
    for k in range(1, NP):
        frm = (dom + NP - k) % NP
        to_owner(k, outgoing.at[frm], received.at[frm], frm).wait_recv()
    rows = jnp.dot(place, received[...].reshape(NP * CAP, CL * WIDE), preferred_element_type=f32)
    slab[...] = rows.astype(bf16).reshape(SIDE, 2, SLAB_ROWS // GROUPS, CL * WIDE)

    def over_orient(i, src, dst, dev):
        return pltpu.make_async_remote_copy(
            src_ref=src, dst_ref=dst, send_sem=ysend.at[i], recv_sem=yrecv.at[i],
            device_id=(dom, dev), device_id_type=MESH,
        )

    swap = over_orient(0, slab.at[:, 1 - core], sib, sibling)
    swap.start()
    swap.wait_recv()
    part_rows = SLAB_ROWS // GROUPS // 2
    sides = ((6, 3), (2, 1))
    far = (high + 2) % SIDE
    chip[far] = (slab[far, core].astype(f32) + sib[far].astype(f32)).astype(bf16)
    first = [
        over_orient(1 + n_, chip.at[far, pl.ds(n_ * part_rows, part_rows)], y1.at[n_], (group + d) % GROUPS)
        for n_, (d, _) in enumerate(sides)
    ]
    for c in first:
        c.start()
    for d in (3, 1, 0):
        to = (high + d) % SIDE
        chip[to] = (slab[to, core].astype(f32) + sib[to].astype(f32)).astype(bf16)
    second = []
    for n_, (d, dy) in enumerate(sides):
        to = (high + dy) % SIDE
        first[n_].wait_recv()
        rows = pl.ds(n_ * part_rows, part_rows)
        chip[to, rows] = (chip[to, rows].astype(f32) + y1[n_].astype(f32)).astype(bf16)
        c = over_orient(3 + n_, chip.at[to], y2.at[n_], (group + d) % GROUPS)
        c.start()
        second.append(c)
    for c in second:
        c.wait_recv()
    out_ref[...] = chip[high].astype(f32) + y2[0].astype(f32) + y2[1].astype(f32)

    for c in range(CHUNKS):
        for h in (0, 1):
            for stage in range(2):
                for cp_ in copies(c, h, stage):
                    cp_.wait_send()
    for k in range(1, NP):
        to = (dom + k) % NP
        to_owner(k, outgoing.at[to], received.at[dom], to).wait_send()
    for c in (swap, *first, *second):
        c.wait_send()


VM = pl.BlockSpec(memory_space=pltpu.VMEM)
ANY = pl.BlockSpec(memory_space=pl.ANY)


def shards(
    images, defocus, noise_var, references, orient_list, class_label, owner, slab_row, kernel_index, interp
):
    refs = jnp.transpose(references, (2, 1, 0, 3)).reshape(PL, KO, WIDE)
    post, evidence, weighted = pl.pallas_call(
        score_kernel,
        out_shape=(
            jax.ShapeDtypeStruct((BASES * KO, N), bf16),
            jax.ShapeDtypeStruct((1, N), f32),
            jax.ShapeDtypeStruct((NP, N, PK), bf16),
        ),
        in_specs=[VM, ANY] + [VM] * 4,
        out_specs=(VM, VM, ANY),
        scratch_shapes=[
            pltpu.VMEM((NP, PL, KO, WIDE), bf16),
            pltpu.VMEM((2, SHARED, PL, WIDE), bf16),
            pltpu.VMEM((SHARED * PL, COLS), f32),
            pltpu.VMEM((SHARED * PL, COLS), f32),
            pltpu.VMEM((NP, N, PK), bf16),
            pltpu.VMEM((NP, N, PL * COLS), bf16),
            pltpu.VMEM((BASES * KO, PK), bf16),
            pltpu.VMEM((KO, PL * COLS), bf16),
            pltpu.VMEM((BASES * KO, N), f32),
            pltpu.VMEM((N, KO), f32),
            pltpu.VMEM((SHARED, COLS), f32),
            pltpu.VMEM((SHARED, COLS), f32),
            pltpu.VMEM((SHARED, COLS), f32),
            pltpu.VMEM((SHARED, COLS), f32),
            pltpu.VMEM((2 * PL, COLS), f32),
            pltpu.VMEM((BASES * KO, N), f32),
            pltpu.VMEM((GROUPS, 16, N), f32),
            pltpu.SemaphoreType.DMA((len(MSGS),)),
            pltpu.SemaphoreType.DMA((len(MSGS),)),
            pltpu.SemaphoreType.DMA((GROUPS,)),
            pltpu.SemaphoreType.DMA((GROUPS,)),
            pltpu.SemaphoreType.DMA((2,)),
        ]
        + [pltpu.SemaphoreType.DMA((NP,))] * 5,
        compiler_params=pltpu.CompilerParams(
            collective_id=0, has_side_effects=True, vmem_limit_bytes=58 * 2**20
        ),
    )(
        refs, images, defocus.reshape(1, N), noise_var.reshape(NP, PL, COLS), orient_list.T, class_label.reshape(1, N)
    )
    piece = SLAB_ROWS // GROUPS
    volume = pl.pallas_call(
        back_kernel,
        out_shape=jax.ShapeDtypeStruct((piece, CL * WIDE), f32),
        in_specs=[VM, ANY] + [VM] * 4,
        out_specs=VM,
        scratch_shapes=[
            pltpu.VMEM((3, N, PK), bf16),
            pltpu.VMEM((CHUNKS, SIDE, SIDE, ROWS, WIDE), bf16),
            pltpu.VMEM((CHUNKS, 2, 3, SIDE, HALF, WIDE), bf16),
            pltpu.VMEM((CHUNKS, 2, SIDE, HALF, WIDE), bf16),
            pltpu.VMEM((CHUNKS, 2, 3, HALF, WIDE), bf16),
            pltpu.VMEM((CHUNKS * ROWS, COLS), f32),
            pltpu.VMEM((CHUNKS * ROWS, COLS), f32),
            pltpu.VMEM((4 * COLS, CL * WIDE), bf16),
            pltpu.VMEM((NP, CAP, CL * WIDE), bf16),
            pltpu.VMEM((NP, CAP, CL * WIDE), bf16),
            pltpu.VMEM((NP * CAP, SLAB_ROWS), f32),
            pltpu.VMEM((NP * CAP, 4 * COLS), bf16),
            pltpu.VMEM((SIDE, 2, piece, CL * WIDE), bf16),
            pltpu.VMEM((SIDE, piece, CL * WIDE), bf16),
            pltpu.VMEM((SIDE, piece, CL * WIDE), bf16),
            pltpu.VMEM((2, piece // 2, CL * WIDE), bf16),
            pltpu.VMEM((2, piece, CL * WIDE), bf16),
            pltpu.VMEM((2 * PL, COLS), f32),
            pltpu.SemaphoreType.DMA((3,)),
            pltpu.SemaphoreType.DMA((CHUNKS, 12)),
            pltpu.SemaphoreType.DMA((CHUNKS, 12)),
            pltpu.SemaphoreType.DMA((NP,)),
            pltpu.SemaphoreType.DMA((NP,)),
            pltpu.SemaphoreType.DMA((5,)),
            pltpu.SemaphoreType.DMA((5,)),
        ],
        compiler_params=pltpu.CompilerParams(
            collective_id=1, has_side_effects=True, vmem_limit_bytes=40 * 2**20
        ),
    )(post, weighted, owner[:, :, 0], slab_row, kernel_index, interp)
    return volume.reshape(piece, CL, WIDE), evidence.reshape(N)


def solution(mesh):
    return jax.shard_map(
        shards,
        mesh=mesh,
        in_specs=(
            P("dom", None, None),
            P("dom"),
            P(),
            P(None, "orient", "dom", None),
            P("dom", None),
            P("dom"),
            P(),
            P(),
            P(),
            P(),
        ),
        out_specs=(P(("dom", "orient"), None, None), P("dom")),
        check_vma=False,
    )
```

```python
import functools
import math

import jax
import jax.numpy as jnp
import numpy as np
from jax import lax
from jax.experimental import pallas as pl
from jax.experimental.pallas import tpu as pltpu
from jax.sharding import PartitionSpec as P

SLAB_ROWS = 512
LINES = 256
COLS = 128
WIDE = 2 * COLS
N = 192
CL = 4
OG = 8
KO = CL * OG
PL = 16
NP = LINES // PL
PK = PL * WIDE
SIDE = 4
GROUPS = 8
BASES = 9
AHEAD = 2
SHARED = N // 2
CAP = 16

prior_hit = math.log(0.55)
prior_miss = math.log(0.15)
excluded = -1e30
MESH = pl.DeviceIdType.MESH
bf16 = jnp.bfloat16
f32 = jnp.float32

ORDER = (
    (0, 0), (0, 1), (0, 3), (1, 0), (3, 0), (1, 1), (1, 3), (3, 1), (3, 3),
    (0, 2), (2, 0), (1, 2), (3, 2), (2, 1), (2, 3), (2, 2),
)


def gather_plan():
    msgs = []
    for first, lo in (("x", 0), ("z", PL // 2)):
        mid, hi = lo + PL // 4, lo + PL // 2
        second = "z" if first == "x" else "x"

        def rel(f, s):
            return (s, f) if first == "x" else (f, s)

        msgs += [(0, rel(0, 0), lo, hi, first, d) for d in (1, -1)]
        msgs += [(1, rel(1, 0), lo, mid, first, -1), (1, rel(3, 0), mid, hi, first, 1)]
        for rank, f in ((0.5, 0), (2, 1), (2, 3), (4, 2)):
            msgs += [(rank, rel(f, 0), lo, hi, second, d) for d in (1, -1)]
            msgs += [
                (rank + 1, rel(f, 1), lo, mid, second, -1),
                (rank + 1, rel(f, 3), mid, hi, second, 1),
            ]
    msgs.sort(key=lambda m: m[0])
    msgs = [m[1:] for m in msgs]

    def landing(m):
        (dz, dx), lo, hi, axis, d = m
        return ((dz, (dx - d) % 4) if axis == "x" else ((dz - d) % 4, dx), lo, hi)

    land = [landing(m) for m in msgs]
    early = {
        1: [(0, 1, 0), (0, 3, 0), (1, 0, 1), (3, 0, 1), (0, 1, 1), (0, 3, 1), (1, 0, 0), (3, 0, 0)],
        3: [(0, 2, 0), (2, 0, 1)],
        5: [(1, 1, 0), (3, 1, 0), (1, 3, 0), (3, 3, 0), (1, 1, 1), (1, 3, 1), (3, 1, 1), (3, 3, 1)],
        10: [(1, 2, 0), (3, 2, 0), (2, 1, 1), (2, 3, 1)],
    }
    have = {((0, 0), line) for line in range(PL)}
    waited, sent, steps = set(), set(), []

    def ready(m):
        return all((m[0], line) in have for line in range(m[1], m[2]))

    for step in range(NP):
        acts = []
        if step == 0:
            for i, m in enumerate(msgs):
                if ready(m):
                    acts.append(("send", i))
                    sent.add(i)
        wanted = [((dz, dx), half) for dz, dx, half in early.get(step, [])]
        wanted += [(ORDER[step], half) for half in (0, 1)] if step else []
        for piece, half in wanted:
            for i, (at, lo, hi) in enumerate(land):
                if at == piece and lo // (PL // 2) == half and i not in waited:
                    waited.add(i)
                    acts.append(("wait", i))
                    have |= {(at, line) for line in range(lo, hi)}
            for i, m in enumerate(msgs):
                if i not in sent and ready(m):
                    acts.append(("send", i))
                    sent.add(i)
        steps.append(acts)
    assert len(waited) == len(msgs) == len(sent)
    return msgs, land, steps


MSGS, LAND, STEPS = gather_plan()


def fine_sin(angle):
    turns = jnp.floor(angle * (1.0 / math.pi) + 0.5)
    x = angle - turns * 3.140625
    x = x - turns * (math.pi - 3.140625)
    odd = turns - 2.0 * jnp.floor(turns * 0.5)
    x2 = x * x
    poly = -1.0 / 39916800.0
    for c in (1.0 / 362880.0, -1.0 / 5040.0, 1.0 / 120.0, -1.0 / 6.0):
        poly = poly * x2 + c
    s = x + x * x2 * poly
    return s * (1.0 - 2.0 * odd)


def column_waves():
    ang = lax.broadcasted_iota(jnp.int32, (1, COLS), 1).astype(f32) * (math.pi / COLS)
    return fine_sin(ang + math.pi / 2), fine_sin(ang)


def line_waves(share):
    row = lax.broadcasted_iota(jnp.int32, (2 * PL, COLS), 0)
    line = (share * PL - LINES // 2 + row % PL).astype(f32)
    return fine_sin(line * (2 * math.pi / LINES) + jnp.where(row < PL, math.pi / 2, 0.0))


def line_angles(share):
    lane = lax.broadcasted_iota(jnp.int32, (1, COLS), 1)
    line = (share * PL - LINES // 2 + lane % PL).astype(f32) * (2.0 / LINES)
    return line * line, jnp.where(lane < PL, 0.3, 0.3 + math.pi / 2)


def pick(step, values):
    out = jnp.int32(0)
    for i, v in enumerate(values):
        if v:
            out = out + jnp.where(step == i, v, 0)
    return out


def score_kernel(
    refs_ref, images_hbm, focus_ref, noise_ref, list_ref, label_ref,
    post_ref, evid_ref, weighted_hbm,
    refs_all, ibuf, fre, fim, wall, call, sbuf, rbuf, acc, eacc, focus, colsin, colcos, angtab, waves, sc, stats,
    send_sem, recv_sem, ssend_sem, srecv_sem, in_sem, out_sem, wsend, wrecv, csend, crecv,
):
    dom = lax.axis_index("dom")
    group = lax.axis_index("orient")
    z, x = dom // SIDE, dom % SIDE
    core = group % 2
    sibling = group + 1 - 2 * core
    mine = pl.ds(pl.multiple_of(core * SHARED, SHARED), SHARED)
    theirs = pl.ds(pl.multiple_of((1 - core) * SHARED, SHARED), SHARED)

    def origin(dz, dx):
        return ((z + dz) % SIDE) * SIDE + (x + dx) % SIDE

    def step_origin(step):
        return origin(pick(step, [o[0] for o in ORDER]), pick(step, [o[1] for o in ORDER]))

    def image_copy(step):
        lines = pl.ds(pl.multiple_of(step_origin(step) * PL, PL), PL)
        return pltpu.make_async_copy(images_hbm.at[mine, lines, :], ibuf.at[step % 2], in_sem.at[step % 2])

    def weighted_copy(step):
        return pltpu.make_async_copy(wall.at[step], weighted_hbm.at[step_origin(step)], out_sem.at[step])

    def swap(step, rows):
        def one(buf, send, recv):
            part = buf.at[step, rows]
            return pltpu.make_async_remote_copy(
                src_ref=part, dst_ref=part, send_sem=send.at[step], recv_sem=recv.at[step],
                device_id=(dom, sibling), device_id_type=MESH,
            )

        return one(wall, wsend, wrecv), one(call, csend, crecv)

    image_copy(0).start()

    barrier = pltpu.get_barrier_semaphore()
    for dz, dx in ((0, 1), (0, 3), (1, 0), (3, 0)):
        pl.semaphore_signal(barrier, inc=1, device_id=(origin(dz, dx), group), device_id_type=MESH)
    for k in range(1, GROUPS):
        pl.semaphore_signal(barrier, inc=1, device_id=(dom, (group + k) % GROUPS), device_id_type=MESH)
    pl.semaphore_wait(barrier, 4 + GROUPS - 1)

    def message(i):
        (dz, dx), lo, hi, axis, d = MSGS[i]
        to = origin(0, d % 4) if axis == "x" else origin(d % 4, 0)
        at = origin(dz, dx)
        rows = refs_all.at[at, pl.ds(lo, hi - lo)]
        src = refs_ref.at[pl.ds(lo, hi - lo)] if (dz, dx) == (0, 0) else rows
        return pltpu.make_async_remote_copy(
            src_ref=src, dst_ref=rows, send_sem=send_sem.at[i], recv_sem=recv_sem.at[i],
            device_id=(to, group), device_id_type=MESH,
        )

    def arrival(i):
        (dz, dx), lo, hi = LAND[i]
        rows = refs_all.at[origin(dz, dx), pl.ds(lo, hi - lo)]
        axis, d = MSGS[i][3:]
        frm = origin(0, -d % 4) if axis == "x" else origin(-d % 4, 0)
        return pltpu.make_async_remote_copy(
            src_ref=rows, dst_ref=rows, send_sem=send_sem.at[i], recv_sem=recv_sem.at[i],
            device_id=(frm, group), device_id_type=MESH,
        )

    def traffic(acts):
        for kind, i in acts:
            if kind == "send":
                message(i).start()
            else:
                arrival(i).wait_recv()

    traffic(STEPS[0])
    refs_all[dom] = refs_ref[...]
    wide = jnp.transpose(jnp.broadcast_to(focus_ref[...], (COLS, N)))
    focus[...] = jnp.where(core == 0, wide[:SHARED, :], wide[SHARED:, :])
    col = lax.broadcasted_iota(jnp.int32, (1, COLS), 1).astype(f32) * (2.0 / LINES)
    colang = focus[...] * (col * col)
    colsin[...] = fine_sin(colang)
    colcos[...] = fine_sin(colang + math.pi / 2)
    acc[...] = jnp.zeros_like(acc)
    eacc[...] = jnp.zeros_like(eacc)

    def weigh_share(step):
        share = step_origin(step)
        slot = step % 2
        pl.when(step + 1 < NP)(lambda: image_copy(step + 1).start())
        far, start = line_angles(share)
        angtab[...] = fine_sin(focus[...] * far + start)
        image_copy(step).wait()

        def widen(i, c):
            part = ibuf[slot, pl.ds(pl.multiple_of(i * 8, 8), 8)].astype(f32)
            part = part.reshape(128, WIDE)
            rows = pl.ds(pl.multiple_of(i * 128, 128), 128)
            fre[rows, :] = part[:, :COLS]
            fim[rows, :] = part[:, COLS:]
            return c

        lax.fori_loop(0, SHARED // 8, widen, 0)

        def weigh(i, c):
            rows = pl.ds(pl.multiple_of(i * 32, 32), 32)
            to = pl.ds(pl.multiple_of(core * SHARED + i * 32, 32), 32)
            cs, cc = colsin[rows, :], colcos[rows, :]
            ang = angtab[rows, :]
            for j in range(PL):
                inv = 1.0 / noise_ref[share, j : j + 1, :]
                con = ang[:, j : j + 1] * cc + ang[:, PL + j : PL + j + 1] * cs
                fac = con * inv
                take = pl.ds(i * (32 * PL) + j, 32, stride=PL)
                wall[step, to, j * WIDE : j * WIDE + COLS] = (fre[take, :] * fac).astype(bf16)
                wall[step, to, j * WIDE + COLS : (j + 1) * WIDE] = (fim[take, :] * fac).astype(bf16)
                call[step, to, j * COLS : (j + 1) * COLS] = (con * fac).astype(bf16)
            return c

        lax.fori_loop(0, SHARED // 32, weigh, 0)
        for c in swap(step, mine):
            c.start()

    for i in range(AHEAD):
        weigh_share(i)

    def one_share(step, carry):
        pl.when(step + AHEAD < NP)(lambda: weigh_share(step + AHEAD))
        for i in range(1, NP):
            if STEPS[i]:
                pl.when(step == i)(functools.partial(traffic, STEPS[i]))
        share = step_origin(step)
        waves[...] = line_waves(share)
        ca, sa = column_waves()
        for j in range(PL):
            ref = refs_all[share, j].astype(f32)
            re, im = ref[:, :COLS], ref[:, COLS:]
            cp, sp = waves[j : j + 1, :], waves[PL + j : PL + j + 1, :]
            rbuf[:, j * COLS : (j + 1) * COLS] = (re * re + im * im).astype(bf16)
            for a, (r, m) in enumerate(((re, im), (re * ca, im * ca), (im * -sa, re * sa))):
                for b, (r2, m2) in enumerate(((r, m), (r * cp, m * cp), (m * -sp, r * sp))):
                    at = (a * 3 + b) * KO
                    sbuf[at : at + KO, j * WIDE : j * WIDE + COLS] = r2.astype(bf16)
                    sbuf[at : at + KO, j * WIDE + COLS : (j + 1) * WIDE] = m2.astype(bf16)
        nt = (((1,), (1,)), ((), ()))
        for c in swap(step, theirs):
            c.wait_recv()
        weighted_copy(step).start()
        acc[...] += lax.dot_general(sbuf[...], wall[step], nt, preferred_element_type=f32)
        eacc[...] += lax.dot_general(call[step], rbuf[...], nt, preferred_element_type=f32)
        return carry

    lax.fori_loop(0, NP, one_share, 0)

    def band(ref, i):
        return ref[i * KO : (i + 1) * KO, :]

    row = lax.broadcasted_iota(jnp.int32, (KO, N), 0)
    wanted = group * OG + row // CL
    hits = jnp.zeros((KO, N), f32)
    for j in range(list_ref.shape[0]):
        hits = jnp.where(list_ref[j : j + 1, :] == wanted, 1.0, hits)
    usable = hits > 0.5
    base = jnp.where(label_ref[0:1, :] == row % CL, prior_hit, prior_miss) - 0.5 * jnp.transpose(eacc[...])
    xs = [[band(acc, a * 3 + b) for b in range(3)] for a in range(3)]
    peak = jnp.full((KO, N), excluded, f32)
    for t in range(BASES):
        a, b = t // 3 - 1, t % 3 - 1

        def along(row_):
            return row_[0] if b == 0 else row_[1] + b * row_[2]

        cross = along(xs[0]) if a == 0 else along(xs[1]) + a * along(xs[2])
        score = jnp.where(usable, cross + base, excluded)
        sc[t * KO : (t + 1) * KO, :] = score
        peak = jnp.maximum(peak, score)
    peak = jnp.max(peak, axis=0, keepdims=True)
    mass = jnp.zeros((KO, N), f32)
    for t in range(BASES):
        mass = mass + jnp.where(usable, jnp.exp(band(sc, t) - peak), 0.0)
    mass = jnp.sum(mass, axis=0, keepdims=True)
    stats[group, 0:8, :] = jnp.broadcast_to(peak, (8, N))
    stats[group, 8:16, :] = jnp.broadcast_to(mass, (8, N))

    def stat_copy(k, slot_group, to):
        mine = stats.at[slot_group]
        return pltpu.make_async_remote_copy(
            src_ref=mine, dst_ref=mine, send_sem=ssend_sem.at[k], recv_sem=srecv_sem.at[k],
            device_id=(dom, to), device_id_type=MESH,
        )

    for k in range(1, GROUPS):
        stat_copy(k, group, (group + k) % GROUPS).start()
    for k in range(1, GROUPS):
        frm = (group + GROUPS - k) % GROUPS
        stat_copy(k, frm, frm).wait_recv()
    top = stats[0, 0:1, :]
    for g in range(1, GROUPS):
        top = jnp.maximum(top, stats[g, 0:1, :])
    total = jnp.zeros((1, N), f32)
    for g in range(GROUPS):
        total = total + stats[g, 8:9, :] * jnp.exp(stats[g, 0:1, :] - top)
    evid_ref[...] = top + jnp.log(total)
    scale = 1.0 / total
    ps = [
        [jnp.where(usable, jnp.exp(band(sc, a * 3 + b) - top) * scale, 0.0) for b in range(3)]
        for a in range(3)
    ]
    basis = []
    for less, none, more in ps:
        basis.append((none, more + less, more - less))
    for b in range(3):
        less, none, more = basis[0][b], basis[1][b], basis[2][b]
        for a, v in enumerate((none, more + less, more - less)):
            post_ref[(a * 3 + b) * KO : (a * 3 + b + 1) * KO, :] = v.astype(bf16)

    for i in range(NP):
        weighted_copy(i).wait()
        for c in swap(i, mine):
            c.wait_send()
    for i in range(len(MSGS)):
        message(i).wait_send()
    for k in range(1, GROUPS):
        stat_copy(k, group, (group + k) % GROUPS).wait_send()


CHUNKS = 8
LAG = 2
ROWS = PL * CL
HALF = ROWS // 2
QUART = ROWS // 4


def back_kernel(
    post_ref, weighted_hbm, owner_ref, slab_ref, kernel_ref, interp_ref,
    out_ref,
    wbuf, part, r1, r2, p2, q1, q2,
    rowre, rowim, mapped, outgoing, received, placer, sender, slab, sib, chip, y1, y2, waves,
    in_sem, send_sem, recv_sem, xsend, xrecv, ysend, yrecv,
):
    dom = lax.axis_index("dom")
    group = lax.axis_index("orient")
    z, x = dom // SIDE, dom % SIDE

    def neighbour(axis, d):
        return z * SIDE + (x + d) % SIDE if axis == "x" else ((z + d) % SIDE) * SIDE + x

    def share_of(i):
        return i // 2 + CHUNKS * (i % 2)

    def load(i):
        return pltpu.make_async_copy(weighted_hbm.at[share_of(i)], wbuf.at[i % 3], in_sem.at[i % 3])

    load(0).start()
    load(1).start()
    core, high = group % 2, group // 2
    sibling = high * 2 + 1 - core
    barrier = pltpu.get_barrier_semaphore()
    for k in range(1, NP):
        pl.semaphore_signal(barrier, inc=1, device_id=((dom + k) % NP, group), device_id_type=MESH)
    for to in (sibling, (group + 2) % GROUPS, (group + 6) % GROUPS):
        pl.semaphore_signal(barrier, inc=1, device_id=(dom, to), device_id_type=MESH)
    pl.semaphore_wait(barrier, NP + 2)

    ca, sa = column_waves()

    def compute(i):
        load(i).wait()
        pl.when(i + 2 < NP)(lambda: load(i + 2).start())
        chunk, half = i // 2, i % 2
        waves[...] = line_waves(share_of(i))
        for four in range(PL // 4):
            outs = []
            for j in range(four * 4, four * 4 + 4):
                g = jnp.dot(
                    post_ref[...], wbuf[i % 3, :, j * WIDE : (j + 1) * WIDE], preferred_element_type=f32
                )
                cp, sp = waves[j : j + 1, :], waves[PL + j : PL + j + 1, :]
                vs = []
                for a in range(3):
                    g0, gc, gs = (g[(a * 3 + b) * KO : (a * 3 + b + 1) * KO, :] for b in range(3))
                    vs.append(
                        (
                            g0[:, :COLS] + gc[:, :COLS] * cp + gs[:, COLS:] * sp,
                            g0[:, COLS:] + gc[:, COLS:] * cp - gs[:, :COLS] * sp,
                        )
                    )
                outs.append(
                    jnp.concatenate(
                        [
                            vs[0][0] + vs[1][0] * ca + vs[2][1] * sa,
                            vs[0][1] + vs[1][1] * ca - vs[2][0] * sa,
                        ],
                        axis=1,
                    )
                )
            for o in range(OG):
                piece = jnp.concatenate([v[o * CL : (o + 1) * CL, :] for v in outs], axis=0)
                part[chunk, o // 2, (o % 2) * 2 + half, pl.ds(four * 16, 16), :] = piece.astype(bf16)

    def setup(h):
        first, second = ("x", "z") if h == 0 else ("z", "x")
        return (first, x, second, z) if h == 0 else (first, z, second, x)

    def column(c, h, f, lo, size):
        rows = pl.ds(h * HALF + lo, size)
        return part.at[c, :, f, rows, :] if h == 0 else part.at[c, f, :, rows, :]

    def copy(src, dst, c, idx, axis, d):
        return pltpu.make_async_remote_copy(
            src_ref=src, dst_ref=dst, send_sem=send_sem.at[c, idx], recv_sem=recv_sem.at[c, idx],
            device_id=(neighbour(axis, d), group), device_id_type=MESH,
        )

    def copies(c, h, stage):
        first, f, second, s = setup(h)
        far_f, far_s = (f + 2) % 4, (s + 2) % 4
        out = []
        for n_, d in enumerate((3, 1)):
            idx = (h * 4 + stage) * 2 + n_
            if stage == 0:
                out.append(copy(column(c, h, far_f, n_ * QUART, QUART), r1.at[c, h, n_], c, idx, first, d))
            elif stage == 1:
                out.append(copy(column(c, h, (f + d) % 4, 0, HALF), r2.at[c, h, n_], c, idx, first, d))
            elif stage == 2:
                src = p2.at[c, h, far_s, pl.ds(n_ * QUART, QUART), :]
                out.append(copy(src, q1.at[c, h, n_], c, idx, second, d))
            else:
                out.append(copy(p2.at[c, h, (s + d) % 4], q2.at[c, h, n_], c, idx, second, d))
        return out

    def column_get(c, h, f, i, lo, size):
        rows = pl.ds(h * HALF + lo, size)
        return part[c, i, f, rows, :] if h == 0 else part[c, f, i, rows, :]

    def column_set(c, h, f, i, lo, size, value):
        rows = pl.ds(h * HALF + lo, size)
        if h == 0:
            part[c, i, f, rows, :] = value
        else:
            part[c, f, i, rows, :] = value

    def advance(c, stage):
        for h in (0, 1):
            first, f, second, s = setup(h)
            if stage > 0:
                for cp_ in copies(c, h, stage - 1):
                    cp_.wait_recv()
            if stage == 1:
                for n_, d in enumerate((3, 1)):
                    for i in range(SIDE):
                        to = (f + d) % 4
                        mine = column_get(c, h, to, i, n_ * QUART, QUART).astype(f32)
                        new = mine + r1[c, h, n_, i].astype(f32)
                        column_set(c, h, to, i, n_ * QUART, QUART, new.astype(bf16))
            elif stage == 2:
                for i in range(SIDE):
                    new = column_get(c, h, f, i, 0, HALF).astype(f32)
                    new = new + r2[c, h, 0, i].astype(f32) + r2[c, h, 1, i].astype(f32)
                    p2[c, h, i] = new.astype(bf16)
            elif stage == 3:
                for n_, d in enumerate((3, 1)):
                    rows = pl.ds(n_ * QUART, QUART)
                    to = (s + d) % 4
                    new = p2[c, h, to, rows, :].astype(f32) + q1[c, h, n_].astype(f32)
                    p2[c, h, to, rows, :] = new.astype(bf16)
            elif stage == 4:
                new = p2[c, h, s].astype(f32) + q2[c, h, 0].astype(f32) + q2[c, h, 1].astype(f32)
                new = new.astype(bf16).astype(f32)
                rows = pl.ds(pl.multiple_of(c * ROWS, ROWS) + h * HALF, HALF)
                rowre[rows, :] = new[:, :COLS]
                rowim[rows, :] = new[:, COLS:]
            if stage < 4:
                for cp_ in copies(c, h, stage):
                    cp_.start()

    def ranks(own):
        hot = own == lax.broadcasted_iota(jnp.int32, (NP, COLS), 0)
        before = lax.broadcasted_iota(jnp.int32, (COLS, COLS), 0) < lax.broadcasted_iota(
            jnp.int32, (COLS, COLS), 1
        )
        hot = jnp.where(hot, 1.0, 0.0)
        counts = jnp.dot(
            hot.astype(bf16), jnp.where(before, 1.0, 0.0).astype(bf16), preferred_element_type=f32
        )
        return jnp.sum(hot * counts, axis=0, keepdims=True).astype(jnp.int32)

    def prepare():
        slot_row = lax.broadcasted_iota(jnp.int32, (CAP, COLS), 0)
        mine = pl.ds(pl.multiple_of(group * OG, OG), OG)
        owners, slabs, kernels = owner_ref[mine, :], slab_ref[mine, :].astype(f32), kernel_ref[mine, :]

        def block(a, b):
            return a[b // 2 : b // 2 + 1, (b % 2) * COLS : (b % 2 + 1) * COLS]

        def own_block(a):
            a = jnp.where(dom % 2 == 0, a[:, :COLS], a[:, COLS:]).astype(f32)
            row = lax.broadcasted_iota(jnp.int32, (OG, COLS), 0)
            return jnp.sum(jnp.where(row == dom // 2, a, 0.0), axis=0, keepdims=True).astype(jnp.int32)

        for b in range(NP):
            own = block(owners, b)
            live = (own == dom) & (ranks(own) == slot_row)
            target = jnp.sum(jnp.where(live, block(slabs, b) + 1.0, 0.0), axis=1, keepdims=True)
            spot = lax.broadcasted_iota(jnp.int32, (CAP, SLAB_ROWS), 1).astype(f32) + 1.0
            placer[b * CAP : (b + 1) * CAP, :] = jnp.where(target == spot, 1.0, 0.0)
        own = own_block(owners)
        slot = own * CAP + ranks(own)
        hit = slot == lax.broadcasted_iota(jnp.int32, (NP * CAP, COLS), 0)
        kern = own_block(kernels)
        for w in range(4):
            sender[:, w * COLS : (w + 1) * COLS] = jnp.where(hit & (kern == w), 1.0, 0.0).astype(bf16)

    def tick(t, carry):
        @pl.when(t < CHUNKS)
        def _():
            def body(q, c):
                compute(t * 2 + q)
                return c

            lax.fori_loop(0, 2, body, 0)

        pl.when(t == CHUNKS)(prepare)
        for stage in range(5):
            c = t - LAG * stage
            pl.when((c >= 0) & (c < CHUNKS))(functools.partial(advance, c, stage))
        return carry

    lax.fori_loop(0, CHUNKS + 4 * LAG, tick, 0)

    for k in range(CL):
        for n_, ref in enumerate((rowre, rowim)):
            rows = ref[pl.ds(k, COLS, stride=CL), :].astype(bf16)
            for w in range(4):
                new = jnp.dot(rows, interp_ref[w], preferred_element_type=f32)
                at = (2 * k + n_) * COLS
                mapped[w * COLS : (w + 1) * COLS, at : at + COLS] = new.astype(bf16)
    rows = jnp.dot(sender[...], mapped[...], preferred_element_type=f32)
    outgoing[...] = rows.astype(bf16).reshape(NP, CAP, CL * WIDE)

    def to_owner(k, src, dst, dev):
        return pltpu.make_async_remote_copy(
            src_ref=src, dst_ref=dst, send_sem=xsend.at[k], recv_sem=xrecv.at[k],
            device_id=(dev, group), device_id_type=MESH,
        )

    for k in range(1, NP):
        to = (dom + k) % NP
        to_owner(k, outgoing.at[to], received.at[dom], to).start()
    received[dom] = outgoing[dom]
    place = jnp.transpose(placer[...]).astype(bf16)
    for k in range(1, NP):
        frm = (dom + NP - k) % NP
        to_owner(k, outgoing.at[frm], received.at[frm], frm).wait_recv()
    rows = jnp.dot(place, received[...].reshape(NP * CAP, CL * WIDE), preferred_element_type=f32)
    slab[...] = rows.astype(bf16).reshape(SIDE, 2, SLAB_ROWS // GROUPS, CL * WIDE)

    def over_orient(i, src, dst, dev):
        return pltpu.make_async_remote_copy(
            src_ref=src, dst_ref=dst, send_sem=ysend.at[i], recv_sem=yrecv.at[i],
            device_id=(dom, dev), device_id_type=MESH,
        )

    swap = over_orient(0, slab.at[:, 1 - core], sib, sibling)
    swap.start()
    swap.wait_recv()
    part_rows = SLAB_ROWS // GROUPS // 2
    sides = ((6, 3), (2, 1))
    far = (high + 2) % SIDE
    chip[far] = (slab[far, core].astype(f32) + sib[far].astype(f32)).astype(bf16)
    first = [
        over_orient(1 + n_, chip.at[far, pl.ds(n_ * part_rows, part_rows)], y1.at[n_], (group + d) % GROUPS)
        for n_, (d, _) in enumerate(sides)
    ]
    for c in first:
        c.start()
    for d in (3, 1, 0):
        to = (high + d) % SIDE
        chip[to] = (slab[to, core].astype(f32) + sib[to].astype(f32)).astype(bf16)
    second = []
    for n_, (d, dy) in enumerate(sides):
        to = (high + dy) % SIDE
        first[n_].wait_recv()
        rows = pl.ds(n_ * part_rows, part_rows)
        chip[to, rows] = (chip[to, rows].astype(f32) + y1[n_].astype(f32)).astype(bf16)
        c = over_orient(3 + n_, chip.at[to], y2.at[n_], (group + d) % GROUPS)
        c.start()
        second.append(c)
    for c in second:
        c.wait_recv()
    out_ref[...] = chip[high].astype(f32) + y2[0].astype(f32) + y2[1].astype(f32)

    for c in range(CHUNKS):
        for h in (0, 1):
            for stage in range(4):
                for cp_ in copies(c, h, stage):
                    cp_.wait_send()
    for k in range(1, NP):
        to = (dom + k) % NP
        to_owner(k, outgoing.at[to], received.at[dom], to).wait_send()
    for c in (swap, *first, *second):
        c.wait_send()


VM = pl.BlockSpec(memory_space=pltpu.VMEM)
ANY = pl.BlockSpec(memory_space=pl.ANY)


def shards(
    images, defocus, noise_var, references, orient_list, class_label, owner, slab_row, kernel_index, interp
):
    refs = jnp.transpose(references, (2, 1, 0, 3)).reshape(PL, KO, WIDE)
    post, evidence, weighted = pl.pallas_call(
        score_kernel,
        out_shape=(
            jax.ShapeDtypeStruct((BASES * KO, N), bf16),
            jax.ShapeDtypeStruct((1, N), f32),
            jax.ShapeDtypeStruct((NP, N, PK), bf16),
        ),
        in_specs=[VM, ANY] + [VM] * 4,
        out_specs=(VM, VM, ANY),
        scratch_shapes=[
            pltpu.VMEM((NP, PL, KO, WIDE), bf16),
            pltpu.VMEM((2, SHARED, PL, WIDE), bf16),
            pltpu.VMEM((SHARED * PL, COLS), f32),
            pltpu.VMEM((SHARED * PL, COLS), f32),
            pltpu.VMEM((NP, N, PK), bf16),
            pltpu.VMEM((NP, N, PL * COLS), bf16),
            pltpu.VMEM((BASES * KO, PK), bf16),
            pltpu.VMEM((KO, PL * COLS), bf16),
            pltpu.VMEM((BASES * KO, N), f32),
            pltpu.VMEM((N, KO), f32),
            pltpu.VMEM((SHARED, COLS), f32),
            pltpu.VMEM((SHARED, COLS), f32),
            pltpu.VMEM((SHARED, COLS), f32),
            pltpu.VMEM((SHARED, COLS), f32),
            pltpu.VMEM((2 * PL, COLS), f32),
            pltpu.VMEM((BASES * KO, N), f32),
            pltpu.VMEM((GROUPS, 16, N), f32),
            pltpu.SemaphoreType.DMA((len(MSGS),)),
            pltpu.SemaphoreType.DMA((len(MSGS),)),
            pltpu.SemaphoreType.DMA((GROUPS,)),
            pltpu.SemaphoreType.DMA((GROUPS,)),
            pltpu.SemaphoreType.DMA((2,)),
        ]
        + [pltpu.SemaphoreType.DMA((NP,))] * 5,
        compiler_params=pltpu.CompilerParams(
            collective_id=0, has_side_effects=True, vmem_limit_bytes=58 * 2**20
        ),
    )(
        refs, images, defocus.reshape(1, N), noise_var.reshape(NP, PL, COLS), orient_list.T, class_label.reshape(1, N)
    )
    piece = SLAB_ROWS // GROUPS
    volume = pl.pallas_call(
        back_kernel,
        out_shape=jax.ShapeDtypeStruct((piece, CL * WIDE), f32),
        in_specs=[VM, ANY] + [VM] * 4,
        out_specs=VM,
        scratch_shapes=[
            pltpu.VMEM((3, N, PK), bf16),
            pltpu.VMEM((CHUNKS, SIDE, SIDE, ROWS, WIDE), bf16),
            pltpu.VMEM((CHUNKS, 2, 2, SIDE, QUART, WIDE), bf16),
            pltpu.VMEM((CHUNKS, 2, 2, SIDE, HALF, WIDE), bf16),
            pltpu.VMEM((CHUNKS, 2, SIDE, HALF, WIDE), bf16),
            pltpu.VMEM((CHUNKS, 2, 2, QUART, WIDE), bf16),
            pltpu.VMEM((CHUNKS, 2, 2, HALF, WIDE), bf16),
            pltpu.VMEM((CHUNKS * ROWS, COLS), f32),
            pltpu.VMEM((CHUNKS * ROWS, COLS), f32),
            pltpu.VMEM((4 * COLS, CL * WIDE), bf16),
            pltpu.VMEM((NP, CAP, CL * WIDE), bf16),
            pltpu.VMEM((NP, CAP, CL * WIDE), bf16),
            pltpu.VMEM((NP * CAP, SLAB_ROWS), f32),
            pltpu.VMEM((NP * CAP, 4 * COLS), bf16),
            pltpu.VMEM((SIDE, 2, piece, CL * WIDE), bf16),
            pltpu.VMEM((SIDE, piece, CL * WIDE), bf16),
            pltpu.VMEM((SIDE, piece, CL * WIDE), bf16),
            pltpu.VMEM((2, piece // 2, CL * WIDE), bf16),
            pltpu.VMEM((2, piece, CL * WIDE), bf16),
            pltpu.VMEM((2 * PL, COLS), f32),
            pltpu.SemaphoreType.DMA((3,)),
            pltpu.SemaphoreType.DMA((CHUNKS, 16)),
            pltpu.SemaphoreType.DMA((CHUNKS, 16)),
            pltpu.SemaphoreType.DMA((NP,)),
            pltpu.SemaphoreType.DMA((NP,)),
            pltpu.SemaphoreType.DMA((5,)),
            pltpu.SemaphoreType.DMA((5,)),
        ],
        compiler_params=pltpu.CompilerParams(
            collective_id=1, has_side_effects=True, vmem_limit_bytes=40 * 2**20
        ),
    )(post, weighted, owner[:, :, 0], slab_row, kernel_index, interp)
    return volume.reshape(piece, CL, WIDE), evidence.reshape(N)


def solution(mesh):
    return jax.shard_map(
        shards,
        mesh=mesh,
        in_specs=(
            P("dom", None, None),
            P("dom"),
            P(),
            P(None, "orient", "dom", None),
            P("dom", None),
            P("dom"),
            P(),
            P(),
            P(),
            P(),
        ),
        out_specs=(P(("dom", "orient"), None, None), P("dom")),
        check_vma=False,
    )
```

```python
import functools
import math

import jax
import jax.numpy as jnp
import numpy as np
from jax import lax
from jax.experimental import pallas as pl
from jax.experimental.pallas import tpu as pltpu
from jax.sharding import PartitionSpec as P

SLAB_ROWS = 512
LINES = 256
COLS = 128
WIDE = 2 * COLS
N = 192
CL = 4
OG = 8
KO = CL * OG
PL = 16
NP = LINES // PL
PK = PL * WIDE
SIDE = 4
GROUPS = 8
BASES = 9
AHEAD = 2
SHARED = N // 2
CAP = 16

prior_hit = math.log(0.55)
prior_miss = math.log(0.15)
excluded = -1e30
MESH = pl.DeviceIdType.MESH
bf16 = jnp.bfloat16
f32 = jnp.float32

ORDER = (
    (0, 0), (0, 1), (0, 3), (1, 0), (3, 0), (1, 1), (1, 3), (3, 1), (3, 3),
    (0, 2), (2, 0), (1, 2), (3, 2), (2, 1), (2, 3), (2, 2),
)


def gather_plan():
    msgs = []
    for first, lo in (("x", 0), ("z", PL // 2)):
        mid, hi = lo + PL // 4, lo + PL // 2
        second = "z" if first == "x" else "x"

        def rel(f, s):
            return (s, f) if first == "x" else (f, s)

        msgs += [(0, rel(0, 0), lo, hi, first, d) for d in (1, -1)]
        msgs += [(1, rel(1, 0), lo, mid, first, -1), (1, rel(3, 0), mid, hi, first, 1)]
        for rank, f in ((0.5, 0), (2, 1), (2, 3), (4, 2)):
            msgs += [(rank, rel(f, 0), lo, hi, second, d) for d in (1, -1)]
            msgs += [
                (rank + 1, rel(f, 1), lo, mid, second, -1),
                (rank + 1, rel(f, 3), mid, hi, second, 1),
            ]
    msgs.sort(key=lambda m: m[0])
    msgs = [m[1:] for m in msgs]

    def landing(m):
        (dz, dx), lo, hi, axis, d = m
        return ((dz, (dx - d) % 4) if axis == "x" else ((dz - d) % 4, dx), lo, hi)

    land = [landing(m) for m in msgs]
    early = {
        1: [(0, 1, 0), (0, 3, 0), (1, 0, 1), (3, 0, 1), (0, 1, 1), (0, 3, 1), (1, 0, 0), (3, 0, 0)],
        3: [(0, 2, 0), (2, 0, 1)],
        5: [(1, 1, 0), (3, 1, 0), (1, 3, 0), (3, 3, 0), (1, 1, 1), (1, 3, 1), (3, 1, 1), (3, 3, 1)],
        10: [(1, 2, 0), (3, 2, 0), (2, 1, 1), (2, 3, 1)],
    }
    have = {((0, 0), line) for line in range(PL)}
    waited, sent, steps = set(), set(), []

    def ready(m):
        return all((m[0], line) in have for line in range(m[1], m[2]))

    for step in range(NP):
        acts = []
        if step == 0:
            for i, m in enumerate(msgs):
                if ready(m):
                    acts.append(("send", i))
                    sent.add(i)
        wanted = [((dz, dx), half) for dz, dx, half in early.get(step, [])]
        wanted += [(ORDER[step], half) for half in (0, 1)] if step else []
        for piece, half in wanted:
            for i, (at, lo, hi) in enumerate(land):
                if at == piece and lo // (PL // 2) == half and i not in waited:
                    waited.add(i)
                    acts.append(("wait", i))
                    have |= {(at, line) for line in range(lo, hi)}
            for i, m in enumerate(msgs):
                if i not in sent and ready(m):
                    acts.append(("send", i))
                    sent.add(i)
        steps.append(acts)
    assert len(waited) == len(msgs) == len(sent)
    return msgs, land, steps


MSGS, LAND, STEPS = gather_plan()


def fine_sin(angle):
    turns = jnp.floor(angle * (1.0 / math.pi) + 0.5)
    x = angle - turns * 3.140625
    x = x - turns * (math.pi - 3.140625)
    odd = turns - 2.0 * jnp.floor(turns * 0.5)
    x2 = x * x
    poly = -1.0 / 39916800.0
    for c in (1.0 / 362880.0, -1.0 / 5040.0, 1.0 / 120.0, -1.0 / 6.0):
        poly = poly * x2 + c
    s = x + x * x2 * poly
    return s * (1.0 - 2.0 * odd)


def column_waves():
    ang = lax.broadcasted_iota(jnp.int32, (1, COLS), 1).astype(f32) * (math.pi / COLS)
    return fine_sin(ang + math.pi / 2), fine_sin(ang)


def line_waves(share):
    row = lax.broadcasted_iota(jnp.int32, (2 * PL, COLS), 0)
    line = (share * PL - LINES // 2 + row % PL).astype(f32)
    return fine_sin(line * (2 * math.pi / LINES) + jnp.where(row < PL, math.pi / 2, 0.0))


def line_angles(share):
    lane = lax.broadcasted_iota(jnp.int32, (1, COLS), 1)
    line = (share * PL - LINES // 2 + lane % PL).astype(f32) * (2.0 / LINES)
    return line * line, jnp.where(lane < PL, 0.3, 0.3 + math.pi / 2)


def pick(step, values):
    out = jnp.int32(0)
    for i, v in enumerate(values):
        if v:
            out = out + jnp.where(step == i, v, 0)
    return out


def score_kernel(
    refs_ref, images_hbm, focus_ref, noise_ref, list_ref, label_ref,
    post_ref, evid_ref, weighted_hbm,
    refs_all, ibuf, fre, fim, wall, call, sbuf, rbuf, acc, eacc, focus, colsin, colcos, angtab, waves, sc, stats,
    send_sem, recv_sem, ssend_sem, srecv_sem, in_sem, out_sem, wsend, wrecv, csend, crecv,
):
    dom = lax.axis_index("dom")
    group = lax.axis_index("orient")
    z, x = dom // SIDE, dom % SIDE
    core = group % 2
    sibling = group + 1 - 2 * core
    mine = pl.ds(pl.multiple_of(core * SHARED, SHARED), SHARED)
    theirs = pl.ds(pl.multiple_of((1 - core) * SHARED, SHARED), SHARED)

    def origin(dz, dx):
        return ((z + dz) % SIDE) * SIDE + (x + dx) % SIDE

    def step_origin(step):
        return origin(pick(step, [o[0] for o in ORDER]), pick(step, [o[1] for o in ORDER]))

    def image_copy(step):
        lines = pl.ds(pl.multiple_of(step_origin(step) * PL, PL), PL)
        return pltpu.make_async_copy(images_hbm.at[mine, lines, :], ibuf.at[step % 2], in_sem.at[step % 2])

    def weighted_copy(step):
        return pltpu.make_async_copy(wall.at[step], weighted_hbm.at[step_origin(step)], out_sem.at[step])

    def swap(step, rows):
        def one(buf, send, recv):
            part = buf.at[step, rows]
            return pltpu.make_async_remote_copy(
                src_ref=part, dst_ref=part, send_sem=send.at[step], recv_sem=recv.at[step],
                device_id=(dom, sibling), device_id_type=MESH,
            )

        return one(wall, wsend, wrecv), one(call, csend, crecv)

    image_copy(0).start()

    barrier = pltpu.get_barrier_semaphore()
    for dz, dx in ((0, 1), (0, 3), (1, 0), (3, 0)):
        pl.semaphore_signal(barrier, inc=1, device_id=(origin(dz, dx), group), device_id_type=MESH)
    for k in range(1, GROUPS):
        pl.semaphore_signal(barrier, inc=1, device_id=(dom, (group + k) % GROUPS), device_id_type=MESH)
    pl.semaphore_wait(barrier, 4 + GROUPS - 1)

    def message(i):
        (dz, dx), lo, hi, axis, d = MSGS[i]
        to = origin(0, d % 4) if axis == "x" else origin(d % 4, 0)
        at = origin(dz, dx)
        rows = refs_all.at[at, pl.ds(lo, hi - lo)]
        src = refs_ref.at[pl.ds(lo, hi - lo)] if (dz, dx) == (0, 0) else rows
        return pltpu.make_async_remote_copy(
            src_ref=src, dst_ref=rows, send_sem=send_sem.at[i], recv_sem=recv_sem.at[i],
            device_id=(to, group), device_id_type=MESH,
        )

    def arrival(i):
        (dz, dx), lo, hi = LAND[i]
        rows = refs_all.at[origin(dz, dx), pl.ds(lo, hi - lo)]
        axis, d = MSGS[i][3:]
        frm = origin(0, -d % 4) if axis == "x" else origin(-d % 4, 0)
        return pltpu.make_async_remote_copy(
            src_ref=rows, dst_ref=rows, send_sem=send_sem.at[i], recv_sem=recv_sem.at[i],
            device_id=(frm, group), device_id_type=MESH,
        )

    def traffic(acts):
        for kind, i in acts:
            if kind == "send":
                message(i).start()
            else:
                arrival(i).wait_recv()

    traffic(STEPS[0])
    refs_all[dom] = refs_ref[...]
    wide = jnp.transpose(jnp.broadcast_to(focus_ref[...], (COLS, N)))
    focus[...] = jnp.where(core == 0, wide[:SHARED, :], wide[SHARED:, :])
    col = lax.broadcasted_iota(jnp.int32, (1, COLS), 1).astype(f32) * (2.0 / LINES)
    colang = focus[...] * (col * col)
    colsin[...] = fine_sin(colang)
    colcos[...] = fine_sin(colang + math.pi / 2)
    acc[...] = jnp.zeros_like(acc)
    eacc[...] = jnp.zeros_like(eacc)

    def weigh_share(step):
        share = step_origin(step)
        slot = step % 2
        pl.when(step + 1 < NP)(lambda: image_copy(step + 1).start())
        far, start = line_angles(share)
        angtab[...] = fine_sin(focus[...] * far + start)
        image_copy(step).wait()

        def widen(i, c):
            part = ibuf[slot, pl.ds(pl.multiple_of(i * 8, 8), 8)].astype(f32)
            part = part.reshape(128, WIDE)
            rows = pl.ds(pl.multiple_of(i * 128, 128), 128)
            fre[rows, :] = part[:, :COLS]
            fim[rows, :] = part[:, COLS:]
            return c

        lax.fori_loop(0, SHARED // 8, widen, 0)

        def weigh(i, c):
            rows = pl.ds(pl.multiple_of(i * 32, 32), 32)
            to = pl.ds(pl.multiple_of(core * SHARED + i * 32, 32), 32)
            cs, cc = colsin[rows, :], colcos[rows, :]
            ang = angtab[rows, :]
            for j in range(PL):
                inv = 1.0 / noise_ref[share, j : j + 1, :]
                con = ang[:, j : j + 1] * cc + ang[:, PL + j : PL + j + 1] * cs
                fac = con * inv
                take = pl.ds(i * (32 * PL) + j, 32, stride=PL)
                wall[step, to, j * WIDE : j * WIDE + COLS] = (fre[take, :] * fac).astype(bf16)
                wall[step, to, j * WIDE + COLS : (j + 1) * WIDE] = (fim[take, :] * fac).astype(bf16)
                call[step, to, j * COLS : (j + 1) * COLS] = (con * fac).astype(bf16)
            return c

        lax.fori_loop(0, SHARED // 32, weigh, 0)
        for c in swap(step, mine):
            c.start()

    for i in range(AHEAD):
        weigh_share(i)

    def one_share(step, carry):
        pl.when(step + AHEAD < NP)(lambda: weigh_share(step + AHEAD))
        for i in range(1, NP):
            if STEPS[i]:
                pl.when(step == i)(functools.partial(traffic, STEPS[i]))
        share = step_origin(step)
        waves[...] = line_waves(share)
        ca, sa = column_waves()
        for j in range(PL):
            ref = refs_all[share, j].astype(f32)
            re, im = ref[:, :COLS], ref[:, COLS:]
            cp, sp = waves[j : j + 1, :], waves[PL + j : PL + j + 1, :]
            rbuf[:, j * COLS : (j + 1) * COLS] = (re * re + im * im).astype(bf16)
            for a, (r, m) in enumerate(((re, im), (re * ca, im * ca), (im * -sa, re * sa))):
                for b, (r2, m2) in enumerate(((r, m), (r * cp, m * cp), (m * -sp, r * sp))):
                    at = (a * 3 + b) * KO
                    sbuf[at : at + KO, j * WIDE : j * WIDE + COLS] = r2.astype(bf16)
                    sbuf[at : at + KO, j * WIDE + COLS : (j + 1) * WIDE] = m2.astype(bf16)
        nt = (((1,), (1,)), ((), ()))
        for c in swap(step, theirs):
            c.wait_recv()
        weighted_copy(step).start()
        acc[...] += lax.dot_general(sbuf[...], wall[step], nt, preferred_element_type=f32)
        eacc[...] += lax.dot_general(call[step], rbuf[...], nt, preferred_element_type=f32)
        return carry

    lax.fori_loop(0, NP, one_share, 0)

    def band(ref, i):
        return ref[i * KO : (i + 1) * KO, :]

    row = lax.broadcasted_iota(jnp.int32, (KO, N), 0)
    wanted = group * OG + row // CL
    hits = jnp.zeros((KO, N), f32)
    for j in range(list_ref.shape[0]):
        hits = jnp.where(list_ref[j : j + 1, :] == wanted, 1.0, hits)
    usable = hits > 0.5
    base = jnp.where(label_ref[0:1, :] == row % CL, prior_hit, prior_miss) - 0.5 * jnp.transpose(eacc[...])
    xs = [[band(acc, a * 3 + b) for b in range(3)] for a in range(3)]
    peak = jnp.full((KO, N), excluded, f32)
    for t in range(BASES):
        a, b = t // 3 - 1, t % 3 - 1

        def along(row_):
            return row_[0] if b == 0 else row_[1] + b * row_[2]

        cross = along(xs[0]) if a == 0 else along(xs[1]) + a * along(xs[2])
        score = jnp.where(usable, cross + base, excluded)
        sc[t * KO : (t + 1) * KO, :] = score
        peak = jnp.maximum(peak, score)
    peak = jnp.max(peak, axis=0, keepdims=True)
    mass = jnp.zeros((KO, N), f32)
    for t in range(BASES):
        mass = mass + jnp.where(usable, jnp.exp(band(sc, t) - peak), 0.0)
    mass = jnp.sum(mass, axis=0, keepdims=True)
    stats[group, 0:8, :] = jnp.broadcast_to(peak, (8, N))
    stats[group, 8:16, :] = jnp.broadcast_to(mass, (8, N))

    def stat_copy(k, slot_group, to):
        mine = stats.at[slot_group]
        return pltpu.make_async_remote_copy(
            src_ref=mine, dst_ref=mine, send_sem=ssend_sem.at[k], recv_sem=srecv_sem.at[k],
            device_id=(dom, to), device_id_type=MESH,
        )

    for k in range(1, GROUPS):
        stat_copy(k, group, (group + k) % GROUPS).start()
    for k in range(1, GROUPS):
        frm = (group + GROUPS - k) % GROUPS
        stat_copy(k, frm, frm).wait_recv()
    top = stats[0, 0:1, :]
    for g in range(1, GROUPS):
        top = jnp.maximum(top, stats[g, 0:1, :])
    total = jnp.zeros((1, N), f32)
    for g in range(GROUPS):
        total = total + stats[g, 8:9, :] * jnp.exp(stats[g, 0:1, :] - top)
    evid_ref[...] = top + jnp.log(total)
    scale = 1.0 / total
    ps = [
        [jnp.where(usable, jnp.exp(band(sc, a * 3 + b) - top) * scale, 0.0) for b in range(3)]
        for a in range(3)
    ]
    basis = []
    for less, none, more in ps:
        basis.append((none, more + less, more - less))
    for b in range(3):
        less, none, more = basis[0][b], basis[1][b], basis[2][b]
        for a, v in enumerate((none, more + less, more - less)):
            post_ref[(a * 3 + b) * KO : (a * 3 + b + 1) * KO, :] = v.astype(bf16)

    for i in range(NP):
        weighted_copy(i).wait()
        for c in swap(i, mine):
            c.wait_send()
    for i in range(len(MSGS)):
        message(i).wait_send()
    for k in range(1, GROUPS):
        stat_copy(k, group, (group + k) % GROUPS).wait_send()


CHUNKS = 8
LAG = 2
ROWS = PL * CL
HALF = ROWS // 2
QUART = ROWS // 4


def back_kernel(
    post_ref, weighted_hbm, owner_ref, slab_ref, kernel_ref, interp_ref,
    out_ref,
    wbuf, part, r1, r2, p2, q1, q2,
    rowre, rowim, mapped, outgoing, received, placer, sender, slab, sib, chip, y1, y2, waves,
    in_sem, send_sem, recv_sem, xsend, xrecv, ysend, yrecv,
):
    dom = lax.axis_index("dom")
    group = lax.axis_index("orient")
    z, x = dom // SIDE, dom % SIDE

    def neighbour(axis, d):
        return z * SIDE + (x + d) % SIDE if axis == "x" else ((z + d) % SIDE) * SIDE + x

    def share_of(i):
        return i // 2 + CHUNKS * (i % 2)

    def load(i):
        return pltpu.make_async_copy(weighted_hbm.at[share_of(i)], wbuf.at[i % 3], in_sem.at[i % 3])

    load(0).start()
    load(1).start()
    core, high = group % 2, group // 2
    sibling = high * 2 + 1 - core
    barrier = pltpu.get_barrier_semaphore()
    for k in range(1, NP):
        pl.semaphore_signal(barrier, inc=1, device_id=((dom + k) % NP, group), device_id_type=MESH)
    for to in (sibling, (group + 2) % GROUPS, (group + 6) % GROUPS):
        pl.semaphore_signal(barrier, inc=1, device_id=(dom, to), device_id_type=MESH)
    pl.semaphore_wait(barrier, NP + 2)

    ca, sa = column_waves()

    def compute(i):
        load(i).wait()
        pl.when(i + 2 < NP)(lambda: load(i + 2).start())
        chunk, half = i // 2, i % 2
        waves[...] = line_waves(share_of(i))
        for four in range(PL // 4):
            outs = []
            for j in range(four * 4, four * 4 + 4):
                g = jnp.dot(
                    post_ref[...], wbuf[i % 3, :, j * WIDE : (j + 1) * WIDE], preferred_element_type=f32
                )
                cp, sp = waves[j : j + 1, :], waves[PL + j : PL + j + 1, :]
                vs = []
                for a in range(3):
                    g0, gc, gs = (g[(a * 3 + b) * KO : (a * 3 + b + 1) * KO, :] for b in range(3))
                    vs.append(
                        (
                            g0[:, :COLS] + gc[:, :COLS] * cp + gs[:, COLS:] * sp,
                            g0[:, COLS:] + gc[:, COLS:] * cp - gs[:, :COLS] * sp,
                        )
                    )
                outs.append(
                    jnp.concatenate(
                        [
                            vs[0][0] + vs[1][0] * ca + vs[2][1] * sa,
                            vs[0][1] + vs[1][1] * ca - vs[2][0] * sa,
                        ],
                        axis=1,
                    )
                )
            for o in range(OG):
                piece = jnp.concatenate([v[o * CL : (o + 1) * CL, :] for v in outs], axis=0)
                part[chunk, o // 2, (o % 2) * 2 + half, pl.ds(four * 16, 16), :] = piece.astype(bf16)

    def setup(h):
        first, second = ("x", "z") if h == 0 else ("z", "x")
        return (first, x, second, z) if h == 0 else (first, z, second, x)

    def column(c, h, f, lo, size):
        rows = pl.ds(h * HALF + lo, size)
        return part.at[c, :, f, rows, :] if h == 0 else part.at[c, f, :, rows, :]

    def copy(src, dst, c, idx, axis, d):
        return pltpu.make_async_remote_copy(
            src_ref=src, dst_ref=dst, send_sem=send_sem.at[c, idx], recv_sem=recv_sem.at[c, idx],
            device_id=(neighbour(axis, d), group), device_id_type=MESH,
        )

    def copies(c, h, stage):
        first, f, second, s = setup(h)
        far_f, far_s = (f + 2) % 4, (s + 2) % 4
        out = []
        for n_, d in enumerate((3, 1)):
            idx = (h * 4 + stage) * 2 + n_
            if stage == 0:
                out.append(copy(column(c, h, far_f, n_ * QUART, QUART), r1.at[c, h, n_], c, idx, first, d))
            elif stage == 1:
                out.append(copy(column(c, h, (f + d) % 4, 0, HALF), r2.at[c, h, n_], c, idx, first, d))
            elif stage == 2:
                src = p2.at[c, h, far_s, pl.ds(n_ * QUART, QUART), :]
                out.append(copy(src, q1.at[c, h, n_], c, idx, second, d))
            else:
                out.append(copy(p2.at[c, h, (s + d) % 4], q2.at[c, h, n_], c, idx, second, d))
        return out

    def column_get(c, h, f, i, lo, size):
        rows = pl.ds(h * HALF + lo, size)
        return part[c, i, f, rows, :] if h == 0 else part[c, f, i, rows, :]

    def column_set(c, h, f, i, lo, size, value):
        rows = pl.ds(h * HALF + lo, size)
        if h == 0:
            part[c, i, f, rows, :] = value
        else:
            part[c, f, i, rows, :] = value

    def advance(c, stage):
        for h in (0, 1):
            first, f, second, s = setup(h)
            if stage > 0:
                for cp_ in copies(c, h, stage - 1):
                    cp_.wait_recv()
            if stage == 1:
                for n_, d in enumerate((3, 1)):
                    for i in range(SIDE):
                        to = (f + d) % 4
                        mine = column_get(c, h, to, i, n_ * QUART, QUART).astype(f32)
                        new = mine + r1[c, h, n_, i].astype(f32)
                        column_set(c, h, to, i, n_ * QUART, QUART, new.astype(bf16))
            elif stage == 2:
                for i in range(SIDE):
                    new = column_get(c, h, f, i, 0, HALF).astype(f32)
                    new = new + r2[c, h, 0, i].astype(f32) + r2[c, h, 1, i].astype(f32)
                    p2[c, h, i] = new.astype(bf16)
            elif stage == 3:
                for n_, d in enumerate((3, 1)):
                    rows = pl.ds(n_ * QUART, QUART)
                    to = (s + d) % 4
                    new = p2[c, h, to, rows, :].astype(f32) + q1[c, h, n_].astype(f32)
                    p2[c, h, to, rows, :] = new.astype(bf16)
            elif stage == 4:
                new = p2[c, h, s].astype(f32) + q2[c, h, 0].astype(f32) + q2[c, h, 1].astype(f32)
                new = new.astype(bf16).astype(f32)
                rows = pl.ds(pl.multiple_of(c * ROWS, ROWS) + h * HALF, HALF)
                rowre[rows, :] = new[:, :COLS]
                rowim[rows, :] = new[:, COLS:]
            if stage < 4:
                for cp_ in copies(c, h, stage):
                    cp_.start()

    def ranks(own):
        hot = own == lax.broadcasted_iota(jnp.int32, (NP, COLS), 0)
        before = lax.broadcasted_iota(jnp.int32, (COLS, COLS), 0) < lax.broadcasted_iota(
            jnp.int32, (COLS, COLS), 1
        )
        hot = jnp.where(hot, 1.0, 0.0)
        counts = jnp.dot(
            hot.astype(bf16), jnp.where(before, 1.0, 0.0).astype(bf16), preferred_element_type=f32
        )
        return jnp.sum(hot * counts, axis=0, keepdims=True).astype(jnp.int32)

    def prepare():
        slot_row = lax.broadcasted_iota(jnp.int32, (CAP, COLS), 0)
        mine = pl.ds(pl.multiple_of(group * OG, OG), OG)
        owners, slabs, kernels = owner_ref[mine, :], slab_ref[mine, :].astype(f32), kernel_ref[mine, :]

        def block(a, b):
            return a[b // 2 : b // 2 + 1, (b % 2) * COLS : (b % 2 + 1) * COLS]

        def own_block(a):
            a = jnp.where(dom % 2 == 0, a[:, :COLS], a[:, COLS:]).astype(f32)
            row = lax.broadcasted_iota(jnp.int32, (OG, COLS), 0)
            return jnp.sum(jnp.where(row == dom // 2, a, 0.0), axis=0, keepdims=True).astype(jnp.int32)

        for b in range(NP):
            own = block(owners, b)
            live = (own == dom) & (ranks(own) == slot_row)
            target = jnp.sum(jnp.where(live, block(slabs, b) + 1.0, 0.0), axis=1, keepdims=True)
            spot = lax.broadcasted_iota(jnp.int32, (CAP, SLAB_ROWS), 1).astype(f32) + 1.0
            placer[b * CAP : (b + 1) * CAP, :] = jnp.where(target == spot, 1.0, 0.0)
        own = own_block(owners)
        slot = own * CAP + ranks(own)
        hit = slot == lax.broadcasted_iota(jnp.int32, (NP * CAP, COLS), 0)
        kern = own_block(kernels)
        for w in range(4):
            sender[:, w * COLS : (w + 1) * COLS] = jnp.where(hit & (kern == w), 1.0, 0.0).astype(bf16)

    def tick(t, carry):
        pl.when(t < CHUNKS)(lambda: compute(t * 2))
        for stage in range(1, 5):
            c = t - LAG * stage
            pl.when((c >= 0) & (c < CHUNKS))(functools.partial(advance, c, stage))
        pl.when(t == CHUNKS)(prepare)

        @pl.when(t < CHUNKS)
        def _():
            compute(t * 2 + 1)
            advance(t, 0)

        return carry

    lax.fori_loop(0, CHUNKS + 4 * LAG, tick, 0)

    for k in range(CL):
        for n_, ref in enumerate((rowre, rowim)):
            rows = ref[pl.ds(k, COLS, stride=CL), :].astype(bf16)
            for w in range(4):
                new = jnp.dot(rows, interp_ref[w], preferred_element_type=f32)
                at = (2 * k + n_) * COLS
                mapped[w * COLS : (w + 1) * COLS, at : at + COLS] = new.astype(bf16)
    rows = jnp.dot(sender[...], mapped[...], preferred_element_type=f32)
    outgoing[...] = rows.astype(bf16).reshape(NP, CAP, CL * WIDE)

    def to_owner(k, src, dst, dev):
        return pltpu.make_async_remote_copy(
            src_ref=src, dst_ref=dst, send_sem=xsend.at[k], recv_sem=xrecv.at[k],
            device_id=(dev, group), device_id_type=MESH,
        )

    for k in range(1, NP):
        to = (dom + k) % NP
        to_owner(k, outgoing.at[to], received.at[dom], to).start()
    received[dom] = outgoing[dom]
    place = jnp.transpose(placer[...]).astype(bf16)
    for k in range(1, NP):
        frm = (dom + NP - k) % NP
        to_owner(k, outgoing.at[frm], received.at[frm], frm).wait_recv()
    rows = jnp.dot(place, received[...].reshape(NP * CAP, CL * WIDE), preferred_element_type=f32)
    slab[...] = rows.astype(bf16).reshape(SIDE, 2, SLAB_ROWS // GROUPS, CL * WIDE)

    def over_orient(i, src, dst, dev):
        return pltpu.make_async_remote_copy(
            src_ref=src, dst_ref=dst, send_sem=ysend.at[i], recv_sem=yrecv.at[i],
            device_id=(dom, dev), device_id_type=MESH,
        )

    swap = over_orient(0, slab.at[:, 1 - core], sib, sibling)
    swap.start()
    swap.wait_recv()
    part_rows = SLAB_ROWS // GROUPS // 2
    sides = ((6, 3), (2, 1))
    far = (high + 2) % SIDE
    chip[far] = (slab[far, core].astype(f32) + sib[far].astype(f32)).astype(bf16)
    first = [
        over_orient(1 + n_, chip.at[far, pl.ds(n_ * part_rows, part_rows)], y1.at[n_], (group + d) % GROUPS)
        for n_, (d, _) in enumerate(sides)
    ]
    for c in first:
        c.start()
    for d in (3, 1, 0):
        to = (high + d) % SIDE
        chip[to] = (slab[to, core].astype(f32) + sib[to].astype(f32)).astype(bf16)
    second = []
    for n_, (d, dy) in enumerate(sides):
        to = (high + dy) % SIDE
        first[n_].wait_recv()
        rows = pl.ds(n_ * part_rows, part_rows)
        chip[to, rows] = (chip[to, rows].astype(f32) + y1[n_].astype(f32)).astype(bf16)
        c = over_orient(3 + n_, chip.at[to], y2.at[n_], (group + d) % GROUPS)
        c.start()
        second.append(c)
    for c in second:
        c.wait_recv()
    out_ref[...] = chip[high].astype(f32) + y2[0].astype(f32) + y2[1].astype(f32)

    for c in range(CHUNKS):
        for h in (0, 1):
            for stage in range(4):
                for cp_ in copies(c, h, stage):
                    cp_.wait_send()
    for k in range(1, NP):
        to = (dom + k) % NP
        to_owner(k, outgoing.at[to], received.at[dom], to).wait_send()
    for c in (swap, *first, *second):
        c.wait_send()


VM = pl.BlockSpec(memory_space=pltpu.VMEM)
ANY = pl.BlockSpec(memory_space=pl.ANY)


def shards(
    images, defocus, noise_var, references, orient_list, class_label, owner, slab_row, kernel_index, interp
):
    refs = jnp.transpose(references, (2, 1, 0, 3)).reshape(PL, KO, WIDE)
    post, evidence, weighted = pl.pallas_call(
        score_kernel,
        out_shape=(
            jax.ShapeDtypeStruct((BASES * KO, N), bf16),
            jax.ShapeDtypeStruct((1, N), f32),
            jax.ShapeDtypeStruct((NP, N, PK), bf16),
        ),
        in_specs=[VM, ANY] + [VM] * 4,
        out_specs=(VM, VM, ANY),
        scratch_shapes=[
            pltpu.VMEM((NP, PL, KO, WIDE), bf16),
            pltpu.VMEM((2, SHARED, PL, WIDE), bf16),
            pltpu.VMEM((SHARED * PL, COLS), f32),
            pltpu.VMEM((SHARED * PL, COLS), f32),
            pltpu.VMEM((NP, N, PK), bf16),
            pltpu.VMEM((NP, N, PL * COLS), bf16),
            pltpu.VMEM((BASES * KO, PK), bf16),
            pltpu.VMEM((KO, PL * COLS), bf16),
            pltpu.VMEM((BASES * KO, N), f32),
            pltpu.VMEM((N, KO), f32),
            pltpu.VMEM((SHARED, COLS), f32),
            pltpu.VMEM((SHARED, COLS), f32),
            pltpu.VMEM((SHARED, COLS), f32),
            pltpu.VMEM((SHARED, COLS), f32),
            pltpu.VMEM((2 * PL, COLS), f32),
            pltpu.VMEM((BASES * KO, N), f32),
            pltpu.VMEM((GROUPS, 16, N), f32),
            pltpu.SemaphoreType.DMA((len(MSGS),)),
            pltpu.SemaphoreType.DMA((len(MSGS),)),
            pltpu.SemaphoreType.DMA((GROUPS,)),
            pltpu.SemaphoreType.DMA((GROUPS,)),
            pltpu.SemaphoreType.DMA((2,)),
        ]
        + [pltpu.SemaphoreType.DMA((NP,))] * 5,
        compiler_params=pltpu.CompilerParams(
            collective_id=0, has_side_effects=True, vmem_limit_bytes=58 * 2**20
        ),
    )(
        refs, images, defocus.reshape(1, N), noise_var.reshape(NP, PL, COLS), orient_list.T, class_label.reshape(1, N)
    )
    piece = SLAB_ROWS // GROUPS
    volume = pl.pallas_call(
        back_kernel,
        out_shape=jax.ShapeDtypeStruct((piece, CL * WIDE), f32),
        in_specs=[VM, ANY] + [VM] * 4,
        out_specs=VM,
        scratch_shapes=[
            pltpu.VMEM((3, N, PK), bf16),
            pltpu.VMEM((CHUNKS, SIDE, SIDE, ROWS, WIDE), bf16),
            pltpu.VMEM((CHUNKS, 2, 2, SIDE, QUART, WIDE), bf16),
            pltpu.VMEM((CHUNKS, 2, 2, SIDE, HALF, WIDE), bf16),
            pltpu.VMEM((CHUNKS, 2, SIDE, HALF, WIDE), bf16),
            pltpu.VMEM((CHUNKS, 2, 2, QUART, WIDE), bf16),
            pltpu.VMEM((CHUNKS, 2, 2, HALF, WIDE), bf16),
            pltpu.VMEM((CHUNKS * ROWS, COLS), f32),
            pltpu.VMEM((CHUNKS * ROWS, COLS), f32),
            pltpu.VMEM((4 * COLS, CL * WIDE), bf16),
            pltpu.VMEM((NP, CAP, CL * WIDE), bf16),
            pltpu.VMEM((NP, CAP, CL * WIDE), bf16),
            pltpu.VMEM((NP * CAP, SLAB_ROWS), f32),
            pltpu.VMEM((NP * CAP, 4 * COLS), bf16),
            pltpu.VMEM((SIDE, 2, piece, CL * WIDE), bf16),
            pltpu.VMEM((SIDE, piece, CL * WIDE), bf16),
            pltpu.VMEM((SIDE, piece, CL * WIDE), bf16),
            pltpu.VMEM((2, piece // 2, CL * WIDE), bf16),
            pltpu.VMEM((2, piece, CL * WIDE), bf16),
            pltpu.VMEM((2 * PL, COLS), f32),
            pltpu.SemaphoreType.DMA((3,)),
            pltpu.SemaphoreType.DMA((CHUNKS, 16)),
            pltpu.SemaphoreType.DMA((CHUNKS, 16)),
            pltpu.SemaphoreType.DMA((NP,)),
            pltpu.SemaphoreType.DMA((NP,)),
            pltpu.SemaphoreType.DMA((5,)),
            pltpu.SemaphoreType.DMA((5,)),
        ],
        compiler_params=pltpu.CompilerParams(
            collective_id=1, has_side_effects=True, vmem_limit_bytes=40 * 2**20
        ),
    )(post, weighted, owner[:, :, 0], slab_row, kernel_index, interp)
    return volume.reshape(piece, CL, WIDE), evidence.reshape(N)


def solution(mesh):
    return jax.shard_map(
        shards,
        mesh=mesh,
        in_specs=(
            P("dom", None, None),
            P("dom"),
            P(),
            P(None, "orient", "dom", None),
            P("dom", None),
            P("dom"),
            P(),
            P(),
            P(),
            P(),
        ),
        out_specs=(P(("dom", "orient"), None, None), P("dom")),
        check_vma=False,
    )
```
